32 devices in a mesh: ctx: 8 (over y, x, core), fsdp: 4 (over z).
Axes of the slice: x: 2, y: 2, z: 4, core: 2. Of those that a mesh axis runs over, the one named last changes fastest.
Arguments:
- inputs: bfloat16 [4, 1024, 512], P('fsdp', 'ctx'), may hold values from -6 to 6
- block_order: int32 [16], replicated, may hold values from 0 to 15, each once
- ln1_gain: bfloat16 [512], P('fsdp'), may hold values from 0.5 to 1.5
- ln1_bias: bfloat16 [512], P('fsdp'), may hold values from -3 to 3
- w_qkv: bfloat16 [512, 1536], P('fsdp'), may hold values from -0.25 to 0.25
- b_qkv: bfloat16 [1536], P('fsdp'), may hold values from -3 to 3
- w_attn_out: bfloat16 [512, 512], P('fsdp'), may hold values from -3 to 3
- b_attn_out: bfloat16 [512], P('fsdp'), may hold values from -3 to 3
- ln2_gain: bfloat16 [512], P('fsdp'), may hold values from 0.5 to 1.5
- ln2_bias: bfloat16 [512], P('fsdp'), may hold values from -3 to 3
- w_up: bfloat16 [512, 2048], P('fsdp'), may hold values from -0.25 to 0.25
- b_up: bfloat16 [2048], P('fsdp'), may hold values from -3 to 3
- w_down: bfloat16 [2048, 512], P('fsdp'), may hold values from -0.125 to 0.125
- b_down: bfloat16 [512], P('fsdp'), may hold values from -3 to 3
- cotangent: bfloat16 [4, 1024, 512], P('fsdp', 'ctx'), may hold values from -6 to 6
Outputs:
- output: bfloat16 [4, 1024, 512], P('fsdp', 'ctx')
- grad_inputs: float32 [4, 1024, 512], P('fsdp', 'ctx')
- grad_ln1_gain: float32 [512], P('fsdp')
- grad_ln1_bias: float32 [512], P('fsdp')
- grad_w_qkv: float32 [512, 1536], P('fsdp')
- grad_b_qkv: float32 [1536], P('fsdp')
- grad_w_attn_out: float32 [512, 512], P('fsdp')
- grad_b_attn_out: float32 [512], P('fsdp')
- grad_ln2_gain: float32 [512], P('fsdp')
- grad_ln2_bias: float32 [512], P('fsdp')
- grad_w_up: float32 [512, 2048], P('fsdp')
- grad_b_up: float32 [2048], P('fsdp')
- grad_w_down: float32 [2048, 512], P('fsdp')
- grad_b_down: float32 [512], P('fsdp')
The draws below stay inside these ranges and needn't reach their ends.
Inputs may be any that keep to these rules, and one draw needn't show every extreme that they name: Each number appears once; storage block j of a sequence (rows j * 64 to (j + 1) * 64 - 1) holds position block block_order[j].
All inputs are finite; a program needn't handle non-finite values.
Results may differ from the reference program's by a relative error of at most 0.018.
Values may be sent and summed in bfloat16 or wider, within the bound.
No kernel may reach another device: no remote copies, remote signals or barrier semaphores. Data moves between devices by JAX's collectives and lax.ppermute only.
A program may use at most 128 MiB of HBM per device.

```python
import jax
import jax.numpy as jnp
from jax import lax

HEADS = 8
HEAD_DIM = 64
FF = 2048
D = 512
ROT = 16
HALF = 64
LEN = 1024
BATCH = 4
N_CTX = 8


def block_levels(stream_key, shape, shards, low, top_value):
    loudness, own = 1.0, jax.random.fold_in(stream_key, 6)
    for dim, parts in shards:
        steps = jnp.exp(jax.random.uniform(jax.random.fold_in(own, dim), (parts,), jnp.float32, low / len(shards), top_value / len(shards)))
        loudness = loudness * jnp.repeat(steps, shape[dim] // parts).reshape([-1 if axis == dim else 1 for axis in range(len(shape))])
    return loudness


def normal_values(stream_key, dims, deviation, limit, pieces=(), kind=jnp.bfloat16):
    values = jax.random.normal(stream_key, dims, jnp.float32) * deviation
    if len(pieces) > 0:
        values = block_levels(stream_key, dims, pieces, -0.22, 0.18) * values
    return jnp.clip(values, min=-limit, max=limit).astype(kind)


def setup_inputs(seed: int = 0) -> dict:
    streams_of = jax.random.split(jax.random.key(seed), 16)
    return {
        "inputs": normal_values(streams_of[0], (BATCH, LEN, D), 1.0, 6.0, ((0, 4), (1, 8))),
        "block_order": jax.random.permutation(streams_of[1], 2 * N_CTX).astype(jnp.int32),
        "ln1_gain": jnp.clip(1.0 + 0.1 * jax.random.normal(streams_of[2], (D,), jnp.float32), 0.5, 1.5).astype(jnp.bfloat16),
        "ln1_bias": normal_values(streams_of[3], (D,), 0.3, 3.0, ((0, 4),)),
        "w_qkv": normal_values(streams_of[4], (D, 3 * D), D ** -0.5, 0.25, ((0, 4),)),
        "b_qkv": normal_values(streams_of[5], (3 * D,), 0.3, 3.0, ((0, 4),)),
        "w_attn_out": normal_values(streams_of[6], (D, D), 4 ** -0.5, 3.0, ((0, 4),)),
        "b_attn_out": normal_values(streams_of[7], (D,), 0.3, 3.0, ((0, 4),)),
        "ln2_gain": jnp.clip(1.0 + 0.1 * jax.random.normal(streams_of[8], (D,), jnp.float32), 0.5, 1.5).astype(jnp.bfloat16),
        "ln2_bias": normal_values(streams_of[9], (D,), 0.3, 3.0, ((0, 4),)),
        "w_up": normal_values(streams_of[10], (D, FF), D ** -0.5, 0.25, ((0, 4),)),
        "b_up": normal_values(streams_of[11], (FF,), 0.3, 3.0, ((0, 4),)),
        "w_down": normal_values(streams_of[12], (FF, D), FF ** -0.5, 0.125, ((0, 4),)),
        "b_down": normal_values(streams_of[13], (D,), 0.3, 3.0, ((0, 4),)),
        "cotangent": normal_values(streams_of[14], (BATCH, LEN, D), 1.0, 6.0, ((0, 4), (1, 8))),
    }


HIGH = lax.Precision.HIGHEST

@jax.custom_vjp
def low(v):
    return lax.optimization_barrier(v.astype(jnp.bfloat16)).astype(jnp.float32)

@jax.custom_vjp
def low_back(v):
    return v

def low_keep(v):
    return (low(v), None)

def low_pass(kept, grad):
    return (grad,)

def back_keep(v):
    return (v, None)

def back_low(kept, grad):
    return (low(grad),)
low.defvjp(low_keep, low_pass)
low_back.defvjp(back_keep, back_low)

def layer_norm(values, scale_vec, shift_vec):
    center = values - lax.optimization_barrier(jnp.mean(values, axis=-1, keepdims=True))
    spread = lax.optimization_barrier(jnp.mean(center * center, axis=-1, keepdims=True))
    return center * lax.rsqrt(spread + 1e-05) * scale_vec + shift_vec

def rotate(tensor, cosine, sine_val):
    half_rot = cosine.shape[-1]
    cos_b = cosine[:, None, :]
    sin_b = sine_val[:, None, :]
    front_half = tensor[..., :half_rot]
    back_half = tensor[..., half_rot:2 * half_rot]
    return jnp.concatenate([front_half * cos_b - back_half * sin_b, back_half * cos_b + front_half * sin_b, tensor[..., 2 * half_rot:]], axis=-1)

def forward(sequence, params, positions, cosine, sine_val):
    ln1_scale, ln1_shift, qkv_weight, qkv_bias, out_weight, out_bias, ln2_scale, ln2_shift, up_weight, up_bias, down_weight, down_bias = params
    normed_one = low(layer_norm(sequence, ln1_scale, ln1_shift))
    project = low_back(jnp.dot(normed_one, qkv_weight, precision=HIGH) + qkv_bias)
    queries = low(rotate(project[:, :D].reshape(LEN, HEADS, HEAD_DIM), cosine, sine_val))
    key_rows = low(rotate(project[:, D:2 * D].reshape(LEN, HEADS, HEAD_DIM), cosine, sine_val))
    value_rows = low(project[:, 2 * D:].reshape(LEN, HEADS, HEAD_DIM))
    block_rows = min(512, LEN)
    block_count = LEN // block_rows

    def attend(block_pair):
        query_block, query_pos = block_pair
        logits = low_back(jnp.einsum('qhd,khd->hqk', query_block, key_rows, precision=HIGH) * 0.125)
        allowed = query_pos[:, None] >= positions[None, :]
        logits = jnp.where(allowed[None], logits, -1e+30)
        attn_probs = low(jax.nn.softmax(logits, axis=-1))
        return jnp.einsum('hqk,khd->qhd', attn_probs, value_rows, precision=HIGH)
    mixture = lax.map(jax.checkpoint(attend), (queries.reshape(block_count, block_rows, HEADS, HEAD_DIM), positions.reshape(block_count, block_rows)))
    mixture = low_back(low(mixture.reshape(LEN, D)))
    attn_out = jnp.dot(mixture, out_weight, precision=HIGH) + out_bias
    normed_two = low(layer_norm(sequence, ln2_scale, ln2_shift))
    pre_act = low_back(jnp.dot(normed_two, up_weight, precision=HIGH) + up_bias)
    hidden = low(jax.nn.gelu(pre_act, approximate=False))
    return sequence + attn_out + jnp.dot(hidden, down_weight, precision=HIGH) + down_bias

def reference(inputs, block_order, ln1_gain, ln1_bias, w_qkv, b_qkv, w_attn_out, b_attn_out, ln2_gain, ln2_bias, w_up, b_up, w_down, b_down, cotangent):
    params = tuple((item.astype(jnp.float32) for item in (ln1_gain, ln1_bias, w_qkv, b_qkv, w_attn_out, b_attn_out, ln2_gain, ln2_bias, w_up, b_up, w_down, b_down)))
    rows_all = jnp.arange(LEN, dtype=jnp.int32)
    positions = (block_order[rows_all // HALF] * HALF + rows_all % HALF).astype(jnp.int32)
    inverse = 10000.0 ** (-jnp.arange(ROT // 2, dtype=jnp.float32) * 2.0 / ROT)
    angles = positions.astype(jnp.float32)[:, None] * inverse[None, :]
    cosine = jnp.cos(angles)
    sine_val = jnp.sin(angles)

    def one_sequence(grad_total, seq_pair):
        sequence, grad_seq = seq_pair

        def apply_layer(seq_in, param_in):
            return forward(seq_in, param_in, positions, cosine, sine_val)
        result, pullback = jax.vjp(apply_layer, sequence, params)
        grad_seq_in, grad_params = pullback(grad_seq)
        grad_total = jax.tree.map(jnp.add, grad_total, grad_params)
        return (grad_total, (result, grad_seq_in))
    zeros_init = jax.tree.map(jnp.zeros_like, params)
    grad_total, (outputs, grad_inputs) = lax.scan(one_sequence, zeros_init, (inputs.astype(jnp.float32), cotangent.astype(jnp.float32)))
    return (outputs.astype(jnp.bfloat16), grad_inputs, grad_total[0], grad_total[1], grad_total[2], grad_total[3], grad_total[4], grad_total[5], grad_total[6], grad_total[7], grad_total[8], grad_total[9], grad_total[10], grad_total[11])
```

```python
import functools

import jax
import jax.numpy as jnp
import numpy as np
from jax import lax
from jax.experimental import pallas as pl
from jax.experimental.pallas import tpu as pltpu
from jax.sharding import PartitionSpec as P

HEADS = 8
HEAD_DIM = 64
D = 512
FF = 2048
ROT = 16
HALF = 64
TOK = 128
EPS = 1e-05
F32 = jnp.float32
BF16 = jnp.bfloat16
VMEM_LIMIT = 48 * 1024 * 1024


def mm(left, right, dims):
    return lax.dot_general(left, right, (dims, ((), ())), preferred_element_type=F32)


def mm_nn(left, right):
    return mm(left, right, ((1,), (0,)))


def mm_nt(left, right):
    return mm(left, right, ((1,), (1,)))


def mm_tn(left, right):
    return mm(left, right, ((0,), (0,)))


def vmem_call(body, out_shape, scratch=(), n_smem=0, n_in=0, cost=None, name=None):
    smem = pl.BlockSpec(memory_space=pltpu.SMEM)
    vmem = pl.BlockSpec(memory_space=pltpu.VMEM)
    return pl.pallas_call(
        body,
        out_shape=out_shape,
        in_specs=[smem] * n_smem + [vmem] * n_in,
        out_specs=jax.tree.map(lambda _: vmem, out_shape),
        scratch_shapes=list(scratch),
        compiler_params=pltpu.CompilerParams(vmem_limit_bytes=VMEM_LIMIT),
        cost_estimate=cost,
        name=name,
    )


def half_pick(block, odd, to_upper):
    moved = pltpu.roll(block, 64, 1)
    return jnp.where(odd, block if to_upper else moved, moved if to_upper else block)


def low_lanes(shape):
    return lax.broadcasted_iota(jnp.int32, shape, len(shape) - 1) % 128 < 64


def pack_body(nz, place, w_qkv, w_up, w_down, w_out, out_a, out_b, out_w):
    me = place[0]
    pair = me // 2
    odd = (me % 2) == 1
    lane = pl.multiple_of(pair * 128, 128)

    def take(ref, start):
        return ref[:, pl.ds(pl.multiple_of(start + lane, 128), 128)].astype(F32)

    rows = w_qkv.shape[0]
    low = low_lanes((rows, 128))
    q = half_pick(take(w_qkv, 0), odd, False)
    k = half_pick(take(w_qkv, D), odd, True)
    v = half_pick(take(w_qkv, 2 * D), odd, False)
    out_a[:, 0:128] = jnp.where(low, q, k).astype(BF16)
    out_a[:, 128:256] = jnp.where(low, v, 0.0).astype(BF16)
    span = FF // nz
    for z in range(0, nz, 2):
        even = half_pick(take(w_up, z * span), odd, False)
        later = half_pick(take(w_up, (z + 1) * span), odd, True)
        out_b[:, z * 64 : z * 64 + 128] = jnp.where(low, even, later).astype(BF16)
    down = w_down[pl.ds(pl.multiple_of(me * 64, 64), 64), :]
    out_b[0:64, 256:512] = down[:, 0:256]
    out_b[64:128, 256:512] = down[:, 256:512]
    out_w[...] = w_out[pl.ds(pl.multiple_of((me % 2) * 64, 64), 64), :]


def small_body(nz, place, *refs):
    pieces, out, held = refs[:nz], refs[nz], refs[nz + 1]
    me, zed = place[0], place[1]
    pair = me // 2
    odd = (me % 2) == 1
    for k in range(nz):
        held[zed ^ k] = pieces[k][...].astype(F32)
    out[...] = jnp.zeros_like(out)
    for z in range(nz):
        lanes = slice(z * 128, (z + 1) * 128)
        out[0:4, lanes] = held[z, 0:4, :]
        out[4:5, lanes] = held[z, 4:5, :] + held[z, 5:6, :]
    low = low_lanes((1, 128))

    def qkv_row(group):
        index = group * 4 + pair
        z = index // 3
        return held[z, pl.ds(6 + index - 3 * z, 1), :]

    q = half_pick(qkv_row(0), odd, False)
    k = half_pick(qkv_row(1), odd, True)
    v = half_pick(qkv_row(2), odd, False)
    out[5:6, 0:128] = jnp.where(low, q, k)
    out[5:6, 128:256] = jnp.where(low, v, 0.0)
    for z in range(0, nz, 2):
        even = half_pick(held[z, pl.ds(9 + pair, 1), :], odd, False)
        later = half_pick(held[z + 1, pl.ds(9 + pair, 1), :], odd, True)
        out[6:7, z * 64 : z * 64 + 128] = jnp.where(low, even, later)


def normalized(x):
    center = x - jnp.mean(x, axis=-1, keepdims=True)
    spread = jnp.mean(center * center, axis=-1, keepdims=True)
    inv = lax.rsqrt(spread + EPS)
    return center * inv, inv


def ff_body(n, nz, fast, place, *refs):
    pieces = refs[:n]
    n_w = nz if fast else 2
    weights = refs[n : n + n_w]
    params = refs[n + n_w]
    outs = refs[n + n_w + 1 :]
    n_pay = nz if fast else 2
    acc_o, acc_d, vec = outs[:3]
    pays = outs[3 : 3 + n_pay]
    w_up, w_down, norms, hiddens, dpres, gs, grad_up, grad_down = outs[3 + n_pay :]
    width = w_up.shape[1]
    zed = place[1]
    if fast:
        for k in range(nz):
            z = zed ^ k
            w_up[pl.ds(pl.multiple_of(z * 128, 128), 128), :] = weights[k][:, 0:256]
            rows = pl.ds(pl.multiple_of(z * 64, 64), 64)
            w_down[rows, 0:256] = weights[k][0:64, 256:512]
            w_down[rows, 256:512] = weights[k][64:128, 256:512]
    else:
        w_up[...] = weights[0][...]
        w_down[...] = weights[1][...]
    gain, shift = params[2:3, :], params[3:4, :]
    b_up = params[6:7, 0:width]
    g_gain = jnp.zeros((8, D), F32)
    g_shift = jnp.zeros((8, D), F32)
    g_sum = jnp.zeros((8, D), F32)
    g_bup = jnp.zeros((8, width), F32)

    def fold(values):
        return jnp.sum(values.reshape(values.shape[0] // 8, 8, values.shape[1]), axis=0)

    for p in range(n):
        rows = slice(p * TOK, (p + 1) * TOK)
        x = pieces[p][0:TOK, :].astype(F32)
        g = pieces[p][TOK : 2 * TOK, :]
        nhat, _ = normalized(x)
        norm = (nhat * gain + shift).astype(BF16)
        pre = mm_nn(norm, w_up[...]) + b_up
        cdf = 0.5 * (1.0 + lax.erf(pre * 0.7071067811865476))
        hidden = (pre * cdf).astype(BF16)
        slope = cdf + pre * (0.3989422804014327 * jnp.exp(-0.5 * pre * pre))
        dpre_f = mm_nt(g, w_down[...]) * slope
        dpre = dpre_f.astype(BF16)
        acc_o[rows, :] = mm_nn(hidden, w_down[...]).astype(acc_o.dtype)
        dnorm = mm_nt(dpre, w_up[...])
        acc_d[rows, :] = (dnorm * gain).astype(acc_d.dtype)
        g_gain += fold(dnorm * nhat)
        g_shift += fold(dnorm)
        g_sum += fold(g.astype(F32))
        g_bup += fold(dpre.astype(F32))
        norms[rows, :] = norm
        hiddens[rows, :] = hidden
        dpres[rows, :] = dpre
        gs[rows, :] = g
    vec[...] = jnp.zeros_like(vec)
    vec[2:3, :] = jnp.sum(g_gain, axis=0, keepdims=True)
    vec[3:4, :] = jnp.sum(g_shift, axis=0, keepdims=True)
    vec[4:5, :] = jnp.sum(g_sum, axis=0, keepdims=True)
    vec[6:7, 0:width] = jnp.sum(g_bup, axis=0, keepdims=True)
    up_t = mm_tn(dpres[...], norms[...])
    grad_up[...] = up_t.T.astype(BF16)
    grad_down[...] = mm_tn(hiddens[...], gs[...]).astype(BF16)
    if fast:
        for k in range(nz):
            z = zed ^ k
            pays[k][:, 0:256] = grad_up[pl.ds(pl.multiple_of(z * 128, 128), 128), :]
            rows = pl.ds(pl.multiple_of(z * 64, 64), 64)
            pays[k][0:64, 256:512] = grad_down[rows, 0:256]
            pays[k][64:128, 256:512] = grad_down[rows, 256:512]
    else:
        pays[0][...] = grad_up[...]
        pays[1][...] = grad_down[...]


def attn_body(n, nz, fast, order_list, place, order, *refs):
    seq = n * TOK
    qblk = min(256, seq)
    pieces = refs[:n]
    n_w = nz if fast else 1
    weights = refs[n : n + n_w]
    w_out, params, acc_o, acc_d, vec_in, cos_t, sin_t = refs[n + n_w : n + n_w + 7]
    outs = refs[n + n_w + 7 :]
    n_pay = nz if fast else 2
    keep_pay, send_pay, g_out = outs[:3]
    pays = outs[3 : 3 + n_pay]
    (w_all, norms, nhats, raw, qs, ks, vs, dms, mixs, dks, dvs, dqs, dqkvs, mixn, dqkvn, gs, grad_w, vec) = outs[3 + n_pay :]
    zed = place[1]
    if fast:
        for k in range(nz):
            w_all[pl.ds(pl.multiple_of((zed ^ k) * 128, 128), 128), :] = weights[k][...]
    else:
        w_all[...] = weights[0][...]
    gain, shift = params[0:1, :], params[1:2, :]
    bias = params[5:6, 0:256]

    def sorted_rows(block):
        return pl.ds(pl.multiple_of(order[block] * HALF, HALF), HALF)

    for p in range(n):
        rows = slice(p * TOK, (p + 1) * TOK)
        nhat, _ = normalized(pieces[p][0:TOK, :].astype(F32))
        g = pieces[p][TOK : 2 * TOK, :]
        norm = (nhat * gain + shift).astype(BF16)
        nhats[rows, :] = nhat
        norms[rows, :] = norm
        gs[rows, :] = g
        qkv = mm_nn(norm, w_all[...]) + bias
        dmix = mm_nt(g, w_out[...]).astype(BF16)
        for h in range(TOK // HALF):
            here = slice(h * HALF, (h + 1) * HALF)
            where = sorted_rows(p * (TOK // HALF) + h)
            raw[where, :] = qkv[here, :]
            dms[where, :] = dmix[here, :]

    lanes = lax.broadcasted_iota(jnp.int32, (qblk, 128), 1) % 64

    def swapped(t):
        return jnp.where(lanes < ROT // 2, pltpu.roll(t, 128 - ROT // 2, 1), pltpu.roll(t, ROT // 2, 1))

    for i in range(seq // qblk):
        rows = slice(i * qblk, (i + 1) * qblk)
        qk = raw[rows, 0:128]
        turned = (qk * cos_t[rows, :] + swapped(qk) * sin_t[rows, :]).astype(BF16)
        qs[rows, :] = turned[:, 0:64]
        ks[rows, :] = turned[:, 64:128]
        vs[rows, :] = raw[rows, 128:192].astype(BF16)

    dks[...] = jnp.zeros_like(dks)
    dvs[...] = jnp.zeros_like(dvs)
    for i in range(seq // qblk):
        rows = slice(i * qblk, (i + 1) * qblk)
        span = (i + 1) * qblk
        q = qs[rows, :]
        keys = ks[0:span, :]
        values = vs[0:span, :]
        s = mm_nt(q, keys) * 0.125
        q_at = lax.broadcasted_iota(jnp.int32, (qblk, span), 0) + i * qblk
        k_at = lax.broadcasted_iota(jnp.int32, (qblk, span), 1)
        s = jnp.where(q_at >= k_at, s, -1e30)
        top = jnp.max(s, axis=1, keepdims=True)
        e = jnp.exp(s - top)
        prob = e * (1.0 / jnp.sum(e, axis=1, keepdims=True))
        prob_b = prob.astype(BF16)
        mix = mm_nn(prob_b, values)
        mixs[rows, :] = mix.astype(BF16)
        dmix = dms[rows, :]
        delta = jnp.sum(dmix.astype(F32) * mix, axis=1, keepdims=True)
        dprob = mm_nt(dmix, values)
        ds = (prob * (dprob - delta)).astype(BF16)
        dqs[rows, 0:64] = mm_nn(ds, keys) * 0.125
        dks[:, 0:span] += mm_tn(q, ds)
        dvs[:, 0:span] += mm_tn(dmix, prob_b)
    dqs[:, 64:128] = dks[...].T * 0.125
    dqkvs[:, 128:192] = dvs[...].T.astype(BF16)
    dqkvs[:, 192:256] = jnp.zeros((seq, 64), BF16)
    for i in range(seq // qblk):
        rows = slice(i * qblk, (i + 1) * qblk)
        dqk = dqs[rows, :]
        dqkvs[rows, 0:128] = (dqk * cos_t[rows, :] - swapped(dqk) * sin_t[rows, :]).astype(BF16)

    scale = None
    if n > HEADS:
        scale = jnp.where(place[0] % (n // HEADS) == 0, 1.0, 0.0).astype(BF16)
    for b in range(seq // HALF):
        here = slice(b * HALF, (b + 1) * HALF)
        where = sorted_rows(b)
        mix, dqkv = mixs[where, :], dqkvs[where, :]
        if scale is not None:
            mix, dqkv = mix * scale, dqkv * scale
        mixn[here, :] = mix
        dqkvn[here, :] = dqkv

    g_gain = jnp.zeros((8, D), F32)
    g_shift = jnp.zeros((8, D), F32)
    g_bias = jnp.zeros((8, 256), F32)

    def fold(values):
        return jnp.sum(values.reshape(values.shape[0] // 8, 8, values.shape[1]), axis=0)

    for at, rel in enumerate(order_list):
        rows = slice(at * TOK, (at + 1) * TOK)
        dqkv = dqkvn[rows, :]
        part_o = mm_nn(mixn[rows, :], w_out[...]) + acc_o[rows, :].astype(F32)
        dnorm = mm_nt(dqkv, w_all[...])
        part_d = dnorm * gain + acc_d[rows, :].astype(F32)
        g_gain += fold(dnorm * nhats[rows, :])
        g_shift += fold(dnorm)
        g_bias += fold(dqkv.astype(F32))
        target = send_pay if rel % 2 else keep_pay
        target[rel // 2, :, 0:512] = part_o.astype(BF16)
        target[rel // 2, :, 512:1024] = part_d.astype(BF16)
    vec[...] = vec_in[...]
    vec[0:1, :] = jnp.sum(g_gain, axis=0, keepdims=True)
    vec[1:2, :] = jnp.sum(g_shift, axis=0, keepdims=True)
    vec[5:6, 0:256] = jnp.sum(g_bias, axis=0, keepdims=True)
    grad_w[...] = mm_tn(dqkvn[...], norms[...]).T.astype(BF16)
    g_out[...] = mm_tn(mixn[...], gs[...]).astype(BF16)
    if fast:
        tail = jnp.concatenate([vec[...], jnp.zeros((8, D), F32)], axis=0).astype(BF16)
        for k in range(nz):
            rows = pl.ds(pl.multiple_of((zed ^ k) * 128, 128), 128)
            pays[k][0:128, :] = grad_w[rows, :]
            pays[k][128:144, :] = tail[:, 0:256]
            pays[k][144:160, :] = tail[:, 256:512]
    else:
        pays[0][...] = grad_w[...]
        pays[1][...] = vec[...]


def close_body(place, x_ref, g_ref, params, *refs):
    parts, out, grad = refs[:-2], refs[-2], refs[-1]
    x = x_ref[...].astype(F32)
    nhat, inv = normalized(x)
    total = parts[0][...].astype(F32)
    for part in parts[1:]:
        total = total + part[...].astype(F32)
    out[...] = (x + total[:, 0:512] + params[4:5, :]).astype(BF16)
    dn = total[:, 512:1024]
    lead = jnp.mean(dn, axis=-1, keepdims=True)
    along = jnp.mean(dn * nhat, axis=-1, keepdims=True)
    grad[...] = g_ref[...].astype(F32) + inv * (dn - lead - nhat * along)


def sum_body(n_parts, *refs):
    out = refs[n_parts]
    total = refs[0][...].astype(F32)
    for ref in refs[1:n_parts]:
        total = total + ref[...].astype(F32)
    out[...] = total.astype(BF16)


def finish_body(n, nz, place, *refs):
    ffs, atts, wos = refs[:n], refs[n : 2 * n], refs[2 * n : 3 * n]
    (ln1g, ln1b, gqkv, bqkv, gout, bout, ln2g, ln2b, gup, bup, gdown, bdown) = refs[3 * n : 3 * n + 12]
    held_u, held_d, held_a, held_v, flat = refs[3 * n + 12 :]
    me, zed = place[0], place[1]
    span = FF // nz
    total = jnp.zeros((8, D), F32)
    for k in range(n):
        who = me ^ k
        held_u[who] = ffs[k][:, 0:256].astype(F32)
        rows = pl.ds(pl.multiple_of(who * 64, 64), 64)
        gdown[rows, 0:256] = ffs[k][0:64, 256:512].astype(F32)
        gdown[rows, 256:512] = ffs[k][64:128, 256:512].astype(F32)
        held_a[who] = atts[k][0:128, :].astype(F32)
        small = jnp.concatenate([atts[k][128:144, :].astype(F32)[0:8], atts[k][144:160, :].astype(F32)[0:8]], axis=1)
        held_v[who] = small
        total = total + small
    for h in range(0, n, 2):
        even, later = held_a[h], held_a[h + 1]
        low = low_lanes((128, 128))
        at = h * 64
        gqkv[:, at : at + 128] = jnp.where(low, even[:, 0:128], pltpu.roll(later[:, 0:128], 64, 1))
        gqkv[:, D + at : D + at + 128] = jnp.where(low, pltpu.roll(even[:, 0:128], 64, 1), later[:, 0:128])
        gqkv[:, 2 * D + at : 2 * D + at + 128] = jnp.where(low, even[:, 128:256], pltpu.roll(later[:, 128:256], 64, 1))
        for z in range(0, nz, 2):
            lanes = slice(z * 64, z * 64 + 128)
            e, l = held_u[h][:, lanes], held_u[h + 1][:, lanes]
            gup[:, z * span + at : z * span + at + 128] = jnp.where(low, e, pltpu.roll(l, 64, 1))
            gup[:, (z + 1) * span + at : (z + 1) * span + at + 128] = jnp.where(low, pltpu.roll(e, 64, 1), l)
        low = low_lanes((1, 128))
        e, l = held_v[h], held_v[h + 1]
        flat[h // 2 : h // 2 + 1, :] = jnp.where(low, e[5:6, 0:128], pltpu.roll(l[5:6, 0:128], 64, 1))
        flat[4 + h // 2 : 5 + h // 2, :] = jnp.where(low, pltpu.roll(e[5:6, 0:128], 64, 1), l[5:6, 0:128])
        flat[8 + h // 2 : 9 + h // 2, :] = jnp.where(low, e[5:6, 128:256], pltpu.roll(l[5:6, 128:256], 64, 1))
        lane = pl.ds(pl.multiple_of((zed // 2) * 128, 128), 128)
        odd = (zed % 2) == 1
        e = half_pick(held_v[h, 6:7, lane], odd, False)
        l = half_pick(held_v[h + 1, 6:7, lane], odd, True)
        bup[:, at : at + 128] = jnp.where(low, e, l)
    mine = pl.multiple_of((me % 2) * 64, 64)
    other = pl.multiple_of((1 - me % 2) * 64, 64)
    for parity, start in ((0, mine), (1, other)):
        acc = wos[parity][...].astype(F32)
        for k in range(parity + 2, n, 2):
            acc = acc + wos[k][...].astype(F32)
        gout[pl.ds(start, 64), :] = acc
    flat[12:20, :] = jnp.zeros((8, 128), F32)
    for r in range(3):
        bqkv[:, r * 128 : (r + 1) * 128] = flat[pl.ds(zed * 3 + r, 1), :]
    held_v[0] = total
    lane = pl.ds(pl.multiple_of(zed * 128, 128), 128)
    ln1g[...] = held_v[0, 0:1, lane]
    ln1b[...] = held_v[0, 1:2, lane]
    ln2g[...] = held_v[0, 2:3, lane]
    ln2b[...] = held_v[0, 3:4, lane]
    held_v[1] = total * (1.0 / n)
    bout[...] = held_v[1, 4:5, lane]
    bdown[...] = held_v[1, 4:5, lane]


def xor_pairs(size, k):
    return [(i, i ^ k) for i in range(size)]


def gather_ctx(value, n):
    got = {0: value}
    for k in range(2, n, 2):
        got[k] = lax.ppermute(value, "ctx", xor_pairs(n, k))
    for k in range(0, n, 2):
        got[k + 1] = lax.ppermute(got[k], "ctx", xor_pairs(n, 1))
    return [got[k] for k in range(n)]


def gather_fsdp(value, nz):
    return [value] + [lax.ppermute(value, "fsdp", xor_pairs(nz, k)) for k in range(1, nz)]


def swap_fsdp(values, nz):
    return [values[0]] + [lax.ppermute(values[k], "fsdp", xor_pairs(nz, k)) for k in range(1, nz)]


def rotary_tables(seq):
    pos = np.arange(seq, dtype=np.float32)
    inverse = (np.float32(10000.0) ** (-np.arange(ROT // 2, dtype=np.float32) * np.float32(2.0) / np.float32(ROT))).astype(np.float32)
    angles = (pos[:, None] * inverse[None, :]).astype(np.float32).astype(np.float64)
    cos_t = np.ones((seq, 64), np.float32)
    sin_t = np.zeros((seq, 64), np.float32)
    half = ROT // 2
    cos_t[:, 0:half] = np.cos(angles)
    cos_t[:, half:ROT] = np.cos(angles)
    sin_t[:, 0:half] = -np.sin(angles)
    sin_t[:, half:ROT] = np.sin(angles)
    return np.concatenate([cos_t, cos_t], axis=1), np.concatenate([sin_t, sin_t], axis=1)


def shape(dims, dtype=F32):
    return jax.ShapeDtypeStruct(dims, dtype)


def per_device(
    n,
    nz,
    inputs,
    block_order,
    ln1_gain,
    ln1_bias,
    w_qkv,
    b_qkv,
    w_attn_out,
    b_attn_out,
    ln2_gain,
    ln2_bias,
    w_up,
    b_up,
    w_down,
    b_down,
    cotangent,
):
    fast = n == HEADS and nz * 2 == HEADS
    seq = n * TOK
    width = FF // n
    me = lax.axis_index("ctx").astype(jnp.int32)
    zed = lax.axis_index("fsdp").astype(jnp.int32)
    place = jnp.stack([me, zed])
    x, g = inputs[0], cotangent[0]
    piece = jnp.concatenate([x, g], axis=0)
    order_list = list(range(n))
    blocks = TOK // HALF
    chunk_at = (jnp.arange(n, dtype=jnp.int32) ^ me)[:, None] * blocks + jnp.arange(blocks, dtype=jnp.int32)[None, :]
    pick = chunk_at.reshape(-1)[:, None] == jnp.arange(n * blocks, dtype=jnp.int32)[None, :]
    order = jnp.sum(jnp.where(pick, block_order[None, :], 0), axis=1).astype(jnp.int32)
    cos_t, sin_t = rotary_tables(seq)

    pieces = gather_ctx(piece, n)
    if fast:
        pack_a, pack_b, pack_w = vmem_call(
            functools.partial(pack_body, nz),
            (shape((D // nz, 256), BF16), shape((D // nz, 512), BF16), shape((HEAD_DIM, D), BF16)),
            n_smem=1,
            n_in=4,
            name="pack",
        )(place, w_qkv, w_up, w_down, w_attn_out)
        flat = jnp.concatenate([ln1_gain, ln1_bias, ln2_gain, ln2_bias, b_attn_out, b_down, b_qkv, b_up])
        rows = flat.shape[0] // 128
        flat = jnp.pad(flat.reshape(rows, 128), ((0, 16 - rows), (0, 0)))
        small = gather_fsdp(flat, nz)
        ff_w = gather_fsdp(pack_b, nz)
        attn_w = gather_fsdp(pack_a, nz)
        pairs = []
        for c in range(n):
            for z in range(nz):
                pairs.append((c * nz + z, (2 * z + c % 2) * nz + c // 2))
        head_w = lax.ppermute(pack_w, ("ctx", "fsdp"), pairs)
        params = vmem_call(
            functools.partial(small_body, nz),
            shape((8, D)),
            scratch=[pltpu.VMEM((nz, 16, 128), F32)],
            n_smem=1,
            n_in=nz,
            name="small",
        )(place, *small)
    else:
        whole = [
            lax.all_gather(v, "fsdp", axis=0, tiled=True)
            for v in (ln1_gain, ln1_bias, ln2_gain, ln2_bias, b_attn_out, b_down, b_qkv, b_up)
        ]
        whole = [v.astype(F32) for v in whole]
        head = me // (n // HEADS)
        bq = lax.dynamic_index_in_dim(whole[6].reshape(3, HEADS, HEAD_DIM), head, 1, False).reshape(-1)
        bu = lax.dynamic_index_in_dim(whole[7].reshape(n, width), me, 0, False)
        params = jnp.stack(
            [whole[0], whole[1], whole[2], whole[3], whole[4] + whole[5]]
            + [jnp.pad(bq, (0, D - 3 * HEAD_DIM)), jnp.pad(bu, (0, D - width)), jnp.zeros((D,), F32)]
        )
        wq = lax.dynamic_index_in_dim(w_qkv.reshape(-1, 3, HEADS, HEAD_DIM), head, 2, False).reshape(-1, 3 * HEAD_DIM)
        attn_w = [jnp.pad(lax.all_gather(wq, "fsdp", axis=0, tiled=True), ((0, 0), (0, 64)))]
        wu = lax.dynamic_slice_in_dim(w_up, me * width, width, 1)
        wd = lax.all_gather(w_down, "fsdp", axis=0, tiled=True)
        ff_w = [lax.all_gather(wu, "fsdp", axis=0, tiled=True), lax.dynamic_slice_in_dim(wd, me * width, width, 0)]
        wo = lax.all_gather(w_attn_out, "fsdp", axis=0, tiled=True)
        head_w = lax.dynamic_slice_in_dim(wo, head * HEAD_DIM, HEAD_DIM, 0)

    ff_pays = [shape((D // nz, 512), BF16)] * nz if fast else [shape((D, width), BF16), shape((width, D), BF16)]
    ff_out = vmem_call(
        functools.partial(ff_body, n, nz, fast),
        [shape((seq, D), BF16), shape((seq, D), BF16), shape((8, D))] + ff_pays,
        scratch=[
            pltpu.VMEM((D, width), BF16),
            pltpu.VMEM((width, D), BF16),
            pltpu.VMEM((seq, D), BF16),
            pltpu.VMEM((seq, width), BF16),
            pltpu.VMEM((seq, width), BF16),
            pltpu.VMEM((seq, D), BF16),
            pltpu.VMEM((D, width), BF16),
            pltpu.VMEM((width, D), BF16),
        ],
        n_smem=1,
        n_in=n + len(ff_w) + 1,
        cost=pl.CostEstimate(flops=12 * seq * D * width, bytes_accessed=8 * seq * D, transcendentals=2 * seq * width),
        name="feed_forward",
    )(place, *pieces, *ff_w, params)
    acc_o, acc_d, vec_ff = ff_out[:3]
    ff_pay = ff_out[3:]
    if fast:
        ff_got = swap_fsdp(ff_pay, nz)

    attn_pays = [shape((D // nz + 32, 256), BF16)] * nz if fast else [shape((D, 256), BF16), shape((8, D))]
    half = (n // 2, TOK, 2 * D)
    attn_out = vmem_call(
        functools.partial(attn_body, n, nz, fast, order_list),
        [shape(half, BF16), shape(half, BF16), shape((HEAD_DIM, D), BF16)] + attn_pays,
        scratch=[
            pltpu.VMEM((D, 256), BF16),
            pltpu.VMEM((seq, D), BF16),
            pltpu.VMEM((seq, D), F32),
            pltpu.VMEM((seq, 256), F32),
            pltpu.VMEM((seq, 64), BF16),
            pltpu.VMEM((seq, 64), BF16),
            pltpu.VMEM((seq, 64), BF16),
            pltpu.VMEM((seq, 64), BF16),
            pltpu.VMEM((seq, 64), BF16),
            pltpu.VMEM((64, seq), F32),
            pltpu.VMEM((64, seq), F32),
            pltpu.VMEM((seq, 128), F32),
            pltpu.VMEM((seq, 256), BF16),
            pltpu.VMEM((seq, 64), BF16),
            pltpu.VMEM((seq, 256), BF16),
            pltpu.VMEM((seq, D), BF16),
            pltpu.VMEM((D, 256), BF16),
            pltpu.VMEM((8, D), F32),
        ],
        n_smem=2,
        n_in=n + len(attn_w) + 7,
        cost=pl.CostEstimate(flops=14 * seq * seq * 64, bytes_accessed=12 * seq * D, transcendentals=seq * seq),
        name="attention",
    )(place, order, *pieces, *attn_w, head_w, params, acc_o, acc_d, vec_ff, cos_t, sin_t)
    keep_pay, send_pay, g_out = attn_out[:3]
    attn_pay = attn_out[3:]

    came = lax.ppermute(send_pay, "ctx", xor_pairs(n, 1))
    chip_sum = (keep_pay.astype(F32) + came.astype(F32)).astype(BF16)
    parts = [chip_sum[0]] + [lax.ppermute(chip_sum[k // 2], "ctx", xor_pairs(n, k)) for k in range(2, n, 2)]
    output, grad_inputs = vmem_call(
        close_body,
        (shape((TOK, D), BF16), shape((TOK, D))),
        n_smem=1,
        n_in=3 + len(parts),
        name="close",
    )(place, x, g, params, *parts)

    if fast:
        back = []
        for c in range(n):
            for z in range(nz):
                back.append(((2 * z + c % 2) * nz + c // 2, c * nz + z))
        out_got = lax.ppermute(g_out, ("ctx", "fsdp"), back)
        attn_got = swap_fsdp(attn_pay, nz)
        ff_sum = vmem_call(functools.partial(sum_body, nz), shape(ff_pay[0].shape, BF16), n_in=nz, name="sum_ff")(*ff_got)
        attn_sum = vmem_call(functools.partial(sum_body, nz), shape(attn_pay[0].shape, BF16), n_in=nz, name="sum_attn")(
            *attn_got
        )
        ff_all = gather_ctx(ff_sum, n)
        out_all = gather_ctx(out_got, n)
        attn_all = gather_ctx(attn_sum, n)
        dz = D // nz
        outs = vmem_call(
            functools.partial(finish_body, n, nz),
            [
                shape((1, dz)),
                shape((1, dz)),
                shape((dz, 3 * D)),
                shape((1, 3 * dz)),
                shape((dz, D)),
                shape((1, dz)),
                shape((1, dz)),
                shape((1, dz)),
                shape((dz, FF)),
                shape((1, FF // nz)),
                shape((FF // nz, D)),
                shape((1, dz)),
            ],
            scratch=[
                pltpu.VMEM((n, 128, 256), F32),
                pltpu.VMEM((8, 128), F32),
                pltpu.VMEM((n, 128, 256), F32),
                pltpu.VMEM((n, 8, D), F32),
                pltpu.VMEM((24, 128), F32),
            ],
            n_smem=1,
            n_in=3 * n,
            name="finish",
        )(place, *ff_all, *attn_all, *out_all)
        outs = [o.reshape(-1) if o.shape[0] == 1 else o for o in outs]
    else:
        everyone = ("ctx", "fsdp")
        head = me // (n // HEADS)
        g_up, g_down = ff_pay
        g_qkv, vec = attn_pay

        def own(full, axis=0):
            size = full.shape[axis] // nz
            return lax.dynamic_slice_in_dim(full, zed * size, size, axis)

        def spread(part, dims, index, axis):
            full = jnp.zeros(dims, part.dtype)
            return lax.psum(lax.dynamic_update_index_in_dim(full, part, index, axis), everyone).astype(F32)

        qkv_full = spread(g_qkv[:, 0:192].reshape(D, 3, HEAD_DIM), (D, 3, HEADS, HEAD_DIM), head, 2).reshape(D, 3 * D)
        out_full = spread(g_out, (HEADS, HEAD_DIM, D), head, 0).reshape(D, D)
        up_full = spread(g_up, (D, n, width), me, 1).reshape(D, FF)
        down_full = spread(g_down, (n, width, D), me, 0).reshape(FF, D)
        bq_full = spread(vec[5, 0:192].reshape(3, HEAD_DIM), (3, HEADS, HEAD_DIM), head, 1).reshape(3 * D)
        bu_full = spread(vec[6, 0:width], (n, width), me, 0).reshape(FF)
        flat = lax.psum(vec, everyone)
        b_full = flat[4] * (1.0 / n)
        outs = [own(v) for v in (flat[0], flat[1], qkv_full, bq_full, out_full, b_full)]
        outs += [own(v) for v in (flat[2], flat[3], up_full, bu_full, down_full, b_full)]
    return (output[None], grad_inputs[None], *outs)


def solution(mesh):
    rows, flat, tokens = P("fsdp", None), P("fsdp"), P("fsdp", "ctx", None)
    weights = (flat, flat, rows, flat, rows, flat, flat, flat, rows, flat, rows, flat)
    return jax.shard_map(
        functools.partial(per_device, mesh.shape["ctx"], mesh.shape["fsdp"]),
        mesh=mesh,
        in_specs=(tokens, P(), *weights, tokens),
        out_specs=(tokens, tokens, *weights),
        check_vma=False,
    )
```

```python
import functools

import jax
import jax.numpy as jnp
import numpy as np
from jax import lax
from jax.experimental import pallas as pl
from jax.experimental.pallas import tpu as pltpu
from jax.sharding import PartitionSpec as P

HEADS = 8
HEAD_DIM = 64
D = 512
FF = 2048
ROT = 16
HALF = 64
TOK = 128
EPS = 1e-05
F32 = jnp.float32
BF16 = jnp.bfloat16
VMEM_LIMIT = 32 * 1024 * 1024
WIDE_LIMIT = 60 * 1024 * 1024


def mm(left, right, dims):
    return lax.dot_general(left, right, (dims, ((), ())), preferred_element_type=F32)


def mm_nn(left, right):
    return mm(left, right, ((1,), (0,)))


def mm_nt(left, right):
    return mm(left, right, ((1,), (1,)))


def mm_tn(left, right):
    return mm(left, right, ((0,), (0,)))


def vmem_call(body, out_shape, scratch=(), n_smem=0, n_in=0, n_any=0, cost=None, name=None):
    smem = pl.BlockSpec(memory_space=pltpu.SMEM)
    vmem = pl.BlockSpec(memory_space=pltpu.VMEM)
    return pl.pallas_call(
        body,
        out_shape=out_shape,
        in_specs=[smem] * n_smem + [vmem] * n_in + [pl.BlockSpec(memory_space=pl.ANY)] * n_any,
        out_specs=jax.tree.map(lambda _: vmem, out_shape),
        scratch_shapes=list(scratch),
        compiler_params=pltpu.CompilerParams(vmem_limit_bytes=VMEM_LIMIT),
        cost_estimate=cost,
        name=name,
    )


def half_pick(block, odd, to_upper):
    moved = pltpu.roll(block, 64, 1)
    return jnp.where(odd, block if to_upper else moved, moved if to_upper else block)


def low_lanes(shape):
    return lax.broadcasted_iota(jnp.int32, shape, len(shape) - 1) % 128 < 64


def pack_body(nz, place, *refs):
    q_ref, k_ref, v_ref = refs[:3]
    ups = refs[3 : 3 + nz]
    w_down, x, g = refs[3 + nz : 6 + nz]
    vectors = refs[6 + nz : 14 + nz]
    pay, piece, small = refs[14 + nz :]
    odd = (place[0] % 2) == 1
    rows = q_ref.shape[0]
    low = low_lanes((rows, 128))
    small[...] = jnp.zeros_like(small)
    at = 0
    for vector in vectors:
        for r in range(vector.shape[0] // 128):
            small[at : at + 1, :] = vector[r * 128 : (r + 1) * 128].astype(F32).reshape(1, 128)
            at += 1
    few = small[...]
    spare = jnp.concatenate([pltpu.roll(few, 64, 1), few, jnp.zeros((rows - 32, 128), F32)], axis=0)
    q = half_pick(q_ref[...].astype(F32), odd, False)
    k = half_pick(k_ref[...].astype(F32), odd, True)
    v = half_pick(v_ref[...].astype(F32), odd, False)
    pay[:, 0:128] = jnp.where(low, q, k).astype(BF16)
    pay[:, 128:256] = jnp.where(low, v, spare).astype(BF16)
    for z in range(0, nz, 2):
        even = half_pick(ups[z][...].astype(F32), odd, False)
        later = half_pick(ups[z + 1][...].astype(F32), odd, True)
        pay[:, 256 + z * 64 : 256 + z * 64 + 128] = jnp.where(low, even, later).astype(BF16)
    pay[0:64, 512:768] = w_down[:, 0:256]
    pay[64:128, 512:768] = w_down[:, 256:512]
    piece[0:TOK, :] = x[0]
    piece[TOK : 2 * TOK, :] = g[0]


def later_body(place, pay, w_out, after, again, head_w):
    again[...] = pay[...]
    head_w[...] = w_out[...]


def later_call(place, pay, w_out, after):
    outs = [shape(pay.shape, BF16), shape((HEAD_DIM, D), BF16)]
    return pl.pallas_call(
        later_body,
        out_shape=outs,
        grid_spec=pltpu.PrefetchScalarGridSpec(
            num_scalar_prefetch=1,
            grid=(1,),
            in_specs=[
                pl.BlockSpec(pay.shape, lambda i, s: (0, 0)),
                pl.BlockSpec((HEAD_DIM, D), lambda i, s: (s[0] % 2, 0)),
                pl.BlockSpec(memory_space=pl.ANY),
            ],
            out_specs=[pl.BlockSpec(o.shape, lambda i, s: (0, 0)) for o in outs],
        ),
        compiler_params=pltpu.CompilerParams(vmem_limit_bytes=VMEM_LIMIT),
        name="later",
    )(place, pay, w_out, after)


def pack_call(nz, place, w_qkv, w_up, w_down, x, g, vectors):
    span = FF // nz // 128
    rows = D // nz

    def lane_block(first):
        return pl.BlockSpec((rows, 128), lambda i, s: (0, first + s[0] // 2))

    def whole(array):
        rank = array.ndim
        return pl.BlockSpec(array.shape, lambda i, s: (0,) * rank)

    outs = [shape((rows, 768), BF16), shape((2 * TOK, D), BF16)]
    return pl.pallas_call(
        functools.partial(pack_body, nz),
        out_shape=outs,
        grid_spec=pltpu.PrefetchScalarGridSpec(
            num_scalar_prefetch=1,
            grid=(1,),
            in_specs=[lane_block(0), lane_block(D // 128), lane_block(2 * D // 128)]
            + [lane_block(z * span) for z in range(nz)]
            + [
                pl.BlockSpec((64, D), lambda i, s: (s[0], 0)),
                whole(x),
                whole(g),
            ]
            + [whole(v) for v in vectors],
            out_specs=[whole(o) for o in outs],
            scratch_shapes=[pltpu.VMEM((16, 128), F32)],
        ),
        compiler_params=pltpu.CompilerParams(vmem_limit_bytes=WIDE_LIMIT),
        name="pack",
    )(place, w_qkv, w_qkv, w_qkv, *([w_up] * nz), w_down, x, g, *vectors)


def unpack(nz, place, pieces, w_all, w_up, w_down, params, held):
    me, zed = place[0], place[1]
    pair = me // 2
    odd = (me % 2) == 1
    for k in range(nz):
        z = zed ^ k
        tall = pl.ds(pl.multiple_of(z * 128, 128), 128)
        flat = pl.ds(pl.multiple_of(z * 64, 64), 64)
        w_all[tall, 0:128] = pieces[k][:, 0:128]
        third = pieces[k][:, 128:256].astype(F32)
        w_all[tall, 128:256] = jnp.where(low_lanes((128, 128)), third, 0.0).astype(BF16)
        held[z] = jnp.where(low_lanes((16, 128)), pltpu.roll(third[0:16], 64, 1), third[16:32])
        w_up[tall, :] = pieces[k][:, 256:512]
        w_down[flat, 0:256] = pieces[k][0:64, 512:768]
        w_down[flat, 256:512] = pieces[k][64:128, 512:768]
    params[...] = jnp.zeros_like(params)
    for z in range(nz):
        lanes = slice(z * 128, (z + 1) * 128)
        params[0:4, lanes] = held[z, 0:4, :]
        params[4:5, lanes] = held[z, 4:5, :] + held[z, 5:6, :]
    low = low_lanes((1, 128))

    def qkv_row(group):
        index = group * 4 + pair
        z = index // 3
        return held[z, pl.ds(6 + index - 3 * z, 1), :]

    q = half_pick(qkv_row(0), odd, False)
    k = half_pick(qkv_row(1), odd, True)
    v = half_pick(qkv_row(2), odd, False)
    params[5:6, 0:128] = jnp.where(low, q, k)
    params[5:6, 128:256] = jnp.where(low, v, 0.0)
    for z in range(0, nz, 2):
        even = half_pick(held[z, pl.ds(9 + pair, 1), :], odd, False)
        later = half_pick(held[z + 1, pl.ds(9 + pair, 1), :], odd, True)
        params[6:7, z * 64 : z * 64 + 128] = jnp.where(low, even, later)


def normalized(x):
    center = x - jnp.mean(x, axis=-1, keepdims=True)
    spread = jnp.mean(center * center, axis=-1, keepdims=True)
    inv = lax.rsqrt(spread + EPS)
    return center * inv, inv


def fold(values):
    return jnp.sum(values.reshape(values.shape[0] // 8, 8, values.shape[1]), axis=0)


def layer_body(n, nz, fast, place, order, *refs):
    seq = n * TOK
    qblk = min(256, seq)
    pieces = refs[:n]
    n_w = nz if fast else 4
    given = refs[n : n + n_w]
    w_out, cos_t, sin_t = refs[n + n_w : n + n_w + 3]
    outs = refs[n + n_w + 3 :]
    n_pay = nz if fast else 4
    keep_pay, send_pay, g_out, param_out = outs[:4]
    pays = outs[4 : 4 + n_pay]
    scratch = outs[4 + n_pay :]
    (w_all, w_up, w_down, params, held, spare) = scratch[:6]
    (norms, nhats, raw, qs, ks, vs, dms, mixs, dks, dvs, dqs, dqkvs, mixn, dqkvn, gs) = scratch[6:21]
    (norm2s, hiddens, dpres, grad_w, grad_up, grad_down, vec) = scratch[21:]
    width = w_up.shape[1]
    zed = place[1]
    if fast:
        unpack(nz, place, given, w_all, w_up, w_down, params, held)
    else:
        w_all[...] = given[0][...]
        w_up[...] = given[1][...]
        w_down[...] = given[2][...]
        params[...] = given[3][...]
    param_out[...] = params[...]
    gain, shift = params[0:1, :], params[1:2, :]
    gain2, shift2 = params[2:3, :], params[3:4, :]
    bias = params[5:6, 0:256]
    b_up = params[6:7, 0:width]

    def sorted_rows(block):
        return pl.ds(pl.multiple_of(order[block] * HALF, HALF), HALF)

    for p in range(n):
        rows = slice(p * TOK, (p + 1) * TOK)
        nhat, _ = normalized(pieces[p][0:TOK, :].astype(F32))
        g = pieces[p][TOK : 2 * TOK, :]
        norm = (nhat * gain + shift).astype(BF16)
        nhats[rows, :] = nhat
        norms[rows, :] = norm
        norm2s[rows, :] = (nhat * gain2 + shift2).astype(BF16)
        gs[rows, :] = g
        qkv = mm_nn(norm, w_all[...]) + bias
        dmix = mm_nt(g, w_out[...]).astype(BF16)
        for h in range(TOK // HALF):
            here = slice(h * HALF, (h + 1) * HALF)
            where = sorted_rows(p * (TOK // HALF) + h)
            raw[where, :] = qkv[here, :]
            dms[where, :] = dmix[here, :]

    lanes = lax.broadcasted_iota(jnp.int32, (qblk, 128), 1) % 64

    def swapped(t):
        return jnp.where(lanes < ROT // 2, pltpu.roll(t, 128 - ROT // 2, 1), pltpu.roll(t, ROT // 2, 1))

    for i in range(seq // qblk):
        rows = slice(i * qblk, (i + 1) * qblk)
        qk = raw[rows, 0:128]
        turned = (qk * cos_t[rows, :] + swapped(qk) * sin_t[rows, :]).astype(BF16)
        qs[rows, :] = turned[:, 0:64]
        ks[rows, :] = turned[:, 64:128]
        vs[rows, :] = raw[rows, 128:192].astype(BF16)

    dks[...] = jnp.zeros_like(dks)
    dvs[...] = jnp.zeros_like(dvs)
    for i in range(seq // qblk):
        rows = slice(i * qblk, (i + 1) * qblk)
        span = (i + 1) * qblk
        q = qs[rows, :]
        keys = ks[0:span, :]
        values = vs[0:span, :]
        s = mm_nt(q, keys) * 0.125
        q_at = lax.broadcasted_iota(jnp.int32, (qblk, span), 0) + i * qblk
        k_at = lax.broadcasted_iota(jnp.int32, (qblk, span), 1)
        s = jnp.where(q_at >= k_at, s, -1e30)
        top = jnp.max(s, axis=1, keepdims=True)
        e = jnp.exp(s - top)
        prob = e * (1.0 / jnp.sum(e, axis=1, keepdims=True))
        prob_b = prob.astype(BF16)
        mix = mm_nn(prob_b, values)
        mixs[rows, :] = mix.astype(BF16)
        dmix = dms[rows, :]
        delta = jnp.sum(dmix.astype(F32) * mix, axis=1, keepdims=True)
        dprob = mm_nt(dmix, values)
        ds = (prob * (dprob - delta)).astype(BF16)
        dqs[rows, 0:64] = mm_nn(ds, keys) * 0.125
        dks[:, 0:span] += mm_tn(q, ds)
        dvs[:, 0:span] += mm_tn(dmix, prob_b)
    dqs[:, 64:128] = dks[...].T * 0.125
    dqkvs[:, 128:192] = dvs[...].T.astype(BF16)
    dqkvs[:, 192:256] = jnp.zeros((seq, 64), BF16)
    for i in range(seq // qblk):
        rows = slice(i * qblk, (i + 1) * qblk)
        dqk = dqs[rows, :]
        dqkvs[rows, 0:128] = (dqk * cos_t[rows, :] - swapped(dqk) * sin_t[rows, :]).astype(BF16)

    scale = None
    if n > HEADS:
        scale = jnp.where(place[0] % (n // HEADS) == 0, 1.0, 0.0).astype(BF16)
    for b in range(seq // HALF):
        here = slice(b * HALF, (b + 1) * HALF)
        where = sorted_rows(b)
        mix, dqkv = mixs[where, :], dqkvs[where, :]
        if scale is not None:
            mix, dqkv = mix * scale, dqkv * scale
        mixn[here, :] = mix
        dqkvn[here, :] = dqkv

    g_gain = jnp.zeros((8, D), F32)
    g_shift = jnp.zeros((8, D), F32)
    g_bias = jnp.zeros((8, 256), F32)
    g_gain2 = jnp.zeros((8, D), F32)
    g_shift2 = jnp.zeros((8, D), F32)
    g_sum = jnp.zeros((8, D), F32)
    g_bup = jnp.zeros((8, width), F32)
    for p in range(n):
        rows = slice(p * TOK, (p + 1) * TOK)
        g, nhat = gs[rows, :], nhats[rows, :]
        pre = mm_nn(norm2s[rows, :], w_up[...]) + b_up
        cdf = 0.5 * (1.0 + lax.erf(pre * 0.7071067811865476))
        hidden = (pre * cdf).astype(BF16)
        slope = cdf + pre * (0.3989422804014327 * jnp.exp(-0.5 * pre * pre))
        dpre = (mm_nt(g, w_down[...]) * slope).astype(BF16)
        hiddens[rows, :] = hidden
        dpres[rows, :] = dpre
        dqkv = dqkvn[rows, :]
        part_o = mm_nn(hidden, w_down[...]) + mm_nn(mixn[rows, :], w_out[...])
        dnorm2 = mm_nt(dpre, w_up[...])
        dnorm = mm_nt(dqkv, w_all[...])
        g_gain += fold(dnorm * nhat)
        g_shift += fold(dnorm)
        g_bias += fold(dqkv.astype(F32))
        g_gain2 += fold(dnorm2 * nhat)
        g_shift2 += fold(dnorm2)
        g_sum += fold(g.astype(F32))
        g_bup += fold(dpre.astype(F32))
        target = send_pay if p % 2 else keep_pay
        target[p // 2, :, 0:512] = part_o.astype(BF16)
        target[p // 2, :, 512:1024] = (dnorm * gain + dnorm2 * gain2).astype(BF16)
    vec[...] = jnp.zeros_like(vec)
    for row, value in ((0, g_gain), (1, g_shift), (2, g_gain2), (3, g_shift2), (4, g_sum), (5, g_bias), (6, g_bup)):
        vec[row : row + 1, 0 : value.shape[1]] = jnp.sum(value, axis=0, keepdims=True)
    g_out[...] = mm_tn(mixn[...], gs[...]).astype(BF16)
    grad_w[...] = mm_tn(dqkvn[...], norms[...]).T
    grad_up[...] = mm_tn(dpres[...], norm2s[...]).T.astype(BF16)
    grad_down[...] = mm_tn(hiddens[...], gs[...]).astype(BF16)
    if fast:
        spare[...] = jnp.zeros_like(spare)
        for j in range(8):
            lanes_j = vec[:, (j // 2) * 128 : (j // 2) * 128 + 128]
            spare[8 * j : 8 * j + 8, :] = lanes_j if j % 2 else pltpu.roll(lanes_j, 64, 1)
        low = low_lanes((128, 128))
        for k in range(nz):
            z = zed ^ k
            tall = pl.ds(pl.multiple_of(z * 128, 128), 128)
            flat = pl.ds(pl.multiple_of(z * 64, 64), 64)
            pays[k][:, 0:128] = grad_w[tall, 0:128].astype(BF16)
            pays[k][:, 128:256] = jnp.where(low, grad_w[tall, 128:256], spare[...]).astype(BF16)
            pays[k][:, 256:512] = grad_up[tall, :]
            pays[k][0:64, 512:768] = grad_down[flat, 0:256]
            pays[k][64:128, 512:768] = grad_down[flat, 256:512]
    else:
        pays[0][...] = grad_w[...].astype(BF16)
        pays[1][...] = grad_up[...]
        pays[2][...] = grad_down[...]
        pays[3][...] = vec[...]


def close_body(place, x_ref, g_ref, params, *refs):
    parts, out, grad = refs[:-2], refs[-2], refs[-1]
    x = x_ref[...].astype(F32)
    nhat, inv = normalized(x)
    total = parts[0][...].astype(F32)
    for part in parts[1:]:
        total = total + part[...].astype(F32)
    out[...] = (x + total[:, 0:512] + params[4:5, :]).astype(BF16)
    dn = total[:, 512:1024]
    lead = jnp.mean(dn, axis=-1, keepdims=True)
    along = jnp.mean(dn * nhat, axis=-1, keepdims=True)
    grad[...] = g_ref[...].astype(F32) + inv * (dn - lead - nhat * along)


def chip_body(keep, came, *outs):
    for k, out in enumerate(outs):
        out[...] = (keep[k].astype(F32) + came[k].astype(F32)).astype(BF16)


def gate_body(value, after, out):
    out[...] = value[...]


def sum_body(nz, *refs):
    parts, g_out, out = refs[:nz], refs[nz], refs[-1]
    total = parts[0][...].astype(F32)
    for part in parts[1:]:
        total = total + part[...].astype(F32)
    out[:, 0:768] = total.astype(BF16)
    out[0:64, 768:1024] = g_out[:, 0:256]
    out[64:128, 768:1024] = g_out[:, 256:512]


def finish_body(n, nz, place, *refs):
    alls = refs[:n]
    (ln1g, ln1b, gqkv, bqkv, gout, bout, ln2g, ln2b, gup, bup, gdown, bdown) = refs[n : n + 12]
    held_u, held_a, held_v, flat = refs[n + 12 :]
    me, zed = place[0], place[1]
    span = FF // nz
    total = jnp.zeros((8, D), F32)
    wide = low_lanes((8, 128))
    for k in range(n):
        who = me ^ k
        held_a[who] = alls[k][:, 0:256].astype(F32)
        held_u[who] = alls[k][:, 256:512].astype(F32)
        rows = pl.ds(pl.multiple_of(who * 64, 64), 64)
        gdown[rows, 0:256] = alls[k][0:64, 512:768].astype(F32)
        gdown[rows, 256:512] = alls[k][64:128, 512:768].astype(F32)
        spare = alls[k][0:64, 128:256].astype(F32)
        small = []
        for j in range(0, 8, 2):
            small.append(jnp.where(wide, pltpu.roll(spare[8 * j : 8 * j + 8], 64, 1), spare[8 * j + 8 : 8 * j + 16]))
        small = jnp.concatenate(small, axis=1)
        held_v[who] = small
        total = total + small
    for h in range(0, n, 2):
        even, later = held_a[h], held_a[h + 1]
        low = low_lanes((128, 128))
        at = h * 64
        gqkv[:, at : at + 128] = jnp.where(low, even[:, 0:128], pltpu.roll(later[:, 0:128], 64, 1))
        gqkv[:, D + at : D + at + 128] = jnp.where(low, pltpu.roll(even[:, 0:128], 64, 1), later[:, 0:128])
        gqkv[:, 2 * D + at : 2 * D + at + 128] = jnp.where(low, even[:, 128:256], pltpu.roll(later[:, 128:256], 64, 1))
        for z in range(0, nz, 2):
            lanes = slice(z * 64, z * 64 + 128)
            e, l = held_u[h][:, lanes], held_u[h + 1][:, lanes]
            gup[:, z * span + at : z * span + at + 128] = jnp.where(low, e, pltpu.roll(l, 64, 1))
            gup[:, (z + 1) * span + at : (z + 1) * span + at + 128] = jnp.where(low, pltpu.roll(e, 64, 1), l)
        low = low_lanes((1, 128))
        e, l = held_v[h], held_v[h + 1]
        flat[h // 2 : h // 2 + 1, :] = jnp.where(low, e[5:6, 0:128], pltpu.roll(l[5:6, 0:128], 64, 1))
        flat[4 + h // 2 : 5 + h // 2, :] = jnp.where(low, pltpu.roll(e[5:6, 0:128], 64, 1), l[5:6, 0:128])
        flat[8 + h // 2 : 9 + h // 2, :] = jnp.where(low, e[5:6, 128:256], pltpu.roll(l[5:6, 128:256], 64, 1))
        lane = pl.ds(pl.multiple_of((zed // 2) * 128, 128), 128)
        odd = (zed % 2) == 1
        e = half_pick(held_v[h, 6:7, lane], odd, False)
        l = half_pick(held_v[h + 1, 6:7, lane], odd, True)
        bup[:, at : at + 128] = jnp.where(low, e, l)
    mine = pl.multiple_of((me % 2) * 64, 64)
    other = pl.multiple_of((1 - me % 2) * 64, 64)
    for parity, start in ((0, mine), (1, other)):
        acc = alls[parity][:, 768:1024].astype(F32)
        for k in range(parity + 2, n, 2):
            acc = acc + alls[k][:, 768:1024].astype(F32)
        gout[pl.ds(start, 64), 0:256] = acc[0:64]
        gout[pl.ds(start, 64), 256:512] = acc[64:128]
    flat[12:20, :] = jnp.zeros((8, 128), F32)
    for r in range(3):
        bqkv[:, r * 128 : (r + 1) * 128] = flat[pl.ds(zed * 3 + r, 1), :]
    held_v[0] = total
    lane = pl.ds(pl.multiple_of(zed * 128, 128), 128)
    ln1g[...] = held_v[0, 0:1, lane]
    ln1b[...] = held_v[0, 1:2, lane]
    ln2g[...] = held_v[0, 2:3, lane]
    ln2b[...] = held_v[0, 3:4, lane]
    held_v[1] = total * (1.0 / n)
    bout[...] = held_v[1, 4:5, lane]
    bdown[...] = held_v[1, 4:5, lane]


def xor_pairs(size, k):
    return [(i, i ^ k) for i in range(size)]


def gather_ctx(value, n):
    got = {0: value}
    for k in range(2, n, 2):
        got[k] = lax.ppermute(value, "ctx", xor_pairs(n, k))
    for k in range(0, n, 2):
        got[k + 1] = lax.ppermute(got[k], "ctx", xor_pairs(n, 1))
    return [got[k] for k in range(n)]


def gather_fsdp(value, nz):
    return [value] + [lax.ppermute(value, "fsdp", xor_pairs(nz, k)) for k in range(1, nz)]


def swap_fsdp(values, nz):
    return [values[0]] + [lax.ppermute(values[k], "fsdp", xor_pairs(nz, k)) for k in range(1, nz)]


def rotary_tables(seq):
    pos = np.arange(seq, dtype=np.float32)
    inverse = (np.float32(10000.0) ** (-np.arange(ROT // 2, dtype=np.float32) * np.float32(2.0) / np.float32(ROT))).astype(np.float32)
    angles = (pos[:, None] * inverse[None, :]).astype(np.float32).astype(np.float64)
    cos_t = np.ones((seq, 64), np.float32)
    sin_t = np.zeros((seq, 64), np.float32)
    half = ROT // 2
    cos_t[:, 0:half] = np.cos(angles)
    cos_t[:, half:ROT] = np.cos(angles)
    sin_t[:, 0:half] = -np.sin(angles)
    sin_t[:, half:ROT] = np.sin(angles)
    return np.concatenate([cos_t, cos_t], axis=1), np.concatenate([sin_t, sin_t], axis=1)


def shape(dims, dtype=F32):
    return jax.ShapeDtypeStruct(dims, dtype)


def per_device(
    n,
    nz,
    inputs,
    block_order,
    ln1_gain,
    ln1_bias,
    w_qkv,
    b_qkv,
    w_attn_out,
    b_attn_out,
    ln2_gain,
    ln2_bias,
    w_up,
    b_up,
    w_down,
    b_down,
    cotangent,
):
    fast = n == HEADS and nz * 2 == HEADS
    seq = n * TOK
    width = FF // n
    me = lax.axis_index("ctx").astype(jnp.int32)
    zed = lax.axis_index("fsdp").astype(jnp.int32)
    place = jnp.stack([me, zed])
    x, g = inputs[0], cotangent[0]
    blocks = TOK // HALF
    chunk_at = (jnp.arange(n, dtype=jnp.int32) ^ me)[:, None] * blocks + jnp.arange(blocks, dtype=jnp.int32)[None, :]
    pick = chunk_at.reshape(-1)[:, None] == jnp.arange(n * blocks, dtype=jnp.int32)[None, :]
    order = jnp.sum(jnp.where(pick, block_order[None, :], 0), axis=1).astype(jnp.int32)
    cos_t, sin_t = rotary_tables(seq)

    if fast:
        vectors = (ln1_gain, ln1_bias, ln2_gain, ln2_bias, b_attn_out, b_down, b_qkv, b_up)
        pack, piece = pack_call(nz, place, w_qkv, w_up, w_down, inputs, cotangent, vectors)
        pieces = gather_ctx(piece, n)
        near, pack_w = later_call(place, pack, w_attn_out, pieces[2])
        given = swap_fsdp([pack, near, pack, pack], nz)
        pairs = []
        for c in range(n):
            for z in range(nz):
                pairs.append((c * nz + z, (2 * z + c % 2) * nz + c // 2))
        head_w = lax.ppermute(pack_w, ("ctx", "fsdp"), pairs)
    else:
        whole = [
            lax.all_gather(v, "fsdp", axis=0, tiled=True)
            for v in (ln1_gain, ln1_bias, ln2_gain, ln2_bias, b_attn_out, b_down, b_qkv, b_up)
        ]
        whole = [v.astype(F32) for v in whole]
        head = me // (n // HEADS)
        bq = lax.dynamic_index_in_dim(whole[6].reshape(3, HEADS, HEAD_DIM), head, 1, False).reshape(-1)
        bu = lax.dynamic_index_in_dim(whole[7].reshape(n, width), me, 0, False)
        params = jnp.stack(
            [whole[0], whole[1], whole[2], whole[3], whole[4] + whole[5]]
            + [jnp.pad(bq, (0, D - 3 * HEAD_DIM)), jnp.pad(bu, (0, D - width)), jnp.zeros((D,), F32)]
        )
        wq = lax.dynamic_index_in_dim(w_qkv.reshape(-1, 3, HEADS, HEAD_DIM), head, 2, False).reshape(-1, 3 * HEAD_DIM)
        given = [jnp.pad(lax.all_gather(wq, "fsdp", axis=0, tiled=True), ((0, 0), (0, 64)))]
        wu = lax.dynamic_slice_in_dim(w_up, me * width, width, 1)
        wd = lax.all_gather(w_down, "fsdp", axis=0, tiled=True)
        given += [lax.all_gather(wu, "fsdp", axis=0, tiled=True), lax.dynamic_slice_in_dim(wd, me * width, width, 0)]
        wo = lax.all_gather(w_attn_out, "fsdp", axis=0, tiled=True)
        given.append(params)
        pieces = gather_ctx(jnp.concatenate([x, g], axis=0), n)
        head_w = lax.dynamic_slice_in_dim(wo, head * HEAD_DIM, HEAD_DIM, 0)

    if fast:
        pays = [shape((D // nz, 768), BF16)] * nz
    else:
        pays = [shape((D, 256), BF16), shape((D, width), BF16), shape((width, D), BF16), shape((8, D))]
    half = (n // 2, TOK, 2 * D)
    layer_out = vmem_call(
        functools.partial(layer_body, n, nz, fast),
        [shape(half, BF16), shape(half, BF16), shape((HEAD_DIM, D), BF16), shape((8, D))] + pays,
        scratch=[
            pltpu.VMEM((D, 256), BF16),
            pltpu.VMEM((D, width), BF16),
            pltpu.VMEM((width, D), BF16),
            pltpu.VMEM((8, D), F32),
            pltpu.VMEM((nz, 16, 128), F32),
            pltpu.VMEM((128, 128), F32),
            pltpu.VMEM((seq, D), BF16),
            pltpu.VMEM((seq, D), F32),
            pltpu.VMEM((seq, 256), F32),
            pltpu.VMEM((seq, 64), BF16),
            pltpu.VMEM((seq, 64), BF16),
            pltpu.VMEM((seq, 64), BF16),
            pltpu.VMEM((seq, 64), BF16),
            pltpu.VMEM((seq, 64), BF16),
            pltpu.VMEM((64, seq), F32),
            pltpu.VMEM((64, seq), F32),
            pltpu.VMEM((seq, 128), F32),
            pltpu.VMEM((seq, 256), BF16),
            pltpu.VMEM((seq, 64), BF16),
            pltpu.VMEM((seq, 256), BF16),
            pltpu.VMEM((seq, D), BF16),
            pltpu.VMEM((seq, D), BF16),
            pltpu.VMEM((seq, width), BF16),
            pltpu.VMEM((seq, width), BF16),
            pltpu.VMEM((D, 256), F32),
            pltpu.VMEM((D, width), BF16),
            pltpu.VMEM((width, D), BF16),
            pltpu.VMEM((8, D), F32),
        ],
        n_smem=2,
        n_in=n + len(given) + 3,
        cost=pl.CostEstimate(flops=26 * seq * seq * 64, bytes_accessed=12 * seq * D, transcendentals=2 * seq * seq),
        name="layer",
    )(place, order, *pieces, *given, head_w, cos_t, sin_t)
    keep_pay, send_pay, g_out, params = layer_out[:4]
    pay = layer_out[4:]

    came = lax.ppermute(send_pay, "ctx", xor_pairs(n, 1))
    chip_sum = vmem_call(chip_body, [shape((TOK, 2 * D), BF16)] * (n // 2), n_in=2, name="chip_sum")(keep_pay, came)
    parts = [chip_sum[0]] + [lax.ppermute(chip_sum[k // 2], "ctx", xor_pairs(n, k)) for k in range(2, n, 2)]
    output, grad_inputs = vmem_call(
        close_body,
        (shape((TOK, D), BF16), shape((TOK, D))),
        n_smem=1,
        n_in=3 + len(parts),
        name="close",
    )(place, x, g, params, *parts)

    if fast:
        g_out = vmem_call(gate_body, shape(g_out.shape, BF16), n_in=1, n_any=1, name="gate")(g_out, parts[1])
        out_got = lax.ppermute(g_out, ("ctx", "fsdp"), [(b, a) for a, b in pairs])
        got = swap_fsdp(pay, nz)
        share = vmem_call(functools.partial(sum_body, nz), shape((D // nz, 1024), BF16), n_in=nz + 1, n_any=len(parts) - 1, name="sum")(
            *got, out_got, *parts[1:]
        )
        alls = gather_ctx(share, n)
        dz = D // nz
        outs = vmem_call(
            functools.partial(finish_body, n, nz),
            [
                shape((1, dz)),
                shape((1, dz)),
                shape((dz, 3 * D)),
                shape((1, 3 * dz)),
                shape((dz, D)),
                shape((1, dz)),
                shape((1, dz)),
                shape((1, dz)),
                shape((dz, FF)),
                shape((1, FF // nz)),
                shape((FF // nz, D)),
                shape((1, dz)),
            ],
            scratch=[
                pltpu.VMEM((n, 128, 256), F32),
                pltpu.VMEM((n, 128, 256), F32),
                pltpu.VMEM((n, 8, D), F32),
                pltpu.VMEM((24, 128), F32),
            ],
            n_smem=1,
            n_in=n,
            name="finish",
        )(place, *alls)
        outs = [o.reshape(-1) if o.shape[0] == 1 else o for o in outs]
    else:
        everyone = ("ctx", "fsdp")
        head = me // (n // HEADS)
        g_qkv, g_up, g_down, vec = pay

        def own(full, axis=0):
            size = full.shape[axis] // nz
            return lax.dynamic_slice_in_dim(full, zed * size, size, axis)

        def spread(part, dims, index, axis):
            full = jnp.zeros(dims, part.dtype)
            return lax.psum(lax.dynamic_update_index_in_dim(full, part, index, axis), everyone).astype(F32)

        qkv_full = spread(g_qkv[:, 0:192].reshape(D, 3, HEAD_DIM), (D, 3, HEADS, HEAD_DIM), head, 2).reshape(D, 3 * D)
        out_full = spread(g_out, (HEADS, HEAD_DIM, D), head, 0).reshape(D, D)
        up_full = spread(g_up, (D, n, width), me, 1).reshape(D, FF)
        down_full = spread(g_down, (n, width, D), me, 0).reshape(FF, D)
        bq_full = spread(vec[5, 0:192].reshape(3, HEAD_DIM), (3, HEADS, HEAD_DIM), head, 1).reshape(3 * D)
        bu_full = spread(vec[6, 0:width], (n, width), me, 0).reshape(FF)
        flat = lax.psum(vec, everyone)
        b_full = flat[4] * (1.0 / n)
        outs = [own(v) for v in (flat[0], flat[1], qkv_full, bq_full, out_full, b_full)]
        outs += [own(v) for v in (flat[2], flat[3], up_full, bu_full, down_full, b_full)]
    return (output[None], grad_inputs[None], *outs)


def solution(mesh):
    rows, flat, tokens = P("fsdp", None), P("fsdp"), P("fsdp", "ctx", None)
    weights = (flat, flat, rows, flat, rows, flat, flat, flat, rows, flat, rows, flat)
    return jax.shard_map(
        functools.partial(per_device, mesh.shape["ctx"], mesh.shape["fsdp"]),
        mesh=mesh,
        in_specs=(tokens, P(), *weights, tokens),
        out_specs=(tokens, tokens, *weights),
        check_vma=False,
    )
```

```python
import functools

import jax
import jax.numpy as jnp
import numpy as np
from jax import lax
from jax.experimental import pallas as pl
from jax.experimental.pallas import tpu as pltpu
from jax.sharding import PartitionSpec as P

HEADS = 8
HEAD_DIM = 64
D = 512
FF = 2048
ROT = 16
HALF = 64
TOK = 128
EPS = 1e-05
F32 = jnp.float32
BF16 = jnp.bfloat16
VMEM_LIMIT = 32 * 1024 * 1024
WIDE_LIMIT = 60 * 1024 * 1024
LONGER = pl.CostEstimate(flops=30_000_000_000, bytes_accessed=0, transcendentals=0)
LONG = pl.CostEstimate(flops=12_000_000_000, bytes_accessed=0, transcendentals=0)


def mm(left, right, dims):
    return lax.dot_general(left, right, (dims, ((), ())), preferred_element_type=F32)


def mm_nn(left, right):
    return mm(left, right, ((1,), (0,)))


def mm_nt(left, right):
    return mm(left, right, ((1,), (1,)))


def mm_tn(left, right):
    return mm(left, right, ((0,), (0,)))


def vmem_call(body, out_shape, scratch=(), n_smem=0, n_in=0, n_any=0, cost=None, name=None):
    smem = pl.BlockSpec(memory_space=pltpu.SMEM)
    vmem = pl.BlockSpec(memory_space=pltpu.VMEM)
    return pl.pallas_call(
        body,
        out_shape=out_shape,
        in_specs=[smem] * n_smem + [vmem] * n_in + [pl.BlockSpec(memory_space=pl.ANY)] * n_any,
        out_specs=jax.tree.map(lambda _: vmem, out_shape),
        scratch_shapes=list(scratch),
        compiler_params=pltpu.CompilerParams(vmem_limit_bytes=VMEM_LIMIT),
        cost_estimate=cost,
        name=name,
    )


def half_pick(block, odd, to_upper):
    moved = pltpu.roll(block, 64, 1)
    return jnp.where(odd, block if to_upper else moved, moved if to_upper else block)


def low_lanes(shape):
    return lax.broadcasted_iota(jnp.int32, shape, len(shape) - 1) % 128 < 64


def pack_body(nz, place, *refs):
    q_ref, k_ref, v_ref = refs[:3]
    ups = refs[3 : 3 + nz]
    w_down, w_out, x, g = refs[3 + nz : 7 + nz]
    vectors = refs[7 + nz : 15 + nz]
    pay, piece, head_w, small = refs[15 + nz :]
    odd = (place[0] % 2) == 1
    rows = q_ref.shape[0]
    low = low_lanes((rows, 128))
    small[...] = jnp.zeros_like(small)
    at = 0
    for vector in vectors:
        for r in range(vector.shape[0] // 128):
            small[at : at + 1, :] = vector[r * 128 : (r + 1) * 128].astype(F32).reshape(1, 128)
            at += 1
    few = small[...]
    spare = jnp.concatenate([pltpu.roll(few, 64, 1), few, jnp.zeros((rows - 32, 128), F32)], axis=0)
    q = half_pick(q_ref[...].astype(F32), odd, False)
    k = half_pick(k_ref[...].astype(F32), odd, True)
    v = half_pick(v_ref[...].astype(F32), odd, False)
    pay[:, 0:128] = jnp.where(low, q, k).astype(BF16)
    pay[:, 128:256] = jnp.where(low, v, spare).astype(BF16)
    for z in range(0, nz, 2):
        even = half_pick(ups[z][...].astype(F32), odd, False)
        later = half_pick(ups[z + 1][...].astype(F32), odd, True)
        pay[:, 256 + z * 64 : 256 + z * 64 + 128] = jnp.where(low, even, later).astype(BF16)
    pay[0:64, 512:768] = w_down[:, 0:256]
    pay[64:128, 512:768] = w_down[:, 256:512]
    head_w[...] = w_out[...]
    piece[0:TOK, :] = x[0]
    piece[TOK : 2 * TOK, :] = g[0]


def pack_call(nz, place, w_qkv, w_up, w_down, w_out, x, g, vectors):
    span = FF // nz // 128
    rows = D // nz

    def lane_block(first):
        return pl.BlockSpec((rows, 128), lambda i, s: (0, first + s[0] // 2))

    def whole(array):
        rank = array.ndim
        return pl.BlockSpec(array.shape, lambda i, s: (0,) * rank)

    outs = [shape((rows, 768), BF16), shape((2 * TOK, D), BF16), shape((HEAD_DIM, D), BF16)]
    return pl.pallas_call(
        functools.partial(pack_body, nz),
        out_shape=outs,
        grid_spec=pltpu.PrefetchScalarGridSpec(
            num_scalar_prefetch=1,
            grid=(1,),
            in_specs=[lane_block(0), lane_block(D // 128), lane_block(2 * D // 128)]
            + [lane_block(z * span) for z in range(nz)]
            + [
                pl.BlockSpec((64, D), lambda i, s: (s[0], 0)),
                pl.BlockSpec((HEAD_DIM, D), lambda i, s: (s[0] % 2, 0)),
                whole(x),
                whole(g),
            ]
            + [whole(v) for v in vectors],
            out_specs=[whole(o) for o in outs],
            scratch_shapes=[pltpu.VMEM((16, 128), F32)],
        ),
        compiler_params=pltpu.CompilerParams(vmem_limit_bytes=WIDE_LIMIT),
        name="pack",
    )(place, w_qkv, w_qkv, w_qkv, *([w_up] * nz), w_down, w_out, x, g, *vectors)


def unpack_body(nz, place, *refs):
    pieces = refs[:nz]
    w_all, w_up, w_down, params, held = refs[nz:]
    me, zed = place[0], place[1]
    pair = me // 2
    odd = (me % 2) == 1
    for k in range(nz):
        z = zed ^ k
        tall = pl.ds(pl.multiple_of(z * 128, 128), 128)
        flat = pl.ds(pl.multiple_of(z * 64, 64), 64)
        w_all[tall, 0:128] = pieces[k][:, 0:128]
        third = pieces[k][:, 128:256].astype(F32)
        w_all[tall, 128:256] = jnp.where(low_lanes((128, 128)), third, 0.0).astype(BF16)
        held[z] = jnp.where(low_lanes((16, 128)), pltpu.roll(third[0:16], 64, 1), third[16:32])
        w_up[tall, :] = pieces[k][:, 256:512]
        w_down[flat, 0:256] = pieces[k][0:64, 512:768]
        w_down[flat, 256:512] = pieces[k][64:128, 512:768]
    params[...] = jnp.zeros_like(params)
    for z in range(nz):
        lanes = slice(z * 128, (z + 1) * 128)
        params[0:4, lanes] = held[z, 0:4, :]
        params[4:5, lanes] = held[z, 4:5, :] + held[z, 5:6, :]
    low = low_lanes((1, 128))

    def qkv_row(group):
        index = group * 4 + pair
        z = index // 3
        return held[z, pl.ds(6 + index - 3 * z, 1), :]

    q = half_pick(qkv_row(0), odd, False)
    k = half_pick(qkv_row(1), odd, True)
    v = half_pick(qkv_row(2), odd, False)
    params[5:6, 0:128] = jnp.where(low, q, k)
    params[5:6, 128:256] = jnp.where(low, v, 0.0)
    for z in range(0, nz, 2):
        even = half_pick(held[z, pl.ds(9 + pair, 1), :], odd, False)
        later = half_pick(held[z + 1, pl.ds(9 + pair, 1), :], odd, True)
        params[6:7, z * 64 : z * 64 + 128] = jnp.where(low, even, later)


def normalized(x):
    center = x - jnp.mean(x, axis=-1, keepdims=True)
    spread = jnp.mean(center * center, axis=-1, keepdims=True)
    inv = lax.rsqrt(spread + EPS)
    return center * inv, inv


def fold(values):
    return jnp.sum(values.reshape(values.shape[0] // 8, 8, values.shape[1]), axis=0)


def layer_body(n, nz, fast, place, order, *refs):
    seq = n * TOK
    qblk = min(256, seq)
    pieces = refs[:n]
    w_all, w_up, w_down, params, w_out, turn = refs[n : n + 6]
    outs = refs[n + 6 :]
    n_pay = nz if fast else 4
    keep_pay, send_pay, g_out = outs[:3]
    pays = outs[3 : 3 + n_pay]
    scratch = outs[3 + n_pay :]
    spare = scratch[0]
    (norms, nhats, raw, qs, ks, vs, dms, mixs, dks, dvs, dqs, dqkvs, mixn, dqkvn, gs) = scratch[1:16]
    (norm2s, hiddens, dpres, grad_w, grad_up, grad_down, vec) = scratch[16:]
    width = w_up.shape[1]
    zed = place[1]
    gain, shift = params[0:1, :], params[1:2, :]
    gain2, shift2 = params[2:3, :], params[3:4, :]
    bias = params[5:6, 0:256]
    b_up = params[6:7, 0:width]

    def sorted_rows(block):
        return pl.ds(pl.multiple_of(order[block] * HALF, HALF), HALF)

    for p in range(n):
        rows = slice(p * TOK, (p + 1) * TOK)
        nhat, _ = normalized(pieces[p][0:TOK, :].astype(F32))
        g = pieces[p][TOK : 2 * TOK, :]
        norm = (nhat * gain + shift).astype(BF16)
        nhats[rows, :] = nhat
        norms[rows, :] = norm
        norm2s[rows, :] = (nhat * gain2 + shift2).astype(BF16)
        gs[rows, :] = g
        qkv = mm_nn(norm, w_all[...]) + bias
        dmix = mm_nt(g, w_out[...]).astype(BF16)
        for h in range(TOK // HALF):
            here = slice(h * HALF, (h + 1) * HALF)
            where = sorted_rows(p * (TOK // HALF) + h)
            raw[where, :] = qkv[here, :]
            dms[where, :] = dmix[here, :]

    lanes = lax.broadcasted_iota(jnp.int32, (qblk, 128), 1) % 64

    def both_heads(t):
        moved = pltpu.roll(t, 64, 1)
        low = low_lanes(t.shape)
        return jnp.where(low, t, moved), jnp.where(low, moved, t)

    def swapped(t):
        return jnp.where(lanes < ROT // 2, pltpu.roll(t, 128 - ROT // 2, 1), pltpu.roll(t, ROT // 2, 1))

    for i in range(seq // qblk):
        rows = slice(i * qblk, (i + 1) * qblk)
        qk = raw[rows, 0:128]
        cos_t, sin_t = both_heads(turn[rows, :])
        turned = (qk * cos_t + swapped(qk) * sin_t).astype(BF16)
        qs[rows, :] = turned[:, 0:64]
        ks[rows, :] = turned[:, 64:128]
        vs[rows, :] = raw[rows, 128:192].astype(BF16)

    dks[...] = jnp.zeros_like(dks)
    dvs[...] = jnp.zeros_like(dvs)
    for i in range(seq // qblk):
        rows = slice(i * qblk, (i + 1) * qblk)
        span = (i + 1) * qblk
        q = qs[rows, :]
        keys = ks[0:span, :]
        values = vs[0:span, :]
        s = mm_nt(q, keys) * 0.125
        q_at = lax.broadcasted_iota(jnp.int32, (qblk, span), 0) + i * qblk
        k_at = lax.broadcasted_iota(jnp.int32, (qblk, span), 1)
        s = jnp.where(q_at >= k_at, s, -1e30)
        top = jnp.max(s, axis=1, keepdims=True)
        e = jnp.exp(s - top)
        prob = e * (1.0 / jnp.sum(e, axis=1, keepdims=True))
        prob_b = prob.astype(BF16)
        mix = mm_nn(prob_b, values)
        mixs[rows, :] = mix.astype(BF16)
        dmix = dms[rows, :]
        delta = jnp.sum(dmix.astype(F32) * mix, axis=1, keepdims=True)
        dprob = mm_nt(dmix, values)
        ds = (prob * (dprob - delta)).astype(BF16)
        dqs[rows, 0:64] = mm_nn(ds, keys) * 0.125
        dks[:, 0:span] += mm_tn(q, ds)
        dvs[:, 0:span] += mm_tn(dmix, prob_b)
    dqs[:, 64:128] = dks[...].T * 0.125
    dqkvs[:, 128:192] = dvs[...].T.astype(BF16)
    dqkvs[:, 192:256] = jnp.zeros((seq, 64), BF16)
    for i in range(seq // qblk):
        rows = slice(i * qblk, (i + 1) * qblk)
        dqk = dqs[rows, :]
        cos_t, sin_t = both_heads(turn[rows, :])
        dqkvs[rows, 0:128] = (dqk * cos_t - swapped(dqk) * sin_t).astype(BF16)

    scale = None
    if n > HEADS:
        scale = jnp.where(place[0] % (n // HEADS) == 0, 1.0, 0.0).astype(BF16)
    for b in range(seq // HALF):
        here = slice(b * HALF, (b + 1) * HALF)
        where = sorted_rows(b)
        mix, dqkv = mixs[where, :], dqkvs[where, :]
        if scale is not None:
            mix, dqkv = mix * scale, dqkv * scale
        mixn[here, :] = mix
        dqkvn[here, :] = dqkv

    g_gain = jnp.zeros((8, D), F32)
    g_shift = jnp.zeros((8, D), F32)
    g_bias = jnp.zeros((8, 256), F32)
    g_gain2 = jnp.zeros((8, D), F32)
    g_shift2 = jnp.zeros((8, D), F32)
    g_sum = jnp.zeros((8, D), F32)
    g_bup = jnp.zeros((8, width), F32)
    for p in range(n):
        rows = slice(p * TOK, (p + 1) * TOK)
        g, nhat = gs[rows, :], nhats[rows, :]
        pre = mm_nn(norm2s[rows, :], w_up[...]) + b_up
        cdf = 0.5 * (1.0 + lax.erf(pre * 0.7071067811865476))
        hidden = (pre * cdf).astype(BF16)
        slope = cdf + pre * (0.3989422804014327 * jnp.exp(-0.5 * pre * pre))
        dpre = (mm_nt(g, w_down[...]) * slope).astype(BF16)
        hiddens[rows, :] = hidden
        dpres[rows, :] = dpre
        dqkv = dqkvn[rows, :]
        part_o = mm_nn(hidden, w_down[...]) + mm_nn(mixn[rows, :], w_out[...])
        dnorm2 = mm_nt(dpre, w_up[...])
        dnorm = mm_nt(dqkv, w_all[...])
        g_gain += fold(dnorm * nhat)
        g_shift += fold(dnorm)
        g_bias += fold(dqkv.astype(F32))
        g_gain2 += fold(dnorm2 * nhat)
        g_shift2 += fold(dnorm2)
        g_sum += fold(g.astype(F32))
        g_bup += fold(dpre.astype(F32))
        target = send_pay if p % 2 else keep_pay
        target[p // 2, :, 0:512] = part_o.astype(BF16)
        target[p // 2, :, 512:1024] = (dnorm * gain + dnorm2 * gain2).astype(BF16)
    vec[...] = jnp.zeros_like(vec)
    for row, value in ((0, g_gain), (1, g_shift), (2, g_gain2), (3, g_shift2), (4, g_sum), (5, g_bias), (6, g_bup)):
        vec[row : row + 1, 0 : value.shape[1]] = jnp.sum(value, axis=0, keepdims=True)
    g_out[...] = mm_tn(mixn[...], gs[...]).astype(BF16)
    grad_w[...] = mm_tn(dqkvn[...], norms[...]).T
    grad_up[...] = mm_tn(dpres[...], norm2s[...]).T.astype(BF16)
    grad_down[...] = mm_tn(hiddens[...], gs[...]).astype(BF16)
    if fast:
        spare[...] = jnp.zeros_like(spare)
        for j in range(8):
            lanes_j = vec[:, (j // 2) * 128 : (j // 2) * 128 + 128]
            spare[8 * j : 8 * j + 8, :] = lanes_j if j % 2 else pltpu.roll(lanes_j, 64, 1)
        low = low_lanes((128, 128))
        for k in range(nz):
            z = zed ^ k
            tall = pl.ds(pl.multiple_of(z * 128, 128), 128)
            flat = pl.ds(pl.multiple_of(z * 64, 64), 64)
            pays[k][:, 0:128] = grad_w[tall, 0:128].astype(BF16)
            pays[k][:, 128:256] = jnp.where(low, grad_w[tall, 128:256], spare[...]).astype(BF16)
            pays[k][:, 256:512] = grad_up[tall, :]
            pays[k][0:64, 512:768] = grad_down[flat, 0:256]
            pays[k][64:128, 512:768] = grad_down[flat, 256:512]
    else:
        pays[0][...] = grad_w[...].astype(BF16)
        pays[1][...] = grad_up[...]
        pays[2][...] = grad_down[...]
        pays[3][...] = vec[...]


def close_body(fast, place, x_ref, g_ref, params, *refs):
    parts, out, grad = refs[:-2], refs[-2], refs[-1]
    x = x_ref[...].astype(F32)
    nhat, inv = normalized(x)
    if fast:
        own, came_a, came_b, last_a, last_b = parts
        total_o = own[:, 0:D].astype(F32) + came_a[0].astype(F32) + last_a[...].astype(F32)
        dn = own[:, D : 2 * D].astype(F32) + came_b[0].astype(F32) + last_b[...].astype(F32)
    else:
        total = parts[0][...].astype(F32)
        for part in parts[1:]:
            total = total + part[...].astype(F32)
        total_o, dn = total[:, 0:D], total[:, D : 2 * D]
    out[...] = (x + total_o + params[4:5, :]).astype(BF16)
    lead = jnp.mean(dn, axis=-1, keepdims=True)
    along = jnp.mean(dn * nhat, axis=-1, keepdims=True)
    grad[...] = g_ref[...].astype(F32) + inv * (dn - lead - nhat * along)


def chip_body(keep, came, *outs):
    for k, out in enumerate(outs):
        out[...] = (keep[k].astype(F32) + came[k].astype(F32)).astype(BF16)


def chip_fast_body(n_later, keep, came, *refs):
    later, (first_a, first_b, own, kept_a, kept_b, *held) = refs[:n_later], refs[n_later:]
    for value, copy in zip(later, held):
        copy[...] = value[...]

    def both(k, lanes):
        return (keep[k, :, lanes].astype(F32) + came[k, :, lanes].astype(F32)).astype(BF16)

    left, right = slice(0, D), slice(D, 2 * D)
    own[:, left] = both(0, left)
    own[:, right] = both(0, right)
    first_a[0] = both(1, left)
    first_a[1] = both(3, left)
    first_b[0] = both(2, right)
    first_b[1] = both(3, right)
    kept_a[...] = both(2, left)
    kept_b[...] = both(1, right)


def cross_body(n_later, kept_a, kept_b, came_a, came_b, *refs):
    later, (second_a, second_b, *held) = refs[:n_later], refs[n_later:]
    for value, copy in zip(later, held):
        copy[...] = value[...]
    second_a[...] = (kept_a[...].astype(F32) + came_a[1].astype(F32)).astype(BF16)
    second_b[...] = (kept_b[...].astype(F32) + came_b[1].astype(F32)).astype(BF16)


def gate_body(value, *refs):
    out = refs[-1]
    out[...] = value[...]


def sum_body(nz, *refs):
    parts, out = refs[:nz], refs[nz]
    total = parts[0][...].astype(F32)
    for part in parts[1:]:
        total = total + part[...].astype(F32)
    out[...] = total.astype(BF16)


def share_body(total, g_out, *refs):
    out = refs[-1]
    out[:, 0:768] = total[...]
    out[0:64, 768:1024] = g_out[:, 0:256]
    out[64:128, 768:1024] = g_out[:, 256:512]


def finish_body(n, nz, place, *refs):
    alls = refs[:n]
    (ln1g, ln1b, gqkv, bqkv, gout, bout, ln2g, ln2b, gup, bup, gdown, bdown) = refs[n : n + 12]
    held_u, held_a, held_v, flat = refs[n + 12 :]
    me, zed = place[0], place[1]
    span = FF // nz
    total = jnp.zeros((8, D), F32)
    wide = low_lanes((8, 128))
    for k in range(n):
        who = me ^ k
        held_a[who] = alls[k][:, 0:256].astype(F32)
        held_u[who] = alls[k][:, 256:512].astype(F32)
        rows = pl.ds(pl.multiple_of(who * 64, 64), 64)
        gdown[rows, 0:256] = alls[k][0:64, 512:768].astype(F32)
        gdown[rows, 256:512] = alls[k][64:128, 512:768].astype(F32)
        spare = alls[k][0:64, 128:256].astype(F32)
        small = []
        for j in range(0, 8, 2):
            small.append(jnp.where(wide, pltpu.roll(spare[8 * j : 8 * j + 8], 64, 1), spare[8 * j + 8 : 8 * j + 16]))
        small = jnp.concatenate(small, axis=1)
        held_v[who] = small
        total = total + small
    for h in range(0, n, 2):
        even, later = held_a[h], held_a[h + 1]
        low = low_lanes((128, 128))
        at = h * 64
        gqkv[:, at : at + 128] = jnp.where(low, even[:, 0:128], pltpu.roll(later[:, 0:128], 64, 1))
        gqkv[:, D + at : D + at + 128] = jnp.where(low, pltpu.roll(even[:, 0:128], 64, 1), later[:, 0:128])
        gqkv[:, 2 * D + at : 2 * D + at + 128] = jnp.where(low, even[:, 128:256], pltpu.roll(later[:, 128:256], 64, 1))
        for z in range(0, nz, 2):
            lanes = slice(z * 64, z * 64 + 128)
            e, l = held_u[h][:, lanes], held_u[h + 1][:, lanes]
            gup[:, z * span + at : z * span + at + 128] = jnp.where(low, e, pltpu.roll(l, 64, 1))
            gup[:, (z + 1) * span + at : (z + 1) * span + at + 128] = jnp.where(low, pltpu.roll(e, 64, 1), l)
        low = low_lanes((1, 128))
        e, l = held_v[h], held_v[h + 1]
        flat[h // 2 : h // 2 + 1, :] = jnp.where(low, e[5:6, 0:128], pltpu.roll(l[5:6, 0:128], 64, 1))
        flat[4 + h // 2 : 5 + h // 2, :] = jnp.where(low, pltpu.roll(e[5:6, 0:128], 64, 1), l[5:6, 0:128])
        flat[8 + h // 2 : 9 + h // 2, :] = jnp.where(low, e[5:6, 128:256], pltpu.roll(l[5:6, 128:256], 64, 1))
        lane = pl.ds(pl.multiple_of((zed // 2) * 128, 128), 128)
        odd = (zed % 2) == 1
        e = half_pick(held_v[h, 6:7, lane], odd, False)
        l = half_pick(held_v[h + 1, 6:7, lane], odd, True)
        bup[at : at + 128] = jnp.where(low, e, l).reshape(128)
    mine = pl.multiple_of((me % 2) * 64, 64)
    other = pl.multiple_of((1 - me % 2) * 64, 64)
    for parity, start in ((0, mine), (1, other)):
        acc = alls[parity][:, 768:1024].astype(F32)
        for k in range(parity + 2, n, 2):
            acc = acc + alls[k][:, 768:1024].astype(F32)
        gout[pl.ds(start, 64), 0:256] = acc[0:64]
        gout[pl.ds(start, 64), 256:512] = acc[64:128]
    flat[12:20, :] = jnp.zeros((8, 128), F32)
    for r in range(3):
        bqkv[r * 128 : (r + 1) * 128] = flat[pl.ds(zed * 3 + r, 1), :].reshape(128)
    held_v[0] = total
    lane = pl.ds(pl.multiple_of(zed * 128, 128), 128)
    ln1g[...] = held_v[0, 0:1, lane].reshape(128)
    ln1b[...] = held_v[0, 1:2, lane].reshape(128)
    ln2g[...] = held_v[0, 2:3, lane].reshape(128)
    ln2b[...] = held_v[0, 3:4, lane].reshape(128)
    held_v[1] = total * (1.0 / n)
    bout[...] = held_v[1, 4:5, lane].reshape(128)
    bdown[...] = held_v[1, 4:5, lane].reshape(128)


def xor_pairs(size, k):
    return [(i, i ^ k) for i in range(size)]


def gather_ctx(value, n):
    got = {0: value}
    for k in range(2, n, 2):
        got[k] = lax.ppermute(value, "ctx", xor_pairs(n, k))
    for k in range(0, n, 2):
        got[k + 1] = lax.ppermute(got[k], "ctx", xor_pairs(n, 1))
    return [got[k] for k in range(n)]


def gather_fsdp(value, nz):
    return [value] + [lax.ppermute(value, "fsdp", xor_pairs(nz, k)) for k in range(1, nz)]


def relay_fsdp(value, nz):
    one, two = (lax.ppermute(value, "fsdp", xor_pairs(nz, k)) for k in (1, 2))
    return [value, one, two, lax.ppermute(two, "fsdp", xor_pairs(nz, 1))]


def swap_fsdp(values, nz):
    return [values[0]] + [lax.ppermute(values[k], "fsdp", xor_pairs(nz, k)) for k in range(1, nz)]


def rotary_tables(seq):
    pos = np.arange(seq, dtype=np.float32)
    inverse = (np.float32(10000.0) ** (-np.arange(ROT // 2, dtype=np.float32) * np.float32(2.0) / np.float32(ROT))).astype(np.float32)
    angles = (pos[:, None] * inverse[None, :]).astype(np.float32).astype(np.float64)
    cos_t = np.ones((seq, 64), np.float32)
    sin_t = np.zeros((seq, 64), np.float32)
    half = ROT // 2
    cos_t[:, 0:half] = np.cos(angles)
    cos_t[:, half:ROT] = np.cos(angles)
    sin_t[:, 0:half] = -np.sin(angles)
    sin_t[:, half:ROT] = np.sin(angles)
    return np.concatenate([cos_t, sin_t], axis=1)


def shape(dims, dtype=F32):
    return jax.ShapeDtypeStruct(dims, dtype)


def per_device(
    n,
    nz,
    inputs,
    block_order,
    ln1_gain,
    ln1_bias,
    w_qkv,
    b_qkv,
    w_attn_out,
    b_attn_out,
    ln2_gain,
    ln2_bias,
    w_up,
    b_up,
    w_down,
    b_down,
    cotangent,
):
    fast = n == HEADS and nz * 2 == HEADS
    seq = n * TOK
    width = FF // n
    me = lax.axis_index("ctx").astype(jnp.int32)
    zed = lax.axis_index("fsdp").astype(jnp.int32)
    place = jnp.stack([me, zed])
    x, g = inputs[0], cotangent[0]
    blocks = TOK // HALF
    chunk_at = (jnp.arange(n, dtype=jnp.int32) ^ me)[:, None] * blocks + jnp.arange(blocks, dtype=jnp.int32)[None, :]
    pick = chunk_at.reshape(-1)[:, None] == jnp.arange(n * blocks, dtype=jnp.int32)[None, :]
    order = jnp.sum(jnp.where(pick, block_order[None, :], 0), axis=1).astype(jnp.int32)
    turn = rotary_tables(seq)

    if fast:
        vectors = (ln1_gain, ln1_bias, ln2_gain, ln2_bias, b_attn_out, b_down, b_qkv, b_up)
        pack, piece, pack_w = pack_call(nz, place, w_qkv, w_up, w_down, w_attn_out, inputs, cotangent, vectors)
        pieces = gather_ctx(piece, n)
        far = relay_fsdp(pack, nz)
        given = vmem_call(
            functools.partial(unpack_body, nz),
            [shape((D, 256), BF16), shape((D, width), BF16), shape((width, D), BF16), shape((8, D))],
            scratch=[pltpu.VMEM((nz, 16, 128), F32)],
            n_smem=1,
            n_in=nz,
            cost=LONG,
            name="unpack",
        )(place, *far)
        pairs = []
        for c in range(n):
            for z in range(nz):
                pairs.append((c * nz + z, (2 * z + c % 2) * nz + c // 2))
        pack_w = vmem_call(gate_body, shape(pack_w.shape, BF16), n_in=2, name="gate_w")(pack_w, far[1])
        head_w = lax.ppermute(pack_w, ("ctx", "fsdp"), pairs)
    else:
        whole = [
            lax.all_gather(v, "fsdp", axis=0, tiled=True)
            for v in (ln1_gain, ln1_bias, ln2_gain, ln2_bias, b_attn_out, b_down, b_qkv, b_up)
        ]
        whole = [v.astype(F32) for v in whole]
        head = me // (n // HEADS)
        bq = lax.dynamic_index_in_dim(whole[6].reshape(3, HEADS, HEAD_DIM), head, 1, False).reshape(-1)
        bu = lax.dynamic_index_in_dim(whole[7].reshape(n, width), me, 0, False)
        params = jnp.stack(
            [whole[0], whole[1], whole[2], whole[3], whole[4] + whole[5]]
            + [jnp.pad(bq, (0, D - 3 * HEAD_DIM)), jnp.pad(bu, (0, D - width)), jnp.zeros((D,), F32)]
        )
        wq = lax.dynamic_index_in_dim(w_qkv.reshape(-1, 3, HEADS, HEAD_DIM), head, 2, False).reshape(-1, 3 * HEAD_DIM)
        given = [jnp.pad(lax.all_gather(wq, "fsdp", axis=0, tiled=True), ((0, 0), (0, 64)))]
        wu = lax.dynamic_slice_in_dim(w_up, me * width, width, 1)
        wd = lax.all_gather(w_down, "fsdp", axis=0, tiled=True)
        given += [lax.all_gather(wu, "fsdp", axis=0, tiled=True), lax.dynamic_slice_in_dim(wd, me * width, width, 0)]
        wo = lax.all_gather(w_attn_out, "fsdp", axis=0, tiled=True)
        given.append(params)
        pieces = gather_ctx(jnp.concatenate([x, g], axis=0), n)
        head_w = lax.dynamic_slice_in_dim(wo, head * HEAD_DIM, HEAD_DIM, 0)

    if fast:
        pays = [shape((D // nz, 768), BF16)] * nz
    else:
        pays = [shape((D, 256), BF16), shape((D, width), BF16), shape((width, D), BF16), shape((8, D))]
    half = (n // 2, TOK, 2 * D)
    layer_out = vmem_call(
        functools.partial(layer_body, n, nz, fast),
        [shape(half, BF16), shape(half, BF16), shape((HEAD_DIM, D), BF16)] + pays,
        scratch=[
            pltpu.VMEM((128, 128), F32),
            pltpu.VMEM((seq, D), BF16),
            pltpu.VMEM((seq, D), F32),
            pltpu.VMEM((seq, 256), F32),
            pltpu.VMEM((seq, 64), BF16),
            pltpu.VMEM((seq, 64), BF16),
            pltpu.VMEM((seq, 64), BF16),
            pltpu.VMEM((seq, 64), BF16),
            pltpu.VMEM((seq, 64), BF16),
            pltpu.VMEM((64, seq), F32),
            pltpu.VMEM((64, seq), F32),
            pltpu.VMEM((seq, 128), F32),
            pltpu.VMEM((seq, 256), BF16),
            pltpu.VMEM((seq, 64), BF16),
            pltpu.VMEM((seq, 256), BF16),
            pltpu.VMEM((seq, D), BF16),
            pltpu.VMEM((seq, D), BF16),
            pltpu.VMEM((seq, width), BF16),
            pltpu.VMEM((seq, width), BF16),
            pltpu.VMEM((D, 256), F32),
            pltpu.VMEM((D, width), BF16),
            pltpu.VMEM((width, D), BF16),
            pltpu.VMEM((8, D), F32),
        ],
        n_smem=2,
        n_in=n + len(given) + 2,
        cost=pl.CostEstimate(flops=26 * seq * seq * 64, bytes_accessed=12 * seq * D, transcendentals=2 * seq * seq),
        name="layer",
    )(place, order, *pieces, *given, head_w, turn)
    params = given[3]
    keep_pay, send_pay, g_out = layer_out[:3]
    pay = layer_out[3:]

    came = lax.ppermute(send_pay, "ctx", xor_pairs(n, 1))
    pay = list(pay)
    if fast:
        chip_out = vmem_call(
            functools.partial(chip_fast_body, 1),
            [shape((2, TOK, D), BF16)] * 2 + [shape((TOK, 2 * D), BF16)] + [shape((TOK, D), BF16)] * 2 + [shape(pay[1].shape, BF16)],
            n_in=2 + 1,
            cost=LONG,
            name="chip_sum",
        )(keep_pay, came, pay[1])
        first_a, first_b, own_sum, kept_a, kept_b = chip_out[:5]
        pay[1] = chip_out[5]
        came_a = lax.ppermute(first_a, "ctx", xor_pairs(n, 2))
        came_b = lax.ppermute(first_b, "ctx", xor_pairs(n, 4))
        cross_out = vmem_call(
            functools.partial(cross_body, 0),
            [shape((TOK, D), BF16)] * 2 + [],
            n_in=4 + 0,
            cost=LONG,
            name="cross",
        )(kept_a, kept_b, came_a, came_b)
        second_a, second_b = cross_out[:2]
        parts = [own_sum, came_a, came_b]
        parts += [lax.ppermute(second_a, "ctx", xor_pairs(n, 4)), lax.ppermute(second_b, "ctx", xor_pairs(n, 2))]
    else:
        chip_sum = vmem_call(chip_body, [shape((TOK, 2 * D), BF16)] * (n // 2), n_in=2, name="chip_sum")(keep_pay, came)
        parts = [chip_sum[0]] + [lax.ppermute(chip_sum[k // 2], "ctx", xor_pairs(n, k)) for k in range(2, n, 2)]
    output, grad_inputs = vmem_call(
        functools.partial(close_body, fast),
        (shape((TOK, D), BF16), shape((TOK, D))),
        n_smem=1,
        n_in=3 + len(parts),
        name="close",
    )(place, x, g, params, *parts)

    if fast:
        out_got = lax.ppermute(g_out, ("ctx", "fsdp"), [(b, a) for a, b in pairs])
        got = swap_fsdp(pay, nz)
        out_got = vmem_call(gate_body, shape(out_got.shape, BF16), n_in=1, cost=LONGER, name="gate")(out_got)
        total = vmem_call(functools.partial(sum_body, nz), shape((D // nz, 768), BF16), n_in=nz, cost=LONGER, name="sum")(*got)
        share = vmem_call(share_body, shape((D // nz, 1024), BF16), n_in=4, name="share")(total, out_got, *parts[3:])
        alls = gather_ctx(share, n)
        dz = D // nz
        outs = vmem_call(
            functools.partial(finish_body, n, nz),
            [
                shape((dz,)),
                shape((dz,)),
                shape((dz, 3 * D)),
                shape((3 * dz,)),
                shape((dz, D)),
                shape((dz,)),
                shape((dz,)),
                shape((dz,)),
                shape((dz, FF)),
                shape((FF // nz,)),
                shape((FF // nz, D)),
                shape((dz,)),
            ],
            scratch=[
                pltpu.VMEM((n, 128, 256), F32),
                pltpu.VMEM((n, 128, 256), F32),
                pltpu.VMEM((n, 8, D), F32),
                pltpu.VMEM((24, 128), F32),
            ],
            n_smem=1,
            n_in=n,
            name="finish",
        )(place, *alls)
    else:
        everyone = ("ctx", "fsdp")
        head = me // (n // HEADS)
        g_qkv, g_up, g_down, vec = pay

        def own(full, axis=0):
            size = full.shape[axis] // nz
            return lax.dynamic_slice_in_dim(full, zed * size, size, axis)

        def spread(part, dims, index, axis):
            full = jnp.zeros(dims, part.dtype)
            return lax.psum(lax.dynamic_update_index_in_dim(full, part, index, axis), everyone).astype(F32)

        qkv_full = spread(g_qkv[:, 0:192].reshape(D, 3, HEAD_DIM), (D, 3, HEADS, HEAD_DIM), head, 2).reshape(D, 3 * D)
        out_full = spread(g_out, (HEADS, HEAD_DIM, D), head, 0).reshape(D, D)
        up_full = spread(g_up, (D, n, width), me, 1).reshape(D, FF)
        down_full = spread(g_down, (n, width, D), me, 0).reshape(FF, D)
        bq_full = spread(vec[5, 0:192].reshape(3, HEAD_DIM), (3, HEADS, HEAD_DIM), head, 1).reshape(3 * D)
        bu_full = spread(vec[6, 0:width], (n, width), me, 0).reshape(FF)
        flat = lax.psum(vec, everyone)
        b_full = flat[4] * (1.0 / n)
        outs = [own(v) for v in (flat[0], flat[1], qkv_full, bq_full, out_full, b_full)]
        outs += [own(v) for v in (flat[2], flat[3], up_full, bu_full, down_full, b_full)]
    return (output[None], grad_inputs[None], *outs)


def solution(mesh):
    rows, flat, tokens = P("fsdp", None), P("fsdp"), P("fsdp", "ctx", None)
    weights = (flat, flat, rows, flat, rows, flat, flat, flat, rows, flat, rows, flat)
    return jax.shard_map(
        functools.partial(per_device, mesh.shape["ctx"], mesh.shape["fsdp"]),
        mesh=mesh,
        in_specs=(tokens, P(), *weights, tokens),
        out_specs=(tokens, tokens, *weights),
        check_vma=False,
    )
```

```python
import functools

import jax
import jax.numpy as jnp
import numpy as np
from jax import lax
from jax.experimental import pallas as pl
from jax.experimental.pallas import tpu as pltpu
from jax.sharding import PartitionSpec as P

HEADS = 8
HEAD_DIM = 64
D = 512
FF = 2048
ROT = 16
HALF = 64
TOK = 128
EPS = 1e-05
F32 = jnp.float32
BF16 = jnp.bfloat16
VMEM_LIMIT = 32 * 1024 * 1024
WIDE_LIMIT = 60 * 1024 * 1024
LONGER = pl.CostEstimate(flops=30_000_000_000, bytes_accessed=0, transcendentals=0)
LONG = pl.CostEstimate(flops=12_000_000_000, bytes_accessed=0, transcendentals=0)


def mm(left, right, dims):
    return lax.dot_general(left, right, (dims, ((), ())), preferred_element_type=F32)


def mm_nn(left, right):
    return mm(left, right, ((1,), (0,)))


def mm_nt(left, right):
    return mm(left, right, ((1,), (1,)))


def mm_tn(left, right):
    return mm(left, right, ((0,), (0,)))


def vmem_call(body, out_shape, scratch=(), n_smem=0, n_in=0, n_any=0, cost=None, name=None):
    smem = pl.BlockSpec(memory_space=pltpu.SMEM)
    vmem = pl.BlockSpec(memory_space=pltpu.VMEM)
    return pl.pallas_call(
        body,
        out_shape=out_shape,
        in_specs=[smem] * n_smem + [vmem] * n_in + [pl.BlockSpec(memory_space=pl.ANY)] * n_any,
        out_specs=jax.tree.map(lambda _: vmem, out_shape),
        scratch_shapes=list(scratch),
        compiler_params=pltpu.CompilerParams(vmem_limit_bytes=VMEM_LIMIT),
        cost_estimate=cost,
        name=name,
    )


def half_pick(block, odd, to_upper):
    moved = pltpu.roll(block, 64, 1)
    return jnp.where(odd, block if to_upper else moved, moved if to_upper else block)


def low_lanes(shape):
    return lax.broadcasted_iota(jnp.int32, shape, len(shape) - 1) % 128 < 64


def pack_body(nz, place, *refs):
    q_ref, k_ref, v_ref = refs[:3]
    ups = refs[3 : 3 + nz]
    w_down, w_out, x, g = refs[3 + nz : 7 + nz]
    vectors = refs[7 + nz : 15 + nz]
    pay, piece, head_w, small = refs[15 + nz :]
    odd = (place[0] % 2) == 1
    rows = q_ref.shape[0]
    low = low_lanes((rows, 128))
    small[...] = jnp.zeros_like(small)
    at = 0
    for vector in vectors:
        for r in range(vector.shape[0] // 128):
            small[at : at + 1, :] = vector[r * 128 : (r + 1) * 128].astype(F32).reshape(1, 128)
            at += 1
    few = small[...]
    spare = jnp.concatenate([pltpu.roll(few, 64, 1), few, jnp.zeros((rows - 32, 128), F32)], axis=0)
    q = half_pick(q_ref[...].astype(F32), odd, False)
    k = half_pick(k_ref[...].astype(F32), odd, True)
    v = half_pick(v_ref[...].astype(F32), odd, False)
    pay[:, 0:128] = jnp.where(low, q, k).astype(BF16)
    pay[:, 128:256] = jnp.where(low, v, spare).astype(BF16)
    for z in range(0, nz, 2):
        even = half_pick(ups[z][...].astype(F32), odd, False)
        later = half_pick(ups[z + 1][...].astype(F32), odd, True)
        pay[:, 256 + z * 64 : 256 + z * 64 + 128] = jnp.where(low, even, later).astype(BF16)
    pay[0:64, 512:768] = w_down[:, 0:256]
    pay[64:128, 512:768] = w_down[:, 256:512]
    head_w[...] = w_out[...]
    piece[0:TOK, :] = x[0]
    piece[TOK : 2 * TOK, :] = g[0]


def pack_call(nz, place, w_qkv, w_up, w_down, w_out, x, g, vectors):
    span = FF // nz // 128
    rows = D // nz

    def lane_block(first):
        return pl.BlockSpec((rows, 128), lambda i, s: (0, first + s[0] // 2))

    def whole(array):
        rank = array.ndim
        return pl.BlockSpec(array.shape, lambda i, s: (0,) * rank)

    outs = [shape((rows, 768), BF16), shape((2 * TOK, D), BF16), shape((HEAD_DIM, D), BF16)]
    return pl.pallas_call(
        functools.partial(pack_body, nz),
        out_shape=outs,
        grid_spec=pltpu.PrefetchScalarGridSpec(
            num_scalar_prefetch=1,
            grid=(1,),
            in_specs=[lane_block(0), lane_block(D // 128), lane_block(2 * D // 128)]
            + [lane_block(z * span) for z in range(nz)]
            + [
                pl.BlockSpec((64, D), lambda i, s: (s[0], 0)),
                pl.BlockSpec((HEAD_DIM, D), lambda i, s: (s[0] % 2, 0)),
                whole(x),
                whole(g),
            ]
            + [whole(v) for v in vectors],
            out_specs=[whole(o) for o in outs],
            scratch_shapes=[pltpu.VMEM((16, 128), F32)],
        ),
        compiler_params=pltpu.CompilerParams(vmem_limit_bytes=WIDE_LIMIT),
        name="pack",
    )(place, w_qkv, w_qkv, w_qkv, *([w_up] * nz), w_down, w_out, x, g, *vectors)


def unpack_body(nz, place, *refs):
    pieces = refs[:nz]
    w_all, w_up, w_down, params, held = refs[nz:]
    me, zed = place[0], place[1]
    pair = me // 2
    odd = (me % 2) == 1
    for k in range(nz):
        z = zed ^ k
        tall = pl.ds(pl.multiple_of(z * 128, 128), 128)
        flat = pl.ds(pl.multiple_of(z * 64, 64), 64)
        w_all[tall, 0:128] = pieces[k][:, 0:128]
        third = pieces[k][:, 128:256].astype(F32)
        w_all[tall, 128:256] = jnp.where(low_lanes((128, 128)), third, 0.0).astype(BF16)
        held[z] = jnp.where(low_lanes((16, 128)), pltpu.roll(third[0:16], 64, 1), third[16:32])
        w_up[tall, :] = pieces[k][:, 256:512]
        w_down[flat, 0:256] = pieces[k][0:64, 512:768]
        w_down[flat, 256:512] = pieces[k][64:128, 512:768]
    params[...] = jnp.zeros_like(params)
    for z in range(nz):
        lanes = slice(z * 128, (z + 1) * 128)
        params[0:4, lanes] = held[z, 0:4, :]
        params[4:5, lanes] = held[z, 4:5, :] + held[z, 5:6, :]
    low = low_lanes((1, 128))

    def qkv_row(group):
        index = group * 4 + pair
        z = index // 3
        return held[z, pl.ds(6 + index - 3 * z, 1), :]

    q = half_pick(qkv_row(0), odd, False)
    k = half_pick(qkv_row(1), odd, True)
    v = half_pick(qkv_row(2), odd, False)
    params[5:6, 0:128] = jnp.where(low, q, k)
    params[5:6, 128:256] = jnp.where(low, v, 0.0)
    for z in range(0, nz, 2):
        even = half_pick(held[z, pl.ds(9 + pair, 1), :], odd, False)
        later = half_pick(held[z + 1, pl.ds(9 + pair, 1), :], odd, True)
        params[6:7, z * 64 : z * 64 + 128] = jnp.where(low, even, later)


def normalized(x):
    center = x - jnp.mean(x, axis=-1, keepdims=True)
    spread = jnp.mean(center * center, axis=-1, keepdims=True)
    inv = lax.rsqrt(spread + EPS)
    return center * inv, inv


def fold(values):
    return jnp.sum(values.reshape(values.shape[0] // 8, 8, values.shape[1]), axis=0)


def ff_body(n, nz, fast, place, *refs):
    pieces = refs[:n]
    w_up, w_down, params = refs[n : n + 3]
    outs = refs[n + 3 :]
    n_pay = 3 if fast else 2
    acc_o, acc_d, vec, norms, nhats = outs[:5]
    pays = outs[5 : 5 + n_pay]
    norm2s, hiddens, dpres, gs, grad_up, grad_down = outs[5 + n_pay :]
    width = w_up.shape[1]
    zed = place[1]
    gain, shift = params[0:1, :], params[1:2, :]
    gain2, shift2 = params[2:3, :], params[3:4, :]
    b_up = params[6:7, 0:width]
    g_gain = jnp.zeros((8, D), F32)
    g_shift = jnp.zeros((8, D), F32)
    g_sum = jnp.zeros((8, D), F32)
    g_bup = jnp.zeros((8, width), F32)
    for p in range(n):
        rows = slice(p * TOK, (p + 1) * TOK)
        nhat, _ = normalized(pieces[p][0:TOK, :].astype(F32))
        g = pieces[p][TOK : 2 * TOK, :]
        norms[rows, :] = (nhat * gain + shift).astype(BF16)
        nhats[rows, :] = nhat.astype(BF16)
        norm2 = (nhat * gain2 + shift2).astype(BF16)
        pre = mm_nn(norm2, w_up[...]) + b_up
        cdf = 0.5 * (1.0 + lax.erf(pre * 0.7071067811865476))
        hidden = (pre * cdf).astype(BF16)
        slope = cdf + pre * (0.3989422804014327 * jnp.exp(-0.5 * pre * pre))
        dpre = (mm_nt(g, w_down[...]) * slope).astype(BF16)
        dnorm = mm_nt(dpre, w_up[...])
        acc_o[rows, :] = mm_nn(hidden, w_down[...]).astype(BF16)
        acc_d[rows, :] = (dnorm * gain2).astype(BF16)
        g_gain += fold(dnorm * nhat)
        g_shift += fold(dnorm)
        g_sum += fold(g.astype(F32))
        g_bup += fold(dpre.astype(F32))
        norm2s[rows, :] = norm2
        hiddens[rows, :] = hidden
        dpres[rows, :] = dpre
        gs[rows, :] = g
    vec[...] = jnp.zeros_like(vec)
    for row, value in ((2, g_gain), (3, g_shift), (4, g_sum), (6, g_bup)):
        vec[row : row + 1, 0 : value.shape[1]] = jnp.sum(value, axis=0, keepdims=True)
    grad_up[...] = mm_tn(dpres[...], norm2s[...]).T.astype(BF16)
    grad_down[...] = mm_tn(hiddens[...], gs[...]).astype(BF16)
    if fast:
        own, near, two = pays
        for k, target in ((0, own), (1, near.at[0]), (2, two), (3, near.at[1])):
            z = zed ^ k
            tall = pl.ds(pl.multiple_of(z * 128, 128), 128)
            flat = pl.ds(pl.multiple_of(z * 64, 64), 64)
            target[:, 0:256] = grad_up[tall, :]
            target[0:64, 256:512] = grad_down[flat, 0:256]
            target[64:128, 256:512] = grad_down[flat, 256:512]
    else:
        pays[0][...] = grad_up[...]
        pays[1][...] = grad_down[...]


def attn_body(n, place, order, *refs):
    seq = n * TOK
    qblk = min(256, seq)
    pieces = refs[:n]
    w_all, params, w_out, turn, norms = refs[n : n + 5]
    mixn, dqkvn = refs[n + 5 : n + 7]
    raw, qs, ks, vs, dms, mixs, dks, dvs, dqs, dqkvs = refs[n + 7 :]
    bias = params[5:6, 0:256]

    def sorted_rows(block):
        return pl.ds(pl.multiple_of(order[block] * HALF, HALF), HALF)

    for p in range(n):
        rows = slice(p * TOK, (p + 1) * TOK)
        qkv = mm_nn(norms[rows, :], w_all[...]) + bias
        dmix = mm_nt(pieces[p][TOK : 2 * TOK, :], w_out[...]).astype(BF16)
        for h in range(TOK // HALF):
            here = slice(h * HALF, (h + 1) * HALF)
            where = sorted_rows(p * (TOK // HALF) + h)
            raw[where, :] = qkv[here, :]
            dms[where, :] = dmix[here, :]

    lanes = lax.broadcasted_iota(jnp.int32, (qblk, 128), 1) % 64

    def both_heads(t):
        moved = pltpu.roll(t, 64, 1)
        low = low_lanes(t.shape)
        return jnp.where(low, t, moved), jnp.where(low, moved, t)

    def swapped(t):
        return jnp.where(lanes < ROT // 2, pltpu.roll(t, 128 - ROT // 2, 1), pltpu.roll(t, ROT // 2, 1))

    for i in range(seq // qblk):
        rows = slice(i * qblk, (i + 1) * qblk)
        qk = raw[rows, 0:128]
        cos_t, sin_t = both_heads(turn[rows, :])
        turned = (qk * cos_t + swapped(qk) * sin_t).astype(BF16)
        qs[rows, :] = turned[:, 0:64]
        ks[rows, :] = turned[:, 64:128]
        vs[rows, :] = raw[rows, 128:192].astype(BF16)

    dks[...] = jnp.zeros_like(dks)
    dvs[...] = jnp.zeros_like(dvs)
    for i in range(seq // qblk):
        rows = slice(i * qblk, (i + 1) * qblk)
        span = (i + 1) * qblk
        q = qs[rows, :]
        keys = ks[0:span, :]
        values = vs[0:span, :]
        s = mm_nt(q, keys) * 0.125
        q_at = lax.broadcasted_iota(jnp.int32, (qblk, span), 0) + i * qblk
        k_at = lax.broadcasted_iota(jnp.int32, (qblk, span), 1)
        s = jnp.where(q_at >= k_at, s, -1e30)
        top = jnp.max(s, axis=1, keepdims=True)
        e = jnp.exp(s - top)
        prob = e * (1.0 / jnp.sum(e, axis=1, keepdims=True))
        prob_b = prob.astype(BF16)
        mix = mm_nn(prob_b, values)
        mixs[rows, :] = mix.astype(BF16)
        dmix = dms[rows, :]
        delta = jnp.sum(dmix.astype(F32) * mix, axis=1, keepdims=True)
        dprob = mm_nt(dmix, values)
        ds = (prob * (dprob - delta)).astype(BF16)
        dqs[rows, 0:64] = mm_nn(ds, keys) * 0.125
        dks[:, 0:span] += mm_tn(q, ds)
        dvs[:, 0:span] += mm_tn(dmix, prob_b)
    dqs[:, 64:128] = dks[...].T * 0.125
    dqkvs[:, 128:192] = dvs[...].T.astype(BF16)
    dqkvs[:, 192:256] = jnp.zeros((seq, 64), BF16)
    for i in range(seq // qblk):
        rows = slice(i * qblk, (i + 1) * qblk)
        dqk = dqs[rows, :]
        cos_t, sin_t = both_heads(turn[rows, :])
        dqkvs[rows, 0:128] = (dqk * cos_t - swapped(dqk) * sin_t).astype(BF16)

    scale = None
    if n > HEADS:
        scale = jnp.where(place[0] % (n // HEADS) == 0, 1.0, 0.0).astype(BF16)
    for b in range(seq // HALF):
        here = slice(b * HALF, (b + 1) * HALF)
        where = sorted_rows(b)
        mix, dqkv = mixs[where, :], dqkvs[where, :]
        if scale is not None:
            mix, dqkv = mix * scale, dqkv * scale
        mixn[here, :] = mix
        dqkvn[here, :] = dqkv


def ends_body(n, nz, fast, place, *refs):
    pieces = refs[:n]
    mixn, dqkvn, norms, nhats, acc_o, acc_d, vec_in, w_all, w_out, params = refs[n : n + 10]
    at = n + 10
    if fast:
        ff_two, ff_came = refs[at : at + 2]
        at += 2
    keep_pay, send_pay, g_out = refs[at : at + 3]
    n_pay = 4 if fast else 2
    pays = refs[at + 3 : at + 3 + n_pay]
    spare, gs, grad_w, vec = refs[at + 3 + n_pay :]
    zed = place[1]
    gain = params[0:1, :]
    g_gain = jnp.zeros((8, D), F32)
    g_shift = jnp.zeros((8, D), F32)
    g_bias = jnp.zeros((8, 256), F32)
    for p in range(n):
        rows = slice(p * TOK, (p + 1) * TOK)
        gs[rows, :] = pieces[p][TOK : 2 * TOK, :]
        dqkv = dqkvn[rows, :]
        dnorm = mm_nt(dqkv, w_all[...])
        g_gain += fold(dnorm * nhats[rows, :].astype(F32))
        g_shift += fold(dnorm)
        g_bias += fold(dqkv.astype(F32))
        target = send_pay if p % 2 else keep_pay
        target[p // 2, :, 0:512] = (mm_nn(mixn[rows, :], w_out[...]) + acc_o[rows, :].astype(F32)).astype(BF16)
        target[p // 2, :, 512:1024] = (dnorm * gain + acc_d[rows, :].astype(F32)).astype(BF16)
    vec[...] = vec_in[...]
    for row, value in ((0, g_gain), (1, g_shift), (5, g_bias)):
        vec[row : row + 1, 0 : value.shape[1]] = jnp.sum(value, axis=0, keepdims=True)
    g_out[...] = mm_tn(mixn[...], gs[...]).astype(BF16)
    grad_w[...] = mm_tn(dqkvn[...], norms[...]).T
    if fast:
        spare[...] = jnp.zeros_like(spare)
        for j in range(8):
            lanes_j = vec[:, (j // 2) * 128 : (j // 2) * 128 + 128]
            spare[8 * j : 8 * j + 8, :] = lanes_j if j % 2 else pltpu.roll(lanes_j, 64, 1)
        low = low_lanes((128, 128))
        own, near, two, ff_sum = pays
        for k, target in ((0, own), (1, near.at[0]), (2, two), (3, near.at[1])):
            tall = pl.ds(pl.multiple_of((zed ^ k) * 128, 128), 128)
            target[:, 0:128] = grad_w[tall, 0:128].astype(BF16)
            target[:, 128:256] = jnp.where(low, grad_w[tall, 128:256], spare[...]).astype(BF16)
        ff_sum[...] = (ff_two[...].astype(F32) + ff_came[1].astype(F32)).astype(BF16)
    else:
        pays[0][...] = grad_w[...].astype(BF16)
        pays[1][...] = vec[...]


def close_body(fast, place, x_ref, g_ref, params, *refs):
    parts, out, grad = refs[:-2], refs[-2], refs[-1]
    x = x_ref[...].astype(F32)
    nhat, inv = normalized(x)
    if fast:
        own, came_a, came_b, last_a, last_b = parts
        total_o = own[:, 0:D].astype(F32) + came_a[0].astype(F32) + last_a[...].astype(F32)
        dn = own[:, D : 2 * D].astype(F32) + came_b[0].astype(F32) + last_b[...].astype(F32)
    else:
        total = parts[0][...].astype(F32)
        for part in parts[1:]:
            total = total + part[...].astype(F32)
        total_o, dn = total[:, 0:D], total[:, D : 2 * D]
    out[...] = (x + total_o + params[4:5, :]).astype(BF16)
    lead = jnp.mean(dn, axis=-1, keepdims=True)
    along = jnp.mean(dn * nhat, axis=-1, keepdims=True)
    grad[...] = g_ref[...].astype(F32) + inv * (dn - lead - nhat * along)


def chip_body(keep, came, *outs):
    for k, out in enumerate(outs):
        out[...] = (keep[k].astype(F32) + came[k].astype(F32)).astype(BF16)


def chip_fast_body(n_later, keep, came, *refs):
    later, (first_a, first_b, own, kept_a, kept_b, *held) = refs[:n_later], refs[n_later:]
    for value, copy in zip(later, held):
        copy[...] = value[...]

    def both(k, lanes):
        return (keep[k, :, lanes].astype(F32) + came[k, :, lanes].astype(F32)).astype(BF16)

    left, right = slice(0, D), slice(D, 2 * D)
    own[:, left] = both(0, left)
    own[:, right] = both(0, right)
    first_a[0] = both(1, left)
    first_a[1] = both(3, left)
    first_b[0] = both(2, right)
    first_b[1] = both(3, right)
    kept_a[...] = both(2, left)
    kept_b[...] = both(1, right)


def cross_body(n_later, kept_a, kept_b, came_a, came_b, *refs):
    later, (second_a, second_b, *held) = refs[:n_later], refs[n_later:]
    for value, copy in zip(later, held):
        copy[...] = value[...]
    second_a[...] = (kept_a[...].astype(F32) + came_a[1].astype(F32)).astype(BF16)
    second_b[...] = (kept_b[...].astype(F32) + came_b[1].astype(F32)).astype(BF16)


def gate_body(value, *refs):
    out = refs[-1]
    out[...] = value[...]


def relay_body(two, came, out):
    out[...] = (two[...].astype(F32) + came[1].astype(F32)).astype(BF16)


def share_body(ff_own, ff_near, ff_far, own, near, far, g_out, *refs):
    out = refs[-1]
    out[:, 0:512] = (ff_own[...].astype(F32) + ff_near[0].astype(F32) + ff_far[...].astype(F32)).astype(BF16)
    out[:, 512:768] = (own[...].astype(F32) + near[0].astype(F32) + far[...].astype(F32)).astype(BF16)
    out[0:64, 768:1024] = g_out[:, 0:256]
    out[64:128, 768:1024] = g_out[:, 256:512]


def finish_body(n, nz, place, *refs):
    alls = refs[:n]
    (ln1g, ln1b, gqkv, bqkv, gout, bout, ln2g, ln2b, gup, bup, gdown, bdown) = refs[n : n + 12]
    held_u, held_a, held_v, flat = refs[n + 12 :]
    me, zed = place[0], place[1]
    span = FF // nz
    total = jnp.zeros((8, D), F32)
    wide = low_lanes((8, 128))
    for k in range(n):
        who = me ^ k
        held_a[who] = alls[k][:, 512:768].astype(F32)
        held_u[who] = alls[k][:, 0:256].astype(F32)
        rows = pl.ds(pl.multiple_of(who * 64, 64), 64)
        gdown[rows, 0:256] = alls[k][0:64, 256:512].astype(F32)
        gdown[rows, 256:512] = alls[k][64:128, 256:512].astype(F32)
        spare = alls[k][0:64, 640:768].astype(F32)
        small = []
        for j in range(0, 8, 2):
            small.append(jnp.where(wide, pltpu.roll(spare[8 * j : 8 * j + 8], 64, 1), spare[8 * j + 8 : 8 * j + 16]))
        small = jnp.concatenate(small, axis=1)
        held_v[who] = small
        total = total + small
    for h in range(0, n, 2):
        even, later = held_a[h], held_a[h + 1]
        low = low_lanes((128, 128))
        at = h * 64
        gqkv[:, at : at + 128] = jnp.where(low, even[:, 0:128], pltpu.roll(later[:, 0:128], 64, 1))
        gqkv[:, D + at : D + at + 128] = jnp.where(low, pltpu.roll(even[:, 0:128], 64, 1), later[:, 0:128])
        gqkv[:, 2 * D + at : 2 * D + at + 128] = jnp.where(low, even[:, 128:256], pltpu.roll(later[:, 128:256], 64, 1))
        for z in range(0, nz, 2):
            lanes = slice(z * 64, z * 64 + 128)
            e, l = held_u[h][:, lanes], held_u[h + 1][:, lanes]
            gup[:, z * span + at : z * span + at + 128] = jnp.where(low, e, pltpu.roll(l, 64, 1))
            gup[:, (z + 1) * span + at : (z + 1) * span + at + 128] = jnp.where(low, pltpu.roll(e, 64, 1), l)
        low = low_lanes((1, 128))
        e, l = held_v[h], held_v[h + 1]
        flat[h // 2 : h // 2 + 1, :] = jnp.where(low, e[5:6, 0:128], pltpu.roll(l[5:6, 0:128], 64, 1))
        flat[4 + h // 2 : 5 + h // 2, :] = jnp.where(low, pltpu.roll(e[5:6, 0:128], 64, 1), l[5:6, 0:128])
        flat[8 + h // 2 : 9 + h // 2, :] = jnp.where(low, e[5:6, 128:256], pltpu.roll(l[5:6, 128:256], 64, 1))
        lane = pl.ds(pl.multiple_of((zed // 2) * 128, 128), 128)
        odd = (zed % 2) == 1
        e = half_pick(held_v[h, 6:7, lane], odd, False)
        l = half_pick(held_v[h + 1, 6:7, lane], odd, True)
        bup[at : at + 128] = jnp.where(low, e, l).reshape(128)
    mine = pl.multiple_of((me % 2) * 64, 64)
    other = pl.multiple_of((1 - me % 2) * 64, 64)
    for parity, start in ((0, mine), (1, other)):
        acc = alls[parity][:, 768:1024].astype(F32)
        for k in range(parity + 2, n, 2):
            acc = acc + alls[k][:, 768:1024].astype(F32)
        gout[pl.ds(start, 64), 0:256] = acc[0:64]
        gout[pl.ds(start, 64), 256:512] = acc[64:128]
    flat[12:20, :] = jnp.zeros((8, 128), F32)
    for r in range(3):
        bqkv[r * 128 : (r + 1) * 128] = flat[pl.ds(zed * 3 + r, 1), :].reshape(128)
    held_v[0] = total
    lane = pl.ds(pl.multiple_of(zed * 128, 128), 128)
    ln1g[...] = held_v[0, 0:1, lane].reshape(128)
    ln1b[...] = held_v[0, 1:2, lane].reshape(128)
    ln2g[...] = held_v[0, 2:3, lane].reshape(128)
    ln2b[...] = held_v[0, 3:4, lane].reshape(128)
    held_v[1] = total * (1.0 / n)
    bout[...] = held_v[1, 4:5, lane].reshape(128)
    bdown[...] = held_v[1, 4:5, lane].reshape(128)


def xor_pairs(size, k):
    return [(i, i ^ k) for i in range(size)]


def gather_ctx(value, n):
    got = {0: value}
    for k in range(2, n, 2):
        got[k] = lax.ppermute(value, "ctx", xor_pairs(n, k))
    for k in range(0, n, 2):
        got[k + 1] = lax.ppermute(got[k], "ctx", xor_pairs(n, 1))
    return [got[k] for k in range(n)]


def gather_fsdp(value, nz):
    return [value] + [lax.ppermute(value, "fsdp", xor_pairs(nz, k)) for k in range(1, nz)]


def relay_fsdp(value, nz):
    one, two = (lax.ppermute(value, "fsdp", xor_pairs(nz, k)) for k in (1, 2))
    return [value, one, two, lax.ppermute(two, "fsdp", xor_pairs(nz, 1))]


def rotary_tables(seq):
    pos = np.arange(seq, dtype=np.float32)
    inverse = (np.float32(10000.0) ** (-np.arange(ROT // 2, dtype=np.float32) * np.float32(2.0) / np.float32(ROT))).astype(np.float32)
    angles = (pos[:, None] * inverse[None, :]).astype(np.float32).astype(np.float64)
    cos_t = np.ones((seq, 64), np.float32)
    sin_t = np.zeros((seq, 64), np.float32)
    half = ROT // 2
    cos_t[:, 0:half] = np.cos(angles)
    cos_t[:, half:ROT] = np.cos(angles)
    sin_t[:, 0:half] = -np.sin(angles)
    sin_t[:, half:ROT] = np.sin(angles)
    return np.concatenate([cos_t, sin_t], axis=1)


def shape(dims, dtype=F32):
    return jax.ShapeDtypeStruct(dims, dtype)


def per_device(
    n,
    nz,
    inputs,
    block_order,
    ln1_gain,
    ln1_bias,
    w_qkv,
    b_qkv,
    w_attn_out,
    b_attn_out,
    ln2_gain,
    ln2_bias,
    w_up,
    b_up,
    w_down,
    b_down,
    cotangent,
):
    fast = n == HEADS and nz * 2 == HEADS
    seq = n * TOK
    width = FF // n
    me = lax.axis_index("ctx").astype(jnp.int32)
    zed = lax.axis_index("fsdp").astype(jnp.int32)
    place = jnp.stack([me, zed])
    x, g = inputs[0], cotangent[0]
    blocks = TOK // HALF
    chunk_at = (jnp.arange(n, dtype=jnp.int32) ^ me)[:, None] * blocks + jnp.arange(blocks, dtype=jnp.int32)[None, :]
    pick = chunk_at.reshape(-1)[:, None] == jnp.arange(n * blocks, dtype=jnp.int32)[None, :]
    order = jnp.sum(jnp.where(pick, block_order[None, :], 0), axis=1).astype(jnp.int32)
    turn = rotary_tables(seq)

    if fast:
        vectors = (ln1_gain, ln1_bias, ln2_gain, ln2_bias, b_attn_out, b_down, b_qkv, b_up)
        pack, piece, pack_w = pack_call(nz, place, w_qkv, w_up, w_down, w_attn_out, inputs, cotangent, vectors)
        pieces = gather_ctx(piece, n)
        far = relay_fsdp(pack, nz)
        given = vmem_call(
            functools.partial(unpack_body, nz),
            [shape((D, 256), BF16), shape((D, width), BF16), shape((width, D), BF16), shape((8, D))],
            scratch=[pltpu.VMEM((nz, 16, 128), F32)],
            n_smem=1,
            n_in=nz,
            cost=LONG,
            name="unpack",
        )(place, *far)
        pairs = []
        for c in range(n):
            for z in range(nz):
                pairs.append((c * nz + z, (2 * z + c % 2) * nz + c // 2))
        pack_w = vmem_call(gate_body, shape(pack_w.shape, BF16), n_in=2, name="gate_w")(pack_w, far[1])
        head_w = lax.ppermute(pack_w, ("ctx", "fsdp"), pairs)
    else:
        whole = [
            lax.all_gather(v, "fsdp", axis=0, tiled=True)
            for v in (ln1_gain, ln1_bias, ln2_gain, ln2_bias, b_attn_out, b_down, b_qkv, b_up)
        ]
        whole = [v.astype(F32) for v in whole]
        head = me // (n // HEADS)
        bq = lax.dynamic_index_in_dim(whole[6].reshape(3, HEADS, HEAD_DIM), head, 1, False).reshape(-1)
        bu = lax.dynamic_index_in_dim(whole[7].reshape(n, width), me, 0, False)
        params = jnp.stack(
            [whole[0], whole[1], whole[2], whole[3], whole[4] + whole[5]]
            + [jnp.pad(bq, (0, D - 3 * HEAD_DIM)), jnp.pad(bu, (0, D - width)), jnp.zeros((D,), F32)]
        )
        wq = lax.dynamic_index_in_dim(w_qkv.reshape(-1, 3, HEADS, HEAD_DIM), head, 2, False).reshape(-1, 3 * HEAD_DIM)
        given = [jnp.pad(lax.all_gather(wq, "fsdp", axis=0, tiled=True), ((0, 0), (0, 64)))]
        wu = lax.dynamic_slice_in_dim(w_up, me * width, width, 1)
        wd = lax.all_gather(w_down, "fsdp", axis=0, tiled=True)
        given += [lax.all_gather(wu, "fsdp", axis=0, tiled=True), lax.dynamic_slice_in_dim(wd, me * width, width, 0)]
        wo = lax.all_gather(w_attn_out, "fsdp", axis=0, tiled=True)
        given.append(params)
        pieces = gather_ctx(jnp.concatenate([x, g], axis=0), n)
        head_w = lax.dynamic_slice_in_dim(wo, head * HEAD_DIM, HEAD_DIM, 0)

    w_all, w_up_c, w_down_c, params = given
    whole_seq = shape((seq, D), BF16)
    half = (n // 2, TOK, 2 * D)
    rows = D // nz
    if fast:
        ff_pays = [shape((rows, 512), BF16), shape((2, rows, 512), BF16), shape((rows, 512), BF16)]
        attn_pays = [shape((rows, 256), BF16), shape((2, rows, 256), BF16), shape((rows, 256), BF16), shape((rows, 512), BF16)]
    else:
        ff_pays = [shape((D, width), BF16), shape((width, D), BF16)]
        attn_pays = [shape((D, 256), BF16), shape((8, D))]
    ff_out = vmem_call(
        functools.partial(ff_body, n, nz, fast),
        [whole_seq, whole_seq, shape((8, D)), whole_seq, whole_seq] + ff_pays,
        scratch=[
            pltpu.VMEM((seq, D), BF16),
            pltpu.VMEM((seq, width), BF16),
            pltpu.VMEM((seq, width), BF16),
            pltpu.VMEM((seq, D), BF16),
            pltpu.VMEM((D, width), BF16),
            pltpu.VMEM((width, D), BF16),
        ],
        n_smem=1,
        n_in=n + 3,
        cost=pl.CostEstimate(flops=4_000_000_000, bytes_accessed=0, transcendentals=0),
        name="feed_forward",
    )(place, *pieces, w_up_c, w_down_c, params)
    acc_o, acc_d, vec_ff, norms, nhats = ff_out[:5]
    ff_pay = ff_out[5:]
    from_ff = []
    if fast:
        ff_near = lax.ppermute(ff_pay[1], "fsdp", xor_pairs(nz, 1))
        from_ff = [ff_pay[2], ff_near]
    mixn, dqkvn = vmem_call(
        functools.partial(attn_body, n),
        [shape((seq, 64), BF16), shape((seq, 256), BF16)],
        scratch=[
            pltpu.VMEM((seq, 256), F32),
            pltpu.VMEM((seq, 64), BF16),
            pltpu.VMEM((seq, 64), BF16),
            pltpu.VMEM((seq, 64), BF16),
            pltpu.VMEM((seq, 64), BF16),
            pltpu.VMEM((seq, 64), BF16),
            pltpu.VMEM((64, seq), F32),
            pltpu.VMEM((64, seq), F32),
            pltpu.VMEM((seq, 128), F32),
            pltpu.VMEM((seq, 256), BF16),
        ],
        n_smem=2,
        n_in=n + 5,
        cost=pl.CostEstimate(flops=6_000_000_000, bytes_accessed=0, transcendentals=0),
        name="attention",
    )(place, order, *pieces, w_all, params, head_w, turn, norms)
    ends_out = vmem_call(
        functools.partial(ends_body, n, nz, fast),
        [shape(half, BF16), shape(half, BF16), shape((HEAD_DIM, D), BF16)] + attn_pays,
        scratch=[
            pltpu.VMEM((128, 128), F32),
            pltpu.VMEM((seq, D), BF16),
            pltpu.VMEM((D, 256), F32),
            pltpu.VMEM((8, D), F32),
        ],
        n_smem=1,
        n_in=n + 10 + len(from_ff),
        cost=pl.CostEstimate(flops=3_000_000_000, bytes_accessed=0, transcendentals=0),
        name="ends",
    )(place, *pieces, mixn, dqkvn, norms, nhats, acc_o, acc_d, vec_ff, w_all, head_w, params, *from_ff)
    keep_pay, send_pay, g_out = ends_out[:3]
    attn_pay = ends_out[3:]

    came = lax.ppermute(send_pay, "ctx", xor_pairs(n, 1))
    if fast:
        chip_out = vmem_call(
            functools.partial(chip_fast_body, 0),
            [shape((2, TOK, D), BF16)] * 2 + [shape((TOK, 2 * D), BF16)] + [shape((TOK, D), BF16)] * 2 + [],
            n_in=2 + 0,
            cost=LONGER,
            name="chip_sum",
        )(keep_pay, came)
        first_a, first_b, own_sum, kept_a, kept_b = chip_out[:5]
        came_a = lax.ppermute(first_a, "ctx", xor_pairs(n, 2))
        came_b = lax.ppermute(first_b, "ctx", xor_pairs(n, 4))
        cross_out = vmem_call(
            functools.partial(cross_body, 0),
            [shape((TOK, D), BF16)] * 2 + [],
            n_in=4 + 0,
            cost=LONGER,
            name="cross",
        )(kept_a, kept_b, came_a, came_b)
        second_a, second_b = cross_out[:2]
        parts = [own_sum, came_a, came_b]
        parts += [lax.ppermute(second_a, "ctx", xor_pairs(n, 4)), lax.ppermute(second_b, "ctx", xor_pairs(n, 2))]
    else:
        chip_sum = vmem_call(chip_body, [shape((TOK, 2 * D), BF16)] * (n // 2), n_in=2, name="chip_sum")(keep_pay, came)
        parts = [chip_sum[0]] + [lax.ppermute(chip_sum[k // 2], "ctx", xor_pairs(n, k)) for k in range(2, n, 2)]
    output, grad_inputs = vmem_call(
        functools.partial(close_body, fast),
        (shape((TOK, D), BF16), shape((TOK, D))),
        n_smem=1,
        n_in=3 + len(parts),
        name="close",
    )(place, x, g, params, *parts)

    if fast:
        out_got = lax.ppermute(g_out, ("ctx", "fsdp"), [(b, a) for a, b in pairs])
        ff_far = lax.ppermute(attn_pay[3], "fsdp", xor_pairs(nz, 2))
        attn_near = lax.ppermute(attn_pay[1], "fsdp", xor_pairs(nz, 1))
        attn_two = vmem_call(relay_body, shape((rows, 256), BF16), n_in=2, cost=LONG, name="relay")(attn_pay[2], attn_near)
        attn_far = lax.ppermute(attn_two, "fsdp", xor_pairs(nz, 2))
        out_got = vmem_call(gate_body, shape(out_got.shape, BF16), n_in=1, cost=LONGER, name="gate")(out_got)
        share = vmem_call(share_body, shape((rows, 1024), BF16), n_in=7 + 2, name="share")(
            ff_pay[0], ff_near, ff_far, attn_pay[0], attn_near, attn_far, out_got, parts[3], parts[4]
        )
        alls = gather_ctx(share, n)
        dz = D // nz
        outs = vmem_call(
            functools.partial(finish_body, n, nz),
            [
                shape((dz,)),
                shape((dz,)),
                shape((dz, 3 * D)),
                shape((3 * dz,)),
                shape((dz, D)),
                shape((dz,)),
                shape((dz,)),
                shape((dz,)),
                shape((dz, FF)),
                shape((FF // nz,)),
                shape((FF // nz, D)),
                shape((dz,)),
            ],
            scratch=[
                pltpu.VMEM((n, 128, 256), F32),
                pltpu.VMEM((n, 128, 256), F32),
                pltpu.VMEM((n, 8, D), F32),
                pltpu.VMEM((24, 128), F32),
            ],
            n_smem=1,
            n_in=n,
            name="finish",
        )(place, *alls)
    else:
        everyone = ("ctx", "fsdp")
        head = me // (n // HEADS)
        g_up, g_down = ff_pay
        g_qkv, vec = attn_pay

        def own(full, axis=0):
            size = full.shape[axis] // nz
            return lax.dynamic_slice_in_dim(full, zed * size, size, axis)

        def spread(part, dims, index, axis):
            full = jnp.zeros(dims, part.dtype)
            return lax.psum(lax.dynamic_update_index_in_dim(full, part, index, axis), everyone).astype(F32)

        qkv_full = spread(g_qkv[:, 0:192].reshape(D, 3, HEAD_DIM), (D, 3, HEADS, HEAD_DIM), head, 2).reshape(D, 3 * D)
        out_full = spread(g_out, (HEADS, HEAD_DIM, D), head, 0).reshape(D, D)
        up_full = spread(g_up, (D, n, width), me, 1).reshape(D, FF)
        down_full = spread(g_down, (n, width, D), me, 0).reshape(FF, D)
        bq_full = spread(vec[5, 0:192].reshape(3, HEAD_DIM), (3, HEADS, HEAD_DIM), head, 1).reshape(3 * D)
        bu_full = spread(vec[6, 0:width], (n, width), me, 0).reshape(FF)
        flat = lax.psum(vec, everyone)
        b_full = flat[4] * (1.0 / n)
        outs = [own(v) for v in (flat[0], flat[1], qkv_full, bq_full, out_full, b_full)]
        outs += [own(v) for v in (flat[2], flat[3], up_full, bu_full, down_full, b_full)]
    return (output[None], grad_inputs[None], *outs)


def solution(mesh):
    rows, flat, tokens = P("fsdp", None), P("fsdp"), P("fsdp", "ctx", None)
    weights = (flat, flat, rows, flat, rows, flat, flat, flat, rows, flat, rows, flat)
    return jax.shard_map(
        functools.partial(per_device, mesh.shape["ctx"], mesh.shape["fsdp"]),
        mesh=mesh,
        in_specs=(tokens, P(), *weights, tokens),
        out_specs=(tokens, tokens, *weights),
        check_vma=False,
    )
```

```python
import functools

import jax
import jax.numpy as jnp
import numpy as np
from jax import lax
from jax.experimental import pallas as pl
from jax.experimental.pallas import tpu as pltpu
from jax.sharding import PartitionSpec as P

HEADS = 8
HEAD_DIM = 64
D = 512
FF = 2048
ROT = 16
HALF = 64
TOK = 128
EPS = 1e-05
F32 = jnp.float32
BF16 = jnp.bfloat16
VMEM_LIMIT = 32 * 1024 * 1024
WIDE_LIMIT = 60 * 1024 * 1024
LONGER = pl.CostEstimate(flops=30_000_000_000, bytes_accessed=0, transcendentals=0)
LONG = pl.CostEstimate(flops=12_000_000_000, bytes_accessed=0, transcendentals=0)


def mm(left, right, dims):
    return lax.dot_general(left, right, (dims, ((), ())), preferred_element_type=F32)


def mm_nn(left, right):
    return mm(left, right, ((1,), (0,)))


def mm_nt(left, right):
    return mm(left, right, ((1,), (1,)))


def mm_tn(left, right):
    return mm(left, right, ((0,), (0,)))


def vmem_call(body, out_shape, scratch=(), n_smem=0, n_in=0, n_any=0, cost=None, name=None):
    smem = pl.BlockSpec(memory_space=pltpu.SMEM)
    vmem = pl.BlockSpec(memory_space=pltpu.VMEM)
    return pl.pallas_call(
        body,
        out_shape=out_shape,
        in_specs=[smem] * n_smem + [vmem] * n_in + [pl.BlockSpec(memory_space=pl.ANY)] * n_any,
        out_specs=jax.tree.map(lambda _: vmem, out_shape),
        scratch_shapes=list(scratch),
        compiler_params=pltpu.CompilerParams(vmem_limit_bytes=VMEM_LIMIT),
        cost_estimate=cost,
        name=name,
    )


def half_pick(block, odd, to_upper):
    moved = pltpu.roll(block, 64, 1)
    return jnp.where(odd, block if to_upper else moved, moved if to_upper else block)


def low_lanes(shape):
    return lax.broadcasted_iota(jnp.int32, shape, len(shape) - 1) % 128 < 64


def pack_body(nz, place, *refs):
    q_ref, k_ref, v_ref = refs[:3]
    ups = refs[3 : 3 + nz]
    w_down, w_out, x, g = refs[3 + nz : 7 + nz]
    vectors = refs[7 + nz : 15 + nz]
    pay, piece, head_w, small = refs[15 + nz :]
    odd = (place[0] % 2) == 1
    rows = q_ref.shape[0]
    low = low_lanes((rows, 128))
    small[...] = jnp.zeros_like(small)
    at = 0
    for vector in vectors:
        for r in range(vector.shape[0] // 128):
            small[at : at + 1, :] = vector[r * 128 : (r + 1) * 128].astype(F32).reshape(1, 128)
            at += 1
    few = small[...]
    spare = jnp.concatenate([pltpu.roll(few, 64, 1), few, jnp.zeros((rows - 32, 128), F32)], axis=0)
    q = half_pick(q_ref[...].astype(F32), odd, False)
    k = half_pick(k_ref[...].astype(F32), odd, True)
    v = half_pick(v_ref[...].astype(F32), odd, False)
    pay[:, 0:128] = jnp.where(low, q, k).astype(BF16)
    pay[:, 128:256] = jnp.where(low, v, spare).astype(BF16)
    for z in range(0, nz, 2):
        even = half_pick(ups[z][...].astype(F32), odd, False)
        later = half_pick(ups[z + 1][...].astype(F32), odd, True)
        pay[:, 256 + z * 64 : 256 + z * 64 + 128] = jnp.where(low, even, later).astype(BF16)
    pay[0:64, 512:768] = w_down[:, 0:256]
    pay[64:128, 512:768] = w_down[:, 256:512]
    head_w[...] = w_out[...]
    piece[0:TOK, :] = x[0]
    piece[TOK : 2 * TOK, :] = g[0]


def pack_call(nz, place, w_qkv, w_up, w_down, w_out, x, g, vectors):
    span = FF // nz // 128
    rows = D // nz

    def lane_block(first):
        return pl.BlockSpec((rows, 128), lambda i, s: (0, first + s[0] // 2))

    def whole(array):
        rank = array.ndim
        return pl.BlockSpec(array.shape, lambda i, s: (0,) * rank)

    outs = [shape((rows, 768), BF16), shape((2 * TOK, D), BF16), shape((HEAD_DIM, D), BF16)]
    return pl.pallas_call(
        functools.partial(pack_body, nz),
        out_shape=outs,
        grid_spec=pltpu.PrefetchScalarGridSpec(
            num_scalar_prefetch=1,
            grid=(1,),
            in_specs=[lane_block(0), lane_block(D // 128), lane_block(2 * D // 128)]
            + [lane_block(z * span) for z in range(nz)]
            + [
                pl.BlockSpec((64, D), lambda i, s: (s[0], 0)),
                pl.BlockSpec((HEAD_DIM, D), lambda i, s: (s[0] % 2, 0)),
                whole(x),
                whole(g),
            ]
            + [whole(v) for v in vectors],
            out_specs=[whole(o) for o in outs],
            scratch_shapes=[pltpu.VMEM((16, 128), F32)],
        ),
        compiler_params=pltpu.CompilerParams(vmem_limit_bytes=WIDE_LIMIT),
        name="pack",
    )(place, w_qkv, w_qkv, w_qkv, *([w_up] * nz), w_down, w_out, x, g, *vectors)


def unpack_body(nz, place, *refs):
    pieces = refs[:nz]
    w_all, w_up, w_down, params, held = refs[nz:]
    me, zed = place[0], place[1]
    pair = me // 2
    odd = (me % 2) == 1
    for k in range(nz):
        z = zed ^ k
        tall = pl.ds(pl.multiple_of(z * 128, 128), 128)
        flat = pl.ds(pl.multiple_of(z * 64, 64), 64)
        w_all[tall, 0:128] = pieces[k][:, 0:128]
        third = pieces[k][:, 128:256].astype(F32)
        w_all[tall, 128:256] = jnp.where(low_lanes((128, 128)), third, 0.0).astype(BF16)
        held[z] = jnp.where(low_lanes((16, 128)), pltpu.roll(third[0:16], 64, 1), third[16:32])
        w_up[tall, :] = pieces[k][:, 256:512]
        w_down[flat, 0:256] = pieces[k][0:64, 512:768]
        w_down[flat, 256:512] = pieces[k][64:128, 512:768]
    params[...] = jnp.zeros_like(params)
    for z in range(nz):
        lanes = slice(z * 128, (z + 1) * 128)
        params[0:4, lanes] = held[z, 0:4, :]
        params[4:5, lanes] = held[z, 4:5, :] + held[z, 5:6, :]
    low = low_lanes((1, 128))

    def qkv_row(group):
        index = group * 4 + pair
        z = index // 3
        return held[z, pl.ds(6 + index - 3 * z, 1), :]

    q = half_pick(qkv_row(0), odd, False)
    k = half_pick(qkv_row(1), odd, True)
    v = half_pick(qkv_row(2), odd, False)
    params[5:6, 0:128] = jnp.where(low, q, k)
    params[5:6, 128:256] = jnp.where(low, v, 0.0)
    for z in range(0, nz, 2):
        even = half_pick(held[z, pl.ds(9 + pair, 1), :], odd, False)
        later = half_pick(held[z + 1, pl.ds(9 + pair, 1), :], odd, True)
        params[6:7, z * 64 : z * 64 + 128] = jnp.where(low, even, later)


def normalized(x):
    center = x - jnp.mean(x, axis=-1, keepdims=True)
    spread = jnp.mean(center * center, axis=-1, keepdims=True)
    inv = lax.rsqrt(spread + EPS)
    return center * inv, inv


def joined(pieces, first):
    if len(pieces) == 1:
        return pieces[0][first : first + TOK, :]
    return jnp.concatenate([piece[first : first + TOK, :] for piece in pieces], axis=0)


def fold(values):
    return jnp.sum(values.reshape(values.shape[0] // 8, 8, values.shape[1]), axis=0)


def ff_body(n, nz, fast, place, *refs):
    pieces = refs[:n]
    w_up, w_down, params = refs[n : n + 3]
    outs = refs[n + 3 :]
    n_pay = nz if fast else 2
    acc_o, acc_d, vec, norms, nhats = outs[:5]
    pays = outs[5 : 5 + n_pay]
    norm2s, hiddens, dpres, gs, grad_up, grad_down = outs[5 + n_pay :]
    width = w_up.shape[1]
    zed = place[1]
    gain, shift = params[0:1, :], params[1:2, :]
    gain2, shift2 = params[2:3, :], params[3:4, :]
    b_up = params[6:7, 0:width]
    g_gain = jnp.zeros((8, D), F32)
    g_shift = jnp.zeros((8, D), F32)
    g_sum = jnp.zeros((8, D), F32)
    g_bup = jnp.zeros((8, width), F32)
    for p in range(0, n, 4):
        rows = slice(p * TOK, (p + 4) * TOK)
        nhat, _ = normalized(joined(pieces[p : p + 4], 0).astype(F32))
        g = joined(pieces[p : p + 4], TOK)
        norms[rows, :] = (nhat * gain + shift).astype(BF16)
        nhats[rows, :] = nhat.astype(BF16)
        norm2 = (nhat * gain2 + shift2).astype(BF16)
        pre = mm_nn(norm2, w_up[...]) + b_up
        cdf = 0.5 * (1.0 + lax.erf(pre * 0.7071067811865476))
        hidden = (pre * cdf).astype(BF16)
        slope = cdf + pre * (0.3989422804014327 * jnp.exp(-0.5 * pre * pre))
        dpre = (mm_nt(g, w_down[...]) * slope).astype(BF16)
        dnorm = mm_nt(dpre, w_up[...])
        acc_o[rows, :] = mm_nn(hidden, w_down[...]).astype(BF16)
        acc_d[rows, :] = (dnorm * gain2).astype(BF16)
        g_gain += fold(dnorm * nhat)
        g_shift += fold(dnorm)
        g_sum += fold(g.astype(F32))
        g_bup += fold(dpre.astype(F32))
        norm2s[rows, :] = norm2
        hiddens[rows, :] = hidden
        dpres[rows, :] = dpre
        gs[rows, :] = g
    vec[...] = jnp.zeros_like(vec)
    for row, value in ((2, g_gain), (3, g_shift), (4, g_sum), (6, g_bup)):
        vec[row : row + 1, 0 : value.shape[1]] = jnp.sum(value, axis=0, keepdims=True)
    grad_up[...] = mm_tn(dpres[...], norm2s[...]).T.astype(BF16)
    grad_down[...] = mm_tn(hiddens[...], gs[...]).astype(BF16)
    if fast:
        for k, target in enumerate(pays):
            z = zed ^ k
            tall = pl.ds(pl.multiple_of(z * 128, 128), 128)
            flat = pl.ds(pl.multiple_of(z * 64, 64), 64)
            target[:, 0:256] = grad_up[tall, :]
            target[0:64, 256:512] = grad_down[flat, 0:256]
            target[64:128, 256:512] = grad_down[flat, 256:512]
    else:
        pays[0][...] = grad_up[...]
        pays[1][...] = grad_down[...]


def attn_body(n, place, order, *refs):
    seq = n * TOK
    qblk = min(512, seq)
    pieces = refs[:n]
    w_all, params, w_out, turn, norms = refs[n : n + 5]
    mixn, dqkvn = refs[n + 5 : n + 7]
    raw, qs, ks, vs, dms, mixs, dks, dvs, dqs, dqkvs = refs[n + 7 :]
    bias = params[5:6, 0:256]

    def sorted_rows(block):
        return pl.ds(pl.multiple_of(order[block] * HALF, HALF), HALF)

    for p in range(0, n, 2):
        rows = slice(p * TOK, (p + 2) * TOK)
        qkv = mm_nn(norms[rows, :], w_all[...]) + bias
        dmix = mm_nt(joined(pieces[p : p + 2], TOK), w_out[...]).astype(BF16)
        for h in range(2 * TOK // HALF):
            here = slice(h * HALF, (h + 1) * HALF)
            where = sorted_rows(p * (TOK // HALF) + h)
            raw[where, :] = qkv[here, :]
            dms[where, :] = dmix[here, :]

    lanes = lax.broadcasted_iota(jnp.int32, (qblk, 128), 1) % 64

    def both_heads(t):
        moved = pltpu.roll(t, 64, 1)
        low = low_lanes(t.shape)
        return jnp.where(low, t, moved), jnp.where(low, moved, t)

    def swapped(t):
        return jnp.where(lanes < ROT // 2, pltpu.roll(t, 128 - ROT // 2, 1), pltpu.roll(t, ROT // 2, 1))

    for i in range(seq // qblk):
        rows = slice(i * qblk, (i + 1) * qblk)
        qk = raw[rows, 0:128]
        cos_t, sin_t = both_heads(turn[rows, :])
        turned = (qk * cos_t + swapped(qk) * sin_t).astype(BF16)
        qs[rows, :] = turned[:, 0:64] * jnp.asarray(0.125, BF16)
        ks[rows, :] = turned[:, 64:128]
        vs[rows, :] = raw[rows, 128:192].astype(BF16)

    q_at = lax.broadcasted_iota(jnp.int32, (qblk, qblk), 0)
    k_at = lax.broadcasted_iota(jnp.int32, (qblk, qblk), 1)
    causal = q_at >= k_at
    dks[...] = jnp.zeros_like(dks)
    dvs[...] = jnp.zeros_like(dvs)
    for i in range(seq // qblk):
        rows = slice(i * qblk, (i + 1) * qblk)
        span = (i + 1) * qblk
        q = qs[rows, :]
        keys = ks[0:span, :]
        values = vs[0:span, :]
        s = jnp.where(causal, mm_nt(q, ks[rows, :]), -1e30)
        if i:
            s = jnp.concatenate([mm_nt(q, ks[0 : i * qblk, :]), s], axis=1)
        top = jnp.max(s, axis=1, keepdims=True)
        e = jnp.exp(s - top)
        inv = 1.0 / jnp.sum(e, axis=1, keepdims=True)
        e_b = e.astype(BF16)
        mix = mm_nn(e_b, values) * inv
        mixs[rows, :] = mix.astype(BF16)
        dmix = (dms[rows, :].astype(F32) * inv).astype(BF16)
        delta = jnp.sum(dmix.astype(F32) * mix, axis=1, keepdims=True)
        ds = (e * (mm_nt(dmix, values) - delta)).astype(BF16)
        dqs[rows, 0:64] = mm_nn(ds, keys) * 0.125
        dks[:, 0:span] += mm_tn(q, ds)
        dvs[:, 0:span] += mm_tn(dmix, e_b)
    dqs[:, 64:128] = dks[...].T
    dqkvs[:, 128:192] = dvs[...].T.astype(BF16)
    dqkvs[:, 192:256] = jnp.zeros((seq, 64), BF16)
    for i in range(seq // qblk):
        rows = slice(i * qblk, (i + 1) * qblk)
        dqk = dqs[rows, :]
        cos_t, sin_t = both_heads(turn[rows, :])
        dqkvs[rows, 0:128] = (dqk * cos_t - swapped(dqk) * sin_t).astype(BF16)

    scale = None
    if n > HEADS:
        scale = jnp.where(place[0] % (n // HEADS) == 0, 1.0, 0.0).astype(BF16)
    for b in range(seq // HALF):
        here = slice(b * HALF, (b + 1) * HALF)
        where = sorted_rows(b)
        mix, dqkv = mixs[where, :], dqkvs[where, :]
        if scale is not None:
            mix, dqkv = mix * scale, dqkv * scale
        mixn[here, :] = mix
        dqkvn[here, :] = dqkv


def ends_body(n, nz, fast, place, *refs):
    pieces = refs[:n]
    mixn, dqkvn, norms, nhats, acc_o, acc_d, vec_in, w_all, w_out, params = refs[n : n + 10]
    at = n + 10
    if fast:
        ff_one, ff_two, ff_came = refs[at : at + 3]
        at += 3
    keep_pay, send_pay, g_out = refs[at : at + 3]
    n_pay = 4 if fast else 2
    pays = refs[at + 3 : at + 3 + n_pay]
    spare, gs, grad_w, vec = refs[at + 3 + n_pay :]
    zed = place[1]
    gain = params[0:1, :]
    g_gain = jnp.zeros((8, D), F32)
    g_shift = jnp.zeros((8, D), F32)
    g_bias = jnp.zeros((8, 256), F32)
    for p in range(0, n, 2):
        rows = slice(p * TOK, (p + 2) * TOK)
        gs[rows, :] = joined(pieces[p : p + 2], TOK)
        dqkv = dqkvn[rows, :]
        dnorm = mm_nt(dqkv, w_all[...])
        g_gain += fold(dnorm * nhats[rows, :].astype(F32))
        g_shift += fold(dnorm)
        g_bias += fold(dqkv.astype(F32))
        part_o = (mm_nn(mixn[rows, :], w_out[...]) + acc_o[rows, :].astype(F32)).astype(BF16)
        part_d = (dnorm * gain + acc_d[rows, :].astype(F32)).astype(BF16)
        for q in range(2):
            target = send_pay if (p + q) % 2 else keep_pay
            here = slice(q * TOK, (q + 1) * TOK)
            target[(p + q) // 2, :, 0:512] = part_o[here, :]
            target[(p + q) // 2, :, 512:1024] = part_d[here, :]
    vec[...] = vec_in[...]
    for row, value in ((0, g_gain), (1, g_shift), (5, g_bias)):
        vec[row : row + 1, 0 : value.shape[1]] = jnp.sum(value, axis=0, keepdims=True)
    g_out[...] = mm_tn(mixn[...], gs[...]).astype(BF16)
    grad_w[...] = mm_tn(dqkvn[...], norms[...]).T
    if fast:
        spare[...] = jnp.zeros_like(spare)
        for j in range(8):
            lanes_j = vec[:, (j // 2) * 128 : (j // 2) * 128 + 128]
            spare[8 * j : 8 * j + 8, :] = lanes_j if j % 2 else pltpu.roll(lanes_j, 64, 1)
        low = low_lanes((128, 128))
        own, near, two, ff_sum = pays
        near[:, 512:1024] = ff_one[...]
        for k, target in ((0, own), (1, near.at[:, 0:256]), (2, two), (3, near.at[:, 256:512])):
            tall = pl.ds(pl.multiple_of((zed ^ k) * 128, 128), 128)
            target[:, 0:128] = grad_w[tall, 0:128].astype(BF16)
            target[:, 128:256] = jnp.where(low, grad_w[tall, 128:256], spare[...]).astype(BF16)
        ff_sum[0:128, :] = (ff_two[...].astype(F32) + ff_came[...].astype(F32)).astype(BF16)
        ff_sum[128:192, :] = g_out[...]
    else:
        pays[0][...] = grad_w[...].astype(BF16)
        pays[1][...] = vec[...]


def close_body(fast, place, x_ref, g_ref, params, *refs):
    parts, out, grad = refs[:-2], refs[-2], refs[-1]
    x = x_ref[...].astype(F32)
    nhat, inv = normalized(x)
    if fast:
        own, came_a, came_b, last_a, last_b = parts
        total_o = own[:, 0:D].astype(F32) + came_a[0].astype(F32) + last_a[...].astype(F32)
        dn = own[:, D : 2 * D].astype(F32) + came_b[0].astype(F32) + last_b[...].astype(F32)
    else:
        total = parts[0][...].astype(F32)
        for part in parts[1:]:
            total = total + part[...].astype(F32)
        total_o, dn = total[:, 0:D], total[:, D : 2 * D]
    out[...] = (x + total_o + params[4:5, :]).astype(BF16)
    lead = jnp.mean(dn, axis=-1, keepdims=True)
    along = jnp.mean(dn * nhat, axis=-1, keepdims=True)
    grad[...] = g_ref[...].astype(F32) + inv * (dn - lead - nhat * along)


def chip_body(keep, came, *outs):
    for k, out in enumerate(outs):
        out[...] = (keep[k].astype(F32) + came[k].astype(F32)).astype(BF16)


def chip_fast_body(n_later, keep, came, *refs):
    later, (first_a, first_b, own, kept_a, kept_b, *held) = refs[:n_later], refs[n_later:]
    for value, copy in zip(later, held):
        copy[...] = value[...]

    def both(k, lanes):
        return (keep[k, :, lanes].astype(F32) + came[k, :, lanes].astype(F32)).astype(BF16)

    left, right = slice(0, D), slice(D, 2 * D)
    own[:, left] = both(0, left)
    own[:, right] = both(0, right)
    first_a[0] = both(1, left)
    first_a[1] = both(3, left)
    first_b[0] = both(2, right)
    first_b[1] = both(3, right)
    kept_a[...] = both(2, left)
    kept_b[...] = both(1, right)


def cross_body(n_later, kept_a, kept_b, came_a, came_b, *refs):
    later, (second_a, second_b, *held) = refs[:n_later], refs[n_later:]
    for value, copy in zip(later, held):
        copy[...] = value[...]
    second_a[...] = (kept_a[...].astype(F32) + came_a[1].astype(F32)).astype(BF16)
    second_b[...] = (kept_b[...].astype(F32) + came_b[1].astype(F32)).astype(BF16)


def gate_body(value, *refs):
    out = refs[-1]
    out[...] = value[...]


def relay_body(two, came, out):
    out[...] = (two[...].astype(F32) + came[:, 256:512].astype(F32)).astype(BF16)


def out_body(mine, came, out):
    out[...] = (mine[...].astype(F32) + came[128:192, :].astype(F32)).astype(BF16)


def share_body(ff_own, ff_far, own, near, far, out_half, out_far, *refs):
    out = refs[-1]
    out[:, 0:512] = (ff_own[...].astype(F32) + near[:, 512:1024].astype(F32) + ff_far[0:128, :].astype(F32)).astype(BF16)
    out[:, 512:768] = (own[...].astype(F32) + near[:, 0:256].astype(F32) + far[...].astype(F32)).astype(BF16)
    g_out = (out_half[...].astype(F32) + out_far[...].astype(F32)).astype(BF16)
    out[0:64, 768:1024] = g_out[:, 0:256]
    out[64:128, 768:1024] = g_out[:, 256:512]


def finish_body(n, nz, place, *refs):
    alls = refs[:n]
    (ln1g, ln1b, gqkv, bqkv, gout, bout, ln2g, ln2b, gup, bup, gdown, bdown) = refs[n : n + 12]
    held_u, held_a, held_v, flat = refs[n + 12 :]
    me, zed = place[0], place[1]
    span = FF // nz
    total = jnp.zeros((8, D), F32)
    wide = low_lanes((8, 128))
    for k in range(n):
        who = me ^ k
        held_a[who] = alls[k][:, 512:768].astype(F32)
        held_u[who] = alls[k][:, 0:256].astype(F32)
        rows = pl.ds(pl.multiple_of(who * 64, 64), 64)
        gdown[rows, 0:256] = alls[k][0:64, 256:512].astype(F32)
        gdown[rows, 256:512] = alls[k][64:128, 256:512].astype(F32)
        spare = alls[k][0:64, 640:768].astype(F32)
        small = []
        for j in range(0, 8, 2):
            small.append(jnp.where(wide, pltpu.roll(spare[8 * j : 8 * j + 8], 64, 1), spare[8 * j + 8 : 8 * j + 16]))
        small = jnp.concatenate(small, axis=1)
        held_v[who] = small
        total = total + small
    for h in range(0, n, 2):
        even, later = held_a[h], held_a[h + 1]
        low = low_lanes((128, 128))
        at = h * 64
        gqkv[:, at : at + 128] = jnp.where(low, even[:, 0:128], pltpu.roll(later[:, 0:128], 64, 1))
        gqkv[:, D + at : D + at + 128] = jnp.where(low, pltpu.roll(even[:, 0:128], 64, 1), later[:, 0:128])
        gqkv[:, 2 * D + at : 2 * D + at + 128] = jnp.where(low, even[:, 128:256], pltpu.roll(later[:, 128:256], 64, 1))
        for z in range(0, nz, 2):
            lanes = slice(z * 64, z * 64 + 128)
            e, l = held_u[h][:, lanes], held_u[h + 1][:, lanes]
            gup[:, z * span + at : z * span + at + 128] = jnp.where(low, e, pltpu.roll(l, 64, 1))
            gup[:, (z + 1) * span + at : (z + 1) * span + at + 128] = jnp.where(low, pltpu.roll(e, 64, 1), l)
        low = low_lanes((1, 128))
        e, l = held_v[h], held_v[h + 1]
        flat[h // 2 : h // 2 + 1, :] = jnp.where(low, e[5:6, 0:128], pltpu.roll(l[5:6, 0:128], 64, 1))
        flat[4 + h // 2 : 5 + h // 2, :] = jnp.where(low, pltpu.roll(e[5:6, 0:128], 64, 1), l[5:6, 0:128])
        flat[8 + h // 2 : 9 + h // 2, :] = jnp.where(low, e[5:6, 128:256], pltpu.roll(l[5:6, 128:256], 64, 1))
        lane = pl.ds(pl.multiple_of((zed // 2) * 128, 128), 128)
        odd = (zed % 2) == 1
        e = half_pick(held_v[h, 6:7, lane], odd, False)
        l = half_pick(held_v[h + 1, 6:7, lane], odd, True)
        bup[at : at + 128] = jnp.where(low, e, l).reshape(128)
    for k in range(n):
        held_a[me ^ k] = alls[k][:, 768:1024].astype(F32)
    for p in range(2):
        rows = held_a[2 * zed + p]
        gout[64 * p : 64 * p + 64, 0:256] = rows[0:64]
        gout[64 * p : 64 * p + 64, 256:512] = rows[64:128]
    flat[12:20, :] = jnp.zeros((8, 128), F32)
    for r in range(3):
        bqkv[r * 128 : (r + 1) * 128] = flat[pl.ds(zed * 3 + r, 1), :].reshape(128)
    held_v[0] = total
    lane = pl.ds(pl.multiple_of(zed * 128, 128), 128)
    ln1g[...] = held_v[0, 0:1, lane].reshape(128)
    ln1b[...] = held_v[0, 1:2, lane].reshape(128)
    ln2g[...] = held_v[0, 2:3, lane].reshape(128)
    ln2b[...] = held_v[0, 3:4, lane].reshape(128)
    held_v[1] = total * (1.0 / n)
    bout[...] = held_v[1, 4:5, lane].reshape(128)
    bdown[...] = held_v[1, 4:5, lane].reshape(128)


def xor_pairs(size, k):
    return [(i, i ^ k) for i in range(size)]


def gather_ctx(value, n):
    got = {0: value}
    for k in range(2, n, 2):
        got[k] = lax.ppermute(value, "ctx", xor_pairs(n, k))
    for k in range(0, n, 2):
        got[k + 1] = lax.ppermute(got[k], "ctx", xor_pairs(n, 1))
    return [got[k] for k in range(n)]


def gather_fsdp(value, nz):
    return [value] + [lax.ppermute(value, "fsdp", xor_pairs(nz, k)) for k in range(1, nz)]


def relay_fsdp(value, nz):
    one, two = (lax.ppermute(value, "fsdp", xor_pairs(nz, k)) for k in (1, 2))
    return [value, one, two, lax.ppermute(two, "fsdp", xor_pairs(nz, 1))]


def rotary_tables(seq):
    pos = np.arange(seq, dtype=np.float32)
    inverse = (np.float32(10000.0) ** (-np.arange(ROT // 2, dtype=np.float32) * np.float32(2.0) / np.float32(ROT))).astype(np.float32)
    angles = (pos[:, None] * inverse[None, :]).astype(np.float32).astype(np.float64)
    cos_t = np.ones((seq, 64), np.float32)
    sin_t = np.zeros((seq, 64), np.float32)
    half = ROT // 2
    cos_t[:, 0:half] = np.cos(angles)
    cos_t[:, half:ROT] = np.cos(angles)
    sin_t[:, 0:half] = -np.sin(angles)
    sin_t[:, half:ROT] = np.sin(angles)
    return np.concatenate([cos_t, sin_t], axis=1)


def shape(dims, dtype=F32):
    return jax.ShapeDtypeStruct(dims, dtype)


def per_device(
    n,
    nz,
    inputs,
    block_order,
    ln1_gain,
    ln1_bias,
    w_qkv,
    b_qkv,
    w_attn_out,
    b_attn_out,
    ln2_gain,
    ln2_bias,
    w_up,
    b_up,
    w_down,
    b_down,
    cotangent,
):
    fast = n == HEADS and nz * 2 == HEADS
    seq = n * TOK
    width = FF // n
    me = lax.axis_index("ctx").astype(jnp.int32)
    zed = lax.axis_index("fsdp").astype(jnp.int32)
    place = jnp.stack([me, zed])
    x, g = inputs[0], cotangent[0]
    blocks = TOK // HALF
    chunk_at = (jnp.arange(n, dtype=jnp.int32) ^ me)[:, None] * blocks + jnp.arange(blocks, dtype=jnp.int32)[None, :]
    pick = chunk_at.reshape(-1)[:, None] == jnp.arange(n * blocks, dtype=jnp.int32)[None, :]
    order = jnp.sum(jnp.where(pick, block_order[None, :], 0), axis=1).astype(jnp.int32)
    turn = rotary_tables(seq)

    if fast:
        vectors = (ln1_gain, ln1_bias, ln2_gain, ln2_bias, b_attn_out, b_down, b_qkv, b_up)
        pack, piece, pack_w = pack_call(nz, place, w_qkv, w_up, w_down, w_attn_out, inputs, cotangent, vectors)
        pieces = gather_ctx(piece, n)
        far = relay_fsdp(pack, nz)
        given = vmem_call(
            functools.partial(unpack_body, nz),
            [shape((D, 256), BF16), shape((D, width), BF16), shape((width, D), BF16), shape((8, D))],
            scratch=[pltpu.VMEM((nz, 16, 128), F32)],
            n_smem=1,
            n_in=nz,
            cost=LONG,
            name="unpack",
        )(place, *far)
        pairs = []
        for c in range(n):
            for z in range(nz):
                pairs.append((c * nz + z, (2 * z + c % 2) * nz + c // 2))
        pack_w = vmem_call(gate_body, shape(pack_w.shape, BF16), n_in=2, name="gate_w")(pack_w, far[1])
        head_w = lax.ppermute(pack_w, ("ctx", "fsdp"), pairs)
    else:
        whole = [
            lax.all_gather(v, "fsdp", axis=0, tiled=True)
            for v in (ln1_gain, ln1_bias, ln2_gain, ln2_bias, b_attn_out, b_down, b_qkv, b_up)
        ]
        whole = [v.astype(F32) for v in whole]
        head = me // (n // HEADS)
        bq = lax.dynamic_index_in_dim(whole[6].reshape(3, HEADS, HEAD_DIM), head, 1, False).reshape(-1)
        bu = lax.dynamic_index_in_dim(whole[7].reshape(n, width), me, 0, False)
        params = jnp.stack(
            [whole[0], whole[1], whole[2], whole[3], whole[4] + whole[5]]
            + [jnp.pad(bq, (0, D - 3 * HEAD_DIM)), jnp.pad(bu, (0, D - width)), jnp.zeros((D,), F32)]
        )
        wq = lax.dynamic_index_in_dim(w_qkv.reshape(-1, 3, HEADS, HEAD_DIM), head, 2, False).reshape(-1, 3 * HEAD_DIM)
        given = [jnp.pad(lax.all_gather(wq, "fsdp", axis=0, tiled=True), ((0, 0), (0, 64)))]
        wu = lax.dynamic_slice_in_dim(w_up, me * width, width, 1)
        wd = lax.all_gather(w_down, "fsdp", axis=0, tiled=True)
        given += [lax.all_gather(wu, "fsdp", axis=0, tiled=True), lax.dynamic_slice_in_dim(wd, me * width, width, 0)]
        wo = lax.all_gather(w_attn_out, "fsdp", axis=0, tiled=True)
        given.append(params)
        pieces = gather_ctx(jnp.concatenate([x, g], axis=0), n)
        head_w = lax.dynamic_slice_in_dim(wo, head * HEAD_DIM, HEAD_DIM, 0)

    w_all, w_up_c, w_down_c, params = given
    whole_seq = shape((seq, D), BF16)
    half = (n // 2, TOK, 2 * D)
    rows = D // nz
    if fast:
        ff_pays = [shape((rows, 512), BF16)] * nz
        attn_pays = [shape((rows, 256), BF16), shape((rows, 1024), BF16), shape((rows, 256), BF16), shape((rows + HEAD_DIM, 512), BF16)]
    else:
        ff_pays = [shape((D, width), BF16), shape((width, D), BF16)]
        attn_pays = [shape((D, 256), BF16), shape((8, D))]
    ff_out = vmem_call(
        functools.partial(ff_body, n, nz, fast),
        [whole_seq, whole_seq, shape((8, D)), whole_seq, whole_seq] + ff_pays,
        scratch=[
            pltpu.VMEM((seq, D), BF16),
            pltpu.VMEM((seq, width), BF16),
            pltpu.VMEM((seq, width), BF16),
            pltpu.VMEM((seq, D), BF16),
            pltpu.VMEM((D, width), BF16),
            pltpu.VMEM((width, D), BF16),
        ],
        n_smem=1,
        n_in=n + 3,
        cost=pl.CostEstimate(flops=4_000_000_000, bytes_accessed=0, transcendentals=0),
        name="feed_forward",
    )(place, *pieces, w_up_c, w_down_c, params)
    acc_o, acc_d, vec_ff, norms, nhats = ff_out[:5]
    ff_pay = ff_out[5:]
    from_ff = []
    if fast:
        ff_pass = lax.ppermute(ff_pay[3], "fsdp", xor_pairs(nz, 1))
        from_ff = [ff_pay[1], ff_pay[2], ff_pass]
    mixn, dqkvn = vmem_call(
        functools.partial(attn_body, n),
        [shape((seq, 64), BF16), shape((seq, 256), BF16)],
        scratch=[
            pltpu.VMEM((seq, 256), F32),
            pltpu.VMEM((seq, 64), BF16),
            pltpu.VMEM((seq, 64), BF16),
            pltpu.VMEM((seq, 64), BF16),
            pltpu.VMEM((seq, 64), BF16),
            pltpu.VMEM((seq, 64), BF16),
            pltpu.VMEM((64, seq), F32),
            pltpu.VMEM((64, seq), F32),
            pltpu.VMEM((seq, 128), F32),
            pltpu.VMEM((seq, 256), BF16),
        ],
        n_smem=2,
        n_in=n + 5,
        cost=pl.CostEstimate(flops=6_000_000_000, bytes_accessed=0, transcendentals=0),
        name="attention",
    )(place, order, *pieces, w_all, params, head_w, turn, norms)
    ends_out = vmem_call(
        functools.partial(ends_body, n, nz, fast),
        [shape(half, BF16), shape(half, BF16), shape((HEAD_DIM, D), BF16)] + attn_pays,
        scratch=[
            pltpu.VMEM((128, 128), F32),
            pltpu.VMEM((seq, D), BF16),
            pltpu.VMEM((D, 256), F32),
            pltpu.VMEM((8, D), F32),
        ],
        n_smem=1,
        n_in=n + 10 + len(from_ff),
        cost=pl.CostEstimate(flops=3_000_000_000, bytes_accessed=0, transcendentals=0),
        name="ends",
    )(place, *pieces, mixn, dqkvn, norms, nhats, acc_o, acc_d, vec_ff, w_all, head_w, params, *from_ff)
    keep_pay, send_pay, g_out = ends_out[:3]
    attn_pay = ends_out[3:]

    came = lax.ppermute(send_pay, "ctx", xor_pairs(n, 1))
    if fast:
        chip_out = vmem_call(
            functools.partial(chip_fast_body, 0),
            [shape((2, TOK, D), BF16)] * 2 + [shape((TOK, 2 * D), BF16)] + [shape((TOK, D), BF16)] * 2 + [],
            n_in=2 + 0,
            cost=LONGER,
            name="chip_sum",
        )(keep_pay, came)
        first_a, first_b, own_sum, kept_a, kept_b = chip_out[:5]
        came_a = lax.ppermute(first_a, "ctx", xor_pairs(n, 2))
        came_b = lax.ppermute(first_b, "ctx", xor_pairs(n, 4))
        cross_out = vmem_call(
            functools.partial(cross_body, 0),
            [shape((TOK, D), BF16)] * 2 + [],
            n_in=4 + 0,
            cost=LONGER,
            name="cross",
        )(kept_a, kept_b, came_a, came_b)
        second_a, second_b = cross_out[:2]
        parts = [own_sum, came_a, came_b]
        parts += [lax.ppermute(second_a, "ctx", xor_pairs(n, 4)), lax.ppermute(second_b, "ctx", xor_pairs(n, 2))]
    else:
        chip_sum = vmem_call(chip_body, [shape((TOK, 2 * D), BF16)] * (n // 2), n_in=2, name="chip_sum")(keep_pay, came)
        parts = [chip_sum[0]] + [lax.ppermute(chip_sum[k // 2], "ctx", xor_pairs(n, k)) for k in range(2, n, 2)]
    output, grad_inputs = vmem_call(
        functools.partial(close_body, fast),
        (shape((TOK, D), BF16), shape((TOK, D))),
        n_smem=1,
        n_in=3 + len(parts),
        name="close",
    )(place, x, g, params, *parts)

    if fast:
        ff_far = lax.ppermute(attn_pay[3], "fsdp", xor_pairs(nz, 2))
        out_half = vmem_call(out_body, shape((HEAD_DIM, D), BF16), n_in=2, cost=LONG, name="out_half")(g_out, ff_far)
        out_far = lax.ppermute(out_half, "fsdp", xor_pairs(nz, 1))
        attn_near = lax.ppermute(attn_pay[1], "fsdp", xor_pairs(nz, 1))
        attn_two = vmem_call(relay_body, shape((rows, 256), BF16), n_in=2, cost=LONG, name="relay")(attn_pay[2], attn_near)
        attn_far = lax.ppermute(attn_two, "fsdp", xor_pairs(nz, 2))
        share = vmem_call(share_body, shape((rows, 1024), BF16), n_in=7 + 2, name="share")(
            ff_pay[0], ff_far, attn_pay[0], attn_near, attn_far, out_half, out_far, parts[3], parts[4]
        )
        alls = gather_ctx(share, n)
        dz = D // nz
        outs = vmem_call(
            functools.partial(finish_body, n, nz),
            [
                shape((dz,)),
                shape((dz,)),
                shape((dz, 3 * D)),
                shape((3 * dz,)),
                shape((dz, D)),
                shape((dz,)),
                shape((dz,)),
                shape((dz,)),
                shape((dz, FF)),
                shape((FF // nz,)),
                shape((FF // nz, D)),
                shape((dz,)),
            ],
            scratch=[
                pltpu.VMEM((n, 128, 256), F32),
                pltpu.VMEM((n, 128, 256), F32),
                pltpu.VMEM((n, 8, D), F32),
                pltpu.VMEM((24, 128), F32),
            ],
            n_smem=1,
            n_in=n,
            name="finish",
        )(place, *alls)
    else:
        everyone = ("ctx", "fsdp")
        head = me // (n // HEADS)
        g_up, g_down = ff_pay
        g_qkv, vec = attn_pay

        def own(full, axis=0):
            size = full.shape[axis] // nz
            return lax.dynamic_slice_in_dim(full, zed * size, size, axis)

        def spread(part, dims, index, axis):
            full = jnp.zeros(dims, part.dtype)
            return lax.psum(lax.dynamic_update_index_in_dim(full, part, index, axis), everyone).astype(F32)

        qkv_full = spread(g_qkv[:, 0:192].reshape(D, 3, HEAD_DIM), (D, 3, HEADS, HEAD_DIM), head, 2).reshape(D, 3 * D)
        out_full = spread(g_out, (HEADS, HEAD_DIM, D), head, 0).reshape(D, D)
        up_full = spread(g_up, (D, n, width), me, 1).reshape(D, FF)
        down_full = spread(g_down, (n, width, D), me, 0).reshape(FF, D)
        bq_full = spread(vec[5, 0:192].reshape(3, HEAD_DIM), (3, HEADS, HEAD_DIM), head, 1).reshape(3 * D)
        bu_full = spread(vec[6, 0:width], (n, width), me, 0).reshape(FF)
        flat = lax.psum(vec, everyone)
        b_full = flat[4] * (1.0 / n)
        outs = [own(v) for v in (flat[0], flat[1], qkv_full, bq_full, out_full, b_full)]
        outs += [own(v) for v in (flat[2], flat[3], up_full, bu_full, down_full, b_full)]
    return (output[None], grad_inputs[None], *outs)


def solution(mesh):
    rows, flat, tokens = P("fsdp", None), P("fsdp"), P("fsdp", "ctx", None)
    weights = (flat, flat, rows, flat, rows, flat, flat, flat, rows, flat, rows, flat)
    return jax.shard_map(
        functools.partial(per_device, mesh.shape["ctx"], mesh.shape["fsdp"]),
        mesh=mesh,
        in_specs=(tokens, P(), *weights, tokens),
        out_specs=(tokens, tokens, *weights),
        check_vma=False,
    )
```

```python
import functools

import jax
import jax.numpy as jnp
import numpy as np
from jax import lax
from jax.experimental import pallas as pl
from jax.experimental.pallas import tpu as pltpu
from jax.sharding import PartitionSpec as P

HEADS = 8
HEAD_DIM = 64
D = 512
FF = 2048
ROT = 16
HALF = 64
TOK = 128
EPS = 1e-05
F32 = jnp.float32
BF16 = jnp.bfloat16
VMEM_LIMIT = 32 * 1024 * 1024
WIDE_LIMIT = 60 * 1024 * 1024
LONGER = pl.CostEstimate(flops=30_000_000_000, bytes_accessed=0, transcendentals=0)
LONG = pl.CostEstimate(flops=12_000_000_000, bytes_accessed=0, transcendentals=0)


def mm(left, right, dims):
    return lax.dot_general(left, right, (dims, ((), ())), preferred_element_type=F32)


def mm_nn(left, right):
    return mm(left, right, ((1,), (0,)))


def mm_nt(left, right):
    return mm(left, right, ((1,), (1,)))


def mm_tn(left, right):
    return mm(left, right, ((0,), (0,)))


def vmem_call(body, out_shape, scratch=(), n_smem=0, n_in=0, n_any=0, cost=None, name=None):
    smem = pl.BlockSpec(memory_space=pltpu.SMEM)
    vmem = pl.BlockSpec(memory_space=pltpu.VMEM)
    return pl.pallas_call(
        body,
        out_shape=out_shape,
        in_specs=[smem] * n_smem + [vmem] * n_in + [pl.BlockSpec(memory_space=pl.ANY)] * n_any,
        out_specs=jax.tree.map(lambda _: vmem, out_shape),
        scratch_shapes=list(scratch),
        compiler_params=pltpu.CompilerParams(vmem_limit_bytes=VMEM_LIMIT),
        cost_estimate=cost,
        name=name,
    )


def half_pick(block, odd, to_upper):
    moved = pltpu.roll(block, 64, 1)
    return jnp.where(odd, block if to_upper else moved, moved if to_upper else block)


def low_lanes(shape):
    return lax.broadcasted_iota(jnp.int32, shape, len(shape) - 1) % 128 < 64


def pack_body(nz, w_qkv, w_up, w_down, w_out, x, g, *refs):
    vectors, (pay, piece, head_w) = refs[:8], refs[8:11]
    qkv, ups, small, sems = refs[11:15]
    lists = refs[15:]
    me = lax.axis_index("ctx").astype(jnp.int32)
    odd = (me % 2) == 1
    rows = w_qkv.shape[0]
    span = FF // nz

    def lanes(start):
        return pl.ds(pl.multiple_of(start + (me // 2) * 128, 128), 128)

    down = pl.ds(pl.multiple_of(me * 64, 64), 64)
    pairs = [(w_qkv.at[:, lanes(i * D)], qkv.at[i]) for i in range(3)]
    pairs += [(w_up.at[:, lanes(z * span)], ups.at[z]) for z in range(nz)]
    pairs += [(w_down.at[down, 0:256], pay.at[0:64, 512:768]), (w_down.at[down, 256:512], pay.at[64:128, 512:768])]
    pairs += [(x.at[0], piece.at[0:TOK, :]), (g.at[0], piece.at[TOK : 2 * TOK, :])]
    pairs += [(w_out.at[pl.ds(pl.multiple_of((me % 2) * 64, 64), 64), :], head_w)]
    pairs += list(zip(vectors, lists))
    copies = [pltpu.make_async_copy(source, target, sems.at[at]) for at, (source, target) in enumerate(pairs)]
    for copy in copies:
        copy.start()
    for copy in copies:
        copy.wait()
    low = low_lanes((rows, 128))
    small[...] = jnp.zeros_like(small)
    at = 0
    for vector in lists:
        for r in range(vector.shape[0] // 128):
            small[at : at + 1, :] = vector[r * 128 : (r + 1) * 128].astype(F32).reshape(1, 128)
            at += 1
    few = small[...]
    spare = jnp.concatenate([pltpu.roll(few, 64, 1), few, jnp.zeros((rows - 32, 128), F32)], axis=0)
    q = half_pick(qkv[0].astype(F32), odd, False)
    k = half_pick(qkv[1].astype(F32), odd, True)
    v = half_pick(qkv[2].astype(F32), odd, False)
    pay[:, 0:128] = jnp.where(low, q, k).astype(BF16)
    pay[:, 128:256] = jnp.where(low, v, spare).astype(BF16)
    for z in range(0, nz, 2):
        even = half_pick(ups[z].astype(F32), odd, False)
        later = half_pick(ups[z + 1].astype(F32), odd, True)
        pay[:, 256 + z * 64 : 256 + z * 64 + 128] = jnp.where(low, even, later).astype(BF16)


def pack_call(nz, w_qkv, w_up, w_down, w_out, x, g, vectors):
    rows = D // nz
    here = pl.BlockSpec(memory_space=pl.ANY)
    return pl.pallas_call(
        functools.partial(pack_body, nz),
        out_shape=[shape((rows, 768), BF16), shape((2 * TOK, D), BF16), shape((HEAD_DIM, D), BF16)],
        in_specs=[here] * (6 + len(vectors)),
        out_specs=[pl.BlockSpec(memory_space=pltpu.VMEM)] * 3,
        scratch_shapes=[
            pltpu.VMEM((3, rows, 128), BF16),
            pltpu.VMEM((nz, rows, 128), BF16),
            pltpu.VMEM((16, 128), F32),
            pltpu.SemaphoreType.DMA((8 + nz + len(vectors),)),
        ]
        + [pltpu.VMEM(v.shape, BF16) for v in vectors],
        compiler_params=pltpu.CompilerParams(vmem_limit_bytes=WIDE_LIMIT),
        name="pack",
    )(w_qkv, w_up, w_down, w_out, x, g, *vectors)


def unpack_body(nz, place, *refs):
    pieces = refs[:nz]
    w_all, w_up, w_down, params, held = refs[nz:]
    me, zed = place[0], place[1]
    pair = me // 2
    odd = (me % 2) == 1
    for k in range(nz):
        z = zed ^ k
        tall = pl.ds(pl.multiple_of(z * 128, 128), 128)
        flat = pl.ds(pl.multiple_of(z * 64, 64), 64)
        w_all[tall, 0:128] = pieces[k][:, 0:128]
        third = pieces[k][:, 128:256].astype(F32)
        w_all[tall, 128:256] = jnp.where(low_lanes((128, 128)), third, 0.0).astype(BF16)
        held[z] = jnp.where(low_lanes((16, 128)), pltpu.roll(third[0:16], 64, 1), third[16:32])
        w_up[tall, :] = pieces[k][:, 256:512]
        w_down[flat, 0:256] = pieces[k][0:64, 512:768]
        w_down[flat, 256:512] = pieces[k][64:128, 512:768]
    params[...] = jnp.zeros_like(params)
    for z in range(nz):
        lanes = slice(z * 128, (z + 1) * 128)
        params[0:4, lanes] = held[z, 0:4, :]
        params[4:5, lanes] = held[z, 4:5, :] + held[z, 5:6, :]
    low = low_lanes((1, 128))

    def qkv_row(group):
        index = group * 4 + pair
        z = index // 3
        return held[z, pl.ds(6 + index - 3 * z, 1), :]

    q = half_pick(qkv_row(0), odd, False)
    k = half_pick(qkv_row(1), odd, True)
    v = half_pick(qkv_row(2), odd, False)
    params[5:6, 0:128] = jnp.where(low, q, k)
    params[5:6, 128:256] = jnp.where(low, v, 0.0)
    for z in range(0, nz, 2):
        even = half_pick(held[z, pl.ds(9 + pair, 1), :], odd, False)
        later = half_pick(held[z + 1, pl.ds(9 + pair, 1), :], odd, True)
        params[6:7, z * 64 : z * 64 + 128] = jnp.where(low, even, later)


def normalized(x):
    center = x - jnp.mean(x, axis=-1, keepdims=True)
    spread = jnp.mean(center * center, axis=-1, keepdims=True)
    inv = lax.rsqrt(spread + EPS)
    return center * inv, inv


def joined(pieces, first):
    if len(pieces) == 1:
        return pieces[0][first : first + TOK, :]
    return jnp.concatenate([piece[first : first + TOK, :] for piece in pieces], axis=0)


def fold(values):
    return jnp.sum(values.reshape(values.shape[0] // 8, 8, values.shape[1]), axis=0)


def ff_body(n, nz, fast, place, *refs):
    pieces = refs[:n]
    w_up, w_down, params = refs[n : n + 3]
    outs = refs[n + 3 :]
    n_pay = nz if fast else 2
    acc_o, acc_d, vec, norms, nhats = outs[:5]
    pays = outs[5 : 5 + n_pay]
    norm2s, hiddens, dpres, gs, grad_up, grad_down = outs[5 + n_pay :]
    width = w_up.shape[1]
    zed = place[1]
    gain, shift = params[0:1, :], params[1:2, :]
    gain2, shift2 = params[2:3, :], params[3:4, :]
    b_up = params[6:7, 0:width]
    g_gain = jnp.zeros((8, D), F32)
    g_shift = jnp.zeros((8, D), F32)
    g_sum = jnp.zeros((8, D), F32)
    g_bup = jnp.zeros((8, width), F32)
    for p in range(0, n, 4):
        rows = slice(p * TOK, (p + 4) * TOK)
        nhat, _ = normalized(joined(pieces[p : p + 4], 0).astype(F32))
        g = joined(pieces[p : p + 4], TOK)
        norms[rows, :] = (nhat * gain + shift).astype(BF16)
        nhats[rows, :] = nhat.astype(BF16)
        norm2 = (nhat * gain2 + shift2).astype(BF16)
        pre = mm_nn(norm2, w_up[...]) + b_up
        cdf = 0.5 * (1.0 + lax.erf(pre * 0.7071067811865476))
        hidden = (pre * cdf).astype(BF16)
        slope = cdf + pre * (0.3989422804014327 * jnp.exp(-0.5 * pre * pre))
        dpre = (mm_nt(g, w_down[...]) * slope).astype(BF16)
        dnorm = mm_nt(dpre, w_up[...])
        acc_o[rows, :] = mm_nn(hidden, w_down[...]).astype(BF16)
        acc_d[rows, :] = (dnorm * gain2).astype(BF16)
        g_gain += fold(dnorm * nhat)
        g_shift += fold(dnorm)
        g_sum += fold(g.astype(F32))
        g_bup += fold(dpre.astype(F32))
        norm2s[rows, :] = norm2
        hiddens[rows, :] = hidden
        dpres[rows, :] = dpre
        gs[rows, :] = g
    vec[...] = jnp.zeros_like(vec)
    for row, value in ((2, g_gain), (3, g_shift), (4, g_sum), (6, g_bup)):
        vec[row : row + 1, 0 : value.shape[1]] = jnp.sum(value, axis=0, keepdims=True)
    grad_up[...] = mm_tn(dpres[...], norm2s[...]).T.astype(BF16)
    grad_down[...] = mm_tn(hiddens[...], gs[...]).astype(BF16)
    if fast:
        for k, target in enumerate(pays):
            z = zed ^ k
            tall = pl.ds(pl.multiple_of(z * 128, 128), 128)
            flat = pl.ds(pl.multiple_of(z * 64, 64), 64)
            target[:, 0:256] = grad_up[tall, :]
            target[0:64, 256:512] = grad_down[flat, 0:256]
            target[64:128, 256:512] = grad_down[flat, 256:512]
    else:
        pays[0][...] = grad_up[...]
        pays[1][...] = grad_down[...]


def attn_body(n, place, order, *refs):
    seq = n * TOK
    qblk = min(512, seq)
    pieces = refs[:n]
    w_all, params, w_out, turn, norms = refs[n : n + 5]
    mixn, dqkvn = refs[n + 5 : n + 7]
    raw, qs, ks, vs, dms, mixs, dks, dvs, dqs, dqkvs = refs[n + 7 :]
    bias = params[5:6, 0:256]

    def sorted_rows(block):
        return pl.ds(pl.multiple_of(order[block] * HALF, HALF), HALF)

    for p in range(0, n, 2):
        rows = slice(p * TOK, (p + 2) * TOK)
        qkv = mm_nn(norms[rows, :], w_all[...]) + bias
        dmix = mm_nt(joined(pieces[p : p + 2], TOK), w_out[...]).astype(BF16)
        for h in range(2 * TOK // HALF):
            here = slice(h * HALF, (h + 1) * HALF)
            where = sorted_rows(p * (TOK // HALF) + h)
            raw[where, :] = qkv[here, :]
            dms[where, :] = dmix[here, :]

    lanes = lax.broadcasted_iota(jnp.int32, (qblk, 128), 1) % 64

    def both_heads(t):
        moved = pltpu.roll(t, 64, 1)
        low = low_lanes(t.shape)
        return jnp.where(low, t, moved), jnp.where(low, moved, t)

    def swapped(t):
        return jnp.where(lanes < ROT // 2, pltpu.roll(t, 128 - ROT // 2, 1), pltpu.roll(t, ROT // 2, 1))

    for i in range(seq // qblk):
        rows = slice(i * qblk, (i + 1) * qblk)
        qk = raw[rows, 0:128]
        cos_t, sin_t = both_heads(turn[rows, :])
        turned = (qk * cos_t + swapped(qk) * sin_t).astype(BF16)
        qs[rows, :] = turned[:, 0:64] * jnp.asarray(0.125, BF16)
        ks[rows, :] = turned[:, 64:128]
        vs[rows, :] = raw[rows, 128:192].astype(BF16)

    q_at = lax.broadcasted_iota(jnp.int32, (qblk, qblk), 0)
    k_at = lax.broadcasted_iota(jnp.int32, (qblk, qblk), 1)
    causal = q_at >= k_at
    dks[...] = jnp.zeros_like(dks)
    dvs[...] = jnp.zeros_like(dvs)
    for i in range(seq // qblk):
        rows = slice(i * qblk, (i + 1) * qblk)
        span = (i + 1) * qblk
        q = qs[rows, :]
        keys = ks[0:span, :]
        values = vs[0:span, :]
        s = jnp.where(causal, mm_nt(q, ks[rows, :]), -1e30)
        if i:
            s = jnp.concatenate([mm_nt(q, ks[0 : i * qblk, :]), s], axis=1)
        top = jnp.max(s, axis=1, keepdims=True)
        e = jnp.exp(s - top)
        inv = 1.0 / jnp.sum(e, axis=1, keepdims=True)
        e_b = e.astype(BF16)
        mix = mm_nn(e_b, values) * inv
        mixs[rows, :] = mix.astype(BF16)
        dmix = (dms[rows, :].astype(F32) * inv).astype(BF16)
        delta = jnp.sum(dmix.astype(F32) * mix, axis=1, keepdims=True)
        ds = (e * (mm_nt(dmix, values) - delta)).astype(BF16)
        dqs[rows, 0:64] = mm_nn(ds, keys) * 0.125
        dks[:, 0:span] += mm_tn(q, ds)
        dvs[:, 0:span] += mm_tn(dmix, e_b)
    dqs[:, 64:128] = dks[...].T
    dqkvs[:, 128:192] = dvs[...].T.astype(BF16)
    dqkvs[:, 192:256] = jnp.zeros((seq, 64), BF16)
    for i in range(seq // qblk):
        rows = slice(i * qblk, (i + 1) * qblk)
        dqk = dqs[rows, :]
        cos_t, sin_t = both_heads(turn[rows, :])
        dqkvs[rows, 0:128] = (dqk * cos_t - swapped(dqk) * sin_t).astype(BF16)

    scale = None
    if n > HEADS:
        scale = jnp.where(place[0] % (n // HEADS) == 0, 1.0, 0.0).astype(BF16)
    for b in range(seq // HALF):
        here = slice(b * HALF, (b + 1) * HALF)
        where = sorted_rows(b)
        mix, dqkv = mixs[where, :], dqkvs[where, :]
        if scale is not None:
            mix, dqkv = mix * scale, dqkv * scale
        mixn[here, :] = mix
        dqkvn[here, :] = dqkv


def ends_body(n, nz, fast, place, *refs):
    pieces = refs[:n]
    mixn, dqkvn, norms, nhats, acc_o, acc_d, vec_in, w_all, w_out, params = refs[n : n + 10]
    at = n + 10
    if fast:
        ff_one, ff_two, ff_came = refs[at : at + 3]
        at += 3
    keep_pay, send_pay, g_out = refs[at : at + 3]
    n_pay = 4 if fast else 2
    pays = refs[at + 3 : at + 3 + n_pay]
    spare, gs, grad_w, vec = refs[at + 3 + n_pay :]
    zed = place[1]
    gain = params[0:1, :]
    g_gain = jnp.zeros((8, D), F32)
    g_shift = jnp.zeros((8, D), F32)
    g_bias = jnp.zeros((8, 256), F32)
    for p in range(0, n, 2):
        rows = slice(p * TOK, (p + 2) * TOK)
        gs[rows, :] = joined(pieces[p : p + 2], TOK)
        dqkv = dqkvn[rows, :]
        dnorm = mm_nt(dqkv, w_all[...])
        g_gain += fold(dnorm * nhats[rows, :].astype(F32))
        g_shift += fold(dnorm)
        g_bias += fold(dqkv.astype(F32))
        part_o = (mm_nn(mixn[rows, :], w_out[...]) + acc_o[rows, :].astype(F32)).astype(BF16)
        part_d = (dnorm * gain + acc_d[rows, :].astype(F32)).astype(BF16)
        for q in range(2):
            target = send_pay if (p + q) % 2 else keep_pay
            here = slice(q * TOK, (q + 1) * TOK)
            target[(p + q) // 2, :, 0:512] = part_o[here, :]
            target[(p + q) // 2, :, 512:1024] = part_d[here, :]
    vec[...] = vec_in[...]
    for row, value in ((0, g_gain), (1, g_shift), (5, g_bias)):
        vec[row : row + 1, 0 : value.shape[1]] = jnp.sum(value, axis=0, keepdims=True)
    g_out[...] = mm_tn(mixn[...], gs[...]).astype(BF16)
    grad_w[...] = mm_tn(dqkvn[...], norms[...]).T
    if fast:
        spare[...] = jnp.zeros_like(spare)
        for j in range(8):
            lanes_j = vec[:, (j // 2) * 128 : (j // 2) * 128 + 128]
            spare[8 * j : 8 * j + 8, :] = lanes_j if j % 2 else pltpu.roll(lanes_j, 64, 1)
        low = low_lanes((128, 128))
        own, near, two, ff_sum = pays
        near[:, 512:1024] = ff_one[...]
        for k, target in ((0, own), (1, near.at[:, 0:256]), (2, two), (3, near.at[:, 256:512])):
            tall = pl.ds(pl.multiple_of((zed ^ k) * 128, 128), 128)
            target[:, 0:128] = grad_w[tall, 0:128].astype(BF16)
            target[:, 128:256] = jnp.where(low, grad_w[tall, 128:256], spare[...]).astype(BF16)
        ff_sum[0:128, :] = (ff_two[...].astype(F32) + ff_came[...].astype(F32)).astype(BF16)
        ff_sum[128:192, :] = g_out[...]
    else:
        pays[0][...] = grad_w[...].astype(BF16)
        pays[1][...] = vec[...]


def close_body(fast, place, x_ref, g_ref, params, *refs):
    if fast:
        parts, (value, out, grad, copy) = refs[:5], refs[5:]
        copy[...] = value[...]
    else:
        parts, out, grad = refs[:-2], refs[-2], refs[-1]
    x = x_ref[...].astype(F32)
    nhat, inv = normalized(x)
    if fast:
        own, came_a, came_b, last_a, last_b = parts
        total_o = own[:, 0:D].astype(F32) + came_a[0].astype(F32) + last_a[...].astype(F32)
        dn = own[:, D : 2 * D].astype(F32) + came_b[0].astype(F32) + last_b[...].astype(F32)
    else:
        total = parts[0][...].astype(F32)
        for part in parts[1:]:
            total = total + part[...].astype(F32)
        total_o, dn = total[:, 0:D], total[:, D : 2 * D]
    out[...] = (x + total_o + params[4:5, :]).astype(BF16)
    lead = jnp.mean(dn, axis=-1, keepdims=True)
    along = jnp.mean(dn * nhat, axis=-1, keepdims=True)
    grad[...] = g_ref[...].astype(F32) + inv * (dn - lead - nhat * along)


def chip_body(keep, came, *outs):
    for k, out in enumerate(outs):
        out[...] = (keep[k].astype(F32) + came[k].astype(F32)).astype(BF16)


def chip_fast_body(n_later, keep, came, *refs):
    later, (first_a, first_b, own, kept_a, kept_b, *held) = refs[:n_later], refs[n_later:]
    for value, copy in zip(later, held):
        copy[...] = value[...]

    def both(k, lanes):
        return (keep[k, :, lanes].astype(F32) + came[k, :, lanes].astype(F32)).astype(BF16)

    left, right = slice(0, D), slice(D, 2 * D)
    own[:, left] = both(0, left)
    own[:, right] = both(0, right)
    first_a[0] = both(1, left)
    first_a[1] = both(3, left)
    first_b[0] = both(2, right)
    first_b[1] = both(3, right)
    kept_a[...] = both(2, left)
    kept_b[...] = both(1, right)


def cross_body(n_later, kept_a, kept_b, came_a, came_b, *refs):
    later, (second_a, second_b, *held) = refs[:n_later], refs[n_later:]
    for value, copy in zip(later, held):
        copy[...] = value[...]
    second_a[...] = (kept_a[...].astype(F32) + came_a[1].astype(F32)).astype(BF16)
    second_b[...] = (kept_b[...].astype(F32) + came_b[1].astype(F32)).astype(BF16)


def gate_body(value, *refs):
    out = refs[-1]
    out[...] = value[...]


def relay_body(two, came, out):
    out[...] = (two[...].astype(F32) + came[:, 256:512].astype(F32)).astype(BF16)


def out_body(mine, came, out):
    out[...] = (mine[...].astype(F32) + came[128:192, :].astype(F32)).astype(BF16)


def share_body(ff_own, ff_far, own, near, far, out_half, out_far, *refs):
    out = refs[-1]
    out[:, 0:512] = (ff_own[...].astype(F32) + near[:, 512:1024].astype(F32) + ff_far[0:128, :].astype(F32)).astype(BF16)
    out[:, 512:768] = (own[...].astype(F32) + near[:, 0:256].astype(F32) + far[...].astype(F32)).astype(BF16)
    g_out = (out_half[...].astype(F32) + out_far[...].astype(F32)).astype(BF16)
    out[0:64, 768:1024] = g_out[:, 0:256]
    out[64:128, 768:1024] = g_out[:, 256:512]


def finish_body(n, nz, place, *refs):
    alls = refs[:n]
    (ln1g, ln1b, gqkv, bqkv, gout, bout, ln2g, ln2b, gup, bup, gdown, bdown) = refs[n : n + 12]
    held_u, held_a, held_v, flat = refs[n + 12 :]
    me, zed = place[0], place[1]
    span = FF // nz
    total = jnp.zeros((8, D), F32)
    wide = low_lanes((8, 128))
    for k in range(n):
        who = me ^ k
        held_a[who] = alls[k][:, 512:768].astype(F32)
        held_u[who] = alls[k][:, 0:256].astype(F32)
        rows = pl.ds(pl.multiple_of(who * 64, 64), 64)
        gdown[rows, 0:256] = alls[k][0:64, 256:512].astype(F32)
        gdown[rows, 256:512] = alls[k][64:128, 256:512].astype(F32)
        spare = alls[k][0:64, 640:768].astype(F32)
        small = []
        for j in range(0, 8, 2):
            small.append(jnp.where(wide, pltpu.roll(spare[8 * j : 8 * j + 8], 64, 1), spare[8 * j + 8 : 8 * j + 16]))
        small = jnp.concatenate(small, axis=1)
        held_v[who] = small
        total = total + small
    for h in range(0, n, 2):
        even, later = held_a[h], held_a[h + 1]
        low = low_lanes((128, 128))
        at = h * 64
        gqkv[:, at : at + 128] = jnp.where(low, even[:, 0:128], pltpu.roll(later[:, 0:128], 64, 1))
        gqkv[:, D + at : D + at + 128] = jnp.where(low, pltpu.roll(even[:, 0:128], 64, 1), later[:, 0:128])
        gqkv[:, 2 * D + at : 2 * D + at + 128] = jnp.where(low, even[:, 128:256], pltpu.roll(later[:, 128:256], 64, 1))
        for z in range(0, nz, 2):
            lanes = slice(z * 64, z * 64 + 128)
            e, l = held_u[h][:, lanes], held_u[h + 1][:, lanes]
            gup[:, z * span + at : z * span + at + 128] = jnp.where(low, e, pltpu.roll(l, 64, 1))
            gup[:, (z + 1) * span + at : (z + 1) * span + at + 128] = jnp.where(low, pltpu.roll(e, 64, 1), l)
        low = low_lanes((1, 128))
        e, l = held_v[h], held_v[h + 1]
        flat[h // 2 : h // 2 + 1, :] = jnp.where(low, e[5:6, 0:128], pltpu.roll(l[5:6, 0:128], 64, 1))
        flat[4 + h // 2 : 5 + h // 2, :] = jnp.where(low, pltpu.roll(e[5:6, 0:128], 64, 1), l[5:6, 0:128])
        flat[8 + h // 2 : 9 + h // 2, :] = jnp.where(low, e[5:6, 128:256], pltpu.roll(l[5:6, 128:256], 64, 1))
        lane = pl.ds(pl.multiple_of((zed // 2) * 128, 128), 128)
        odd = (zed % 2) == 1
        e = half_pick(held_v[h, 6:7, lane], odd, False)
        l = half_pick(held_v[h + 1, 6:7, lane], odd, True)
        bup[at : at + 128] = jnp.where(low, e, l).reshape(128)
    for k in range(n):
        held_a[me ^ k] = alls[k][:, 768:1024].astype(F32)
    for p in range(2):
        rows = held_a[2 * zed + p]
        gout[64 * p : 64 * p + 64, 0:256] = rows[0:64]
        gout[64 * p : 64 * p + 64, 256:512] = rows[64:128]
    flat[12:20, :] = jnp.zeros((8, 128), F32)
    for r in range(3):
        bqkv[r * 128 : (r + 1) * 128] = flat[pl.ds(zed * 3 + r, 1), :].reshape(128)
    held_v[0] = total
    lane = pl.ds(pl.multiple_of(zed * 128, 128), 128)
    ln1g[...] = held_v[0, 0:1, lane].reshape(128)
    ln1b[...] = held_v[0, 1:2, lane].reshape(128)
    ln2g[...] = held_v[0, 2:3, lane].reshape(128)
    ln2b[...] = held_v[0, 3:4, lane].reshape(128)
    held_v[1] = total * (1.0 / n)
    bout[...] = held_v[1, 4:5, lane].reshape(128)
    bdown[...] = held_v[1, 4:5, lane].reshape(128)


def xor_pairs(size, k):
    return [(i, i ^ k) for i in range(size)]


def gather_ctx(value, n, beside=None):
    got = {0: value}
    for k in range(2, n, 2):
        got[k] = lax.ppermute(value, "ctx", xor_pairs(n, k))
    for k in range(0, n, 2):
        source = beside if k == 0 and beside is not None else got[k]
        got[k + 1] = lax.ppermute(source, "ctx", xor_pairs(n, 1))
    return [got[k] for k in range(n)]


def gather_fsdp(value, nz):
    return [value] + [lax.ppermute(value, "fsdp", xor_pairs(nz, k)) for k in range(1, nz)]


def relay_fsdp(value, nz):
    one, two = (lax.ppermute(value, "fsdp", xor_pairs(nz, k)) for k in (1, 2))
    return [value, one, two, lax.ppermute(two, "fsdp", xor_pairs(nz, 1))]


def rotary_tables(seq):
    pos = np.arange(seq, dtype=np.float32)
    inverse = (np.float32(10000.0) ** (-np.arange(ROT // 2, dtype=np.float32) * np.float32(2.0) / np.float32(ROT))).astype(np.float32)
    angles = (pos[:, None] * inverse[None, :]).astype(np.float32).astype(np.float64)
    cos_t = np.ones((seq, 64), np.float32)
    sin_t = np.zeros((seq, 64), np.float32)
    half = ROT // 2
    cos_t[:, 0:half] = np.cos(angles)
    cos_t[:, half:ROT] = np.cos(angles)
    sin_t[:, 0:half] = -np.sin(angles)
    sin_t[:, half:ROT] = np.sin(angles)
    return np.concatenate([cos_t, sin_t], axis=1)


def shape(dims, dtype=F32):
    return jax.ShapeDtypeStruct(dims, dtype)


def per_device(
    n,
    nz,
    inputs,
    block_order,
    ln1_gain,
    ln1_bias,
    w_qkv,
    b_qkv,
    w_attn_out,
    b_attn_out,
    ln2_gain,
    ln2_bias,
    w_up,
    b_up,
    w_down,
    b_down,
    cotangent,
):
    fast = n == HEADS and nz * 2 == HEADS
    seq = n * TOK
    width = FF // n
    me = lax.axis_index("ctx").astype(jnp.int32)
    zed = lax.axis_index("fsdp").astype(jnp.int32)
    place = jnp.stack([me, zed])
    x, g = inputs[0], cotangent[0]
    blocks = TOK // HALF
    chunk_at = (jnp.arange(n, dtype=jnp.int32) ^ me)[:, None] * blocks + jnp.arange(blocks, dtype=jnp.int32)[None, :]
    pick = chunk_at.reshape(-1)[:, None] == jnp.arange(n * blocks, dtype=jnp.int32)[None, :]
    order = jnp.sum(jnp.where(pick, block_order[None, :], 0), axis=1).astype(jnp.int32)
    turn = rotary_tables(seq)

    if fast:
        vectors = (ln1_gain, ln1_bias, ln2_gain, ln2_bias, b_attn_out, b_down, b_qkv, b_up)
        pack, piece, pack_w = pack_call(nz, w_qkv, w_up, w_down, w_attn_out, inputs, cotangent, vectors)
        pieces = gather_ctx(piece, n)
        far = relay_fsdp(pack, nz)
        given = vmem_call(
            functools.partial(unpack_body, nz),
            [shape((D, 256), BF16), shape((D, width), BF16), shape((width, D), BF16), shape((8, D))],
            scratch=[pltpu.VMEM((nz, 16, 128), F32)],
            n_smem=1,
            n_in=nz,
            cost=LONG,
            name="unpack",
        )(place, *far)
        pairs = []
        for c in range(n):
            for z in range(nz):
                pairs.append((c * nz + z, (2 * z + c % 2) * nz + c // 2))
        pack_w = vmem_call(gate_body, shape(pack_w.shape, BF16), n_in=2, name="gate_w")(pack_w, far[1])
        head_w = lax.ppermute(pack_w, ("ctx", "fsdp"), pairs)
    else:
        whole = [
            lax.all_gather(v, "fsdp", axis=0, tiled=True)
            for v in (ln1_gain, ln1_bias, ln2_gain, ln2_bias, b_attn_out, b_down, b_qkv, b_up)
        ]
        whole = [v.astype(F32) for v in whole]
        head = me // (n // HEADS)
        bq = lax.dynamic_index_in_dim(whole[6].reshape(3, HEADS, HEAD_DIM), head, 1, False).reshape(-1)
        bu = lax.dynamic_index_in_dim(whole[7].reshape(n, width), me, 0, False)
        params = jnp.stack(
            [whole[0], whole[1], whole[2], whole[3], whole[4] + whole[5]]
            + [jnp.pad(bq, (0, D - 3 * HEAD_DIM)), jnp.pad(bu, (0, D - width)), jnp.zeros((D,), F32)]
        )
        wq = lax.dynamic_index_in_dim(w_qkv.reshape(-1, 3, HEADS, HEAD_DIM), head, 2, False).reshape(-1, 3 * HEAD_DIM)
        given = [jnp.pad(lax.all_gather(wq, "fsdp", axis=0, tiled=True), ((0, 0), (0, 64)))]
        wu = lax.dynamic_slice_in_dim(w_up, me * width, width, 1)
        wd = lax.all_gather(w_down, "fsdp", axis=0, tiled=True)
        given += [lax.all_gather(wu, "fsdp", axis=0, tiled=True), lax.dynamic_slice_in_dim(wd, me * width, width, 0)]
        wo = lax.all_gather(w_attn_out, "fsdp", axis=0, tiled=True)
        given.append(params)
        pieces = gather_ctx(jnp.concatenate([x, g], axis=0), n)
        head_w = lax.dynamic_slice_in_dim(wo, head * HEAD_DIM, HEAD_DIM, 0)

    w_all, w_up_c, w_down_c, params = given
    whole_seq = shape((seq, D), BF16)
    half = (n // 2, TOK, 2 * D)
    rows = D // nz
    if fast:
        ff_pays = [shape((rows, 512), BF16)] * nz
        attn_pays = [shape((rows, 256), BF16), shape((rows, 1024), BF16), shape((rows, 256), BF16), shape((rows + HEAD_DIM, 512), BF16)]
    else:
        ff_pays = [shape((D, width), BF16), shape((width, D), BF16)]
        attn_pays = [shape((D, 256), BF16), shape((8, D))]
    ff_out = vmem_call(
        functools.partial(ff_body, n, nz, fast),
        [whole_seq, whole_seq, shape((8, D)), whole_seq, whole_seq] + ff_pays,
        scratch=[
            pltpu.VMEM((seq, D), BF16),
            pltpu.VMEM((seq, width), BF16),
            pltpu.VMEM((seq, width), BF16),
            pltpu.VMEM((seq, D), BF16),
            pltpu.VMEM((D, width), BF16),
            pltpu.VMEM((width, D), BF16),
        ],
        n_smem=1,
        n_in=n + 3,
        cost=pl.CostEstimate(flops=4_000_000_000, bytes_accessed=0, transcendentals=0),
        name="feed_forward",
    )(place, *pieces, w_up_c, w_down_c, params)
    acc_o, acc_d, vec_ff, norms, nhats = ff_out[:5]
    ff_pay = ff_out[5:]
    from_ff = []
    if fast:
        ff_pass = lax.ppermute(ff_pay[3], "fsdp", xor_pairs(nz, 1))
        from_ff = [ff_pay[1], ff_pay[2], ff_pass]
    mixn, dqkvn = vmem_call(
        functools.partial(attn_body, n),
        [shape((seq, 64), BF16), shape((seq, 256), BF16)],
        scratch=[
            pltpu.VMEM((seq, 256), F32),
            pltpu.VMEM((seq, 64), BF16),
            pltpu.VMEM((seq, 64), BF16),
            pltpu.VMEM((seq, 64), BF16),
            pltpu.VMEM((seq, 64), BF16),
            pltpu.VMEM((seq, 64), BF16),
            pltpu.VMEM((64, seq), F32),
            pltpu.VMEM((64, seq), F32),
            pltpu.VMEM((seq, 128), F32),
            pltpu.VMEM((seq, 256), BF16),
        ],
        n_smem=2,
        n_in=n + 5,
        cost=pl.CostEstimate(flops=6_000_000_000, bytes_accessed=0, transcendentals=0),
        name="attention",
    )(place, order, *pieces, w_all, params, head_w, turn, norms)
    ends_out = vmem_call(
        functools.partial(ends_body, n, nz, fast),
        [shape(half, BF16), shape(half, BF16), shape((HEAD_DIM, D), BF16)] + attn_pays,
        scratch=[
            pltpu.VMEM((128, 128), F32),
            pltpu.VMEM((seq, D), BF16),
            pltpu.VMEM((D, 256), F32),
            pltpu.VMEM((8, D), F32),
        ],
        n_smem=1,
        n_in=n + 10 + len(from_ff),
        cost=pl.CostEstimate(flops=3_000_000_000, bytes_accessed=0, transcendentals=0),
        name="ends",
    )(place, *pieces, mixn, dqkvn, norms, nhats, acc_o, acc_d, vec_ff, w_all, head_w, params, *from_ff)
    keep_pay, send_pay, g_out = ends_out[:3]
    attn_pay = ends_out[3:]

    came = lax.ppermute(send_pay, "ctx", xor_pairs(n, 1))
    if fast:
        chip_out = vmem_call(
            functools.partial(chip_fast_body, 0),
            [shape((2, TOK, D), BF16)] * 2 + [shape((TOK, 2 * D), BF16)] + [shape((TOK, D), BF16)] * 2 + [],
            n_in=2 + 0,
            cost=LONGER,
            name="chip_sum",
        )(keep_pay, came)
        first_a, first_b, own_sum, kept_a, kept_b = chip_out[:5]
        came_a = lax.ppermute(first_a, "ctx", xor_pairs(n, 2))
        came_b = lax.ppermute(first_b, "ctx", xor_pairs(n, 4))
        cross_out = vmem_call(
            functools.partial(cross_body, 0),
            [shape((TOK, D), BF16)] * 2 + [],
            n_in=4 + 0,
            cost=LONGER,
            name="cross",
        )(kept_a, kept_b, came_a, came_b)
        second_a, second_b = cross_out[:2]
        parts = [own_sum, came_a, came_b]
        parts += [lax.ppermute(second_a, "ctx", xor_pairs(n, 4)), lax.ppermute(second_b, "ctx", xor_pairs(n, 2))]
    else:
        chip_sum = vmem_call(chip_body, [shape((TOK, 2 * D), BF16)] * (n // 2), n_in=2, name="chip_sum")(keep_pay, came)
        parts = [chip_sum[0]] + [lax.ppermute(chip_sum[k // 2], "ctx", xor_pairs(n, k)) for k in range(2, n, 2)]
    if fast:
        ff_far = lax.ppermute(attn_pay[3], "fsdp", xor_pairs(nz, 2))
        out_half = vmem_call(out_body, shape((HEAD_DIM, D), BF16), n_in=2, cost=LONG, name="out_half")(g_out, ff_far)
        out_far = lax.ppermute(out_half, "fsdp", xor_pairs(nz, 1))
        attn_near = lax.ppermute(attn_pay[1], "fsdp", xor_pairs(nz, 1))
        attn_two = vmem_call(relay_body, shape((rows, 256), BF16), n_in=2, cost=LONG, name="relay")(attn_pay[2], attn_near)
        attn_far = lax.ppermute(attn_two, "fsdp", xor_pairs(nz, 2))
        share = vmem_call(share_body, shape((rows, 1024), BF16), n_in=7 + 2, name="share")(
            ff_pay[0], ff_far, attn_pay[0], attn_near, attn_far, out_half, out_far, parts[3], parts[4]
        )
        through = [share]
    else:
        through = []
    closed = vmem_call(
        functools.partial(close_body, fast),
        [shape((TOK, D), BF16), shape((TOK, D))] + [shape(v.shape, BF16) for v in through],
        n_smem=1,
        n_in=3 + len(parts) + len(through),
        name="close",
    )(place, x, g, params, *parts, *through)

    output, grad_inputs = closed[:2]
    if fast:
        alls = gather_ctx(share, n, closed[2])
        dz = D // nz
        outs = vmem_call(
            functools.partial(finish_body, n, nz),
            [
                shape((dz,)),
                shape((dz,)),
                shape((dz, 3 * D)),
                shape((3 * dz,)),
                shape((dz, D)),
                shape((dz,)),
                shape((dz,)),
                shape((dz,)),
                shape((dz, FF)),
                shape((FF // nz,)),
                shape((FF // nz, D)),
                shape((dz,)),
            ],
            scratch=[
                pltpu.VMEM((n, 128, 256), F32),
                pltpu.VMEM((n, 128, 256), F32),
                pltpu.VMEM((n, 8, D), F32),
                pltpu.VMEM((24, 128), F32),
            ],
            n_smem=1,
            n_in=n,
            name="finish",
        )(place, *alls)
    else:
        everyone = ("ctx", "fsdp")
        head = me // (n // HEADS)
        g_up, g_down = ff_pay
        g_qkv, vec = attn_pay

        def own(full, axis=0):
            size = full.shape[axis] // nz
            return lax.dynamic_slice_in_dim(full, zed * size, size, axis)

        def spread(part, dims, index, axis):
            full = jnp.zeros(dims, part.dtype)
            return lax.psum(lax.dynamic_update_index_in_dim(full, part, index, axis), everyone).astype(F32)

        qkv_full = spread(g_qkv[:, 0:192].reshape(D, 3, HEAD_DIM), (D, 3, HEADS, HEAD_DIM), head, 2).reshape(D, 3 * D)
        out_full = spread(g_out, (HEADS, HEAD_DIM, D), head, 0).reshape(D, D)
        up_full = spread(g_up, (D, n, width), me, 1).reshape(D, FF)
        down_full = spread(g_down, (n, width, D), me, 0).reshape(FF, D)
        bq_full = spread(vec[5, 0:192].reshape(3, HEAD_DIM), (3, HEADS, HEAD_DIM), head, 1).reshape(3 * D)
        bu_full = spread(vec[6, 0:width], (n, width), me, 0).reshape(FF)
        flat = lax.psum(vec, everyone)
        b_full = flat[4] * (1.0 / n)
        outs = [own(v) for v in (flat[0], flat[1], qkv_full, bq_full, out_full, b_full)]
        outs += [own(v) for v in (flat[2], flat[3], up_full, bu_full, down_full, b_full)]
    return (output[None], grad_inputs[None], *outs)


def solution(mesh):
    rows, flat, tokens = P("fsdp", None), P("fsdp"), P("fsdp", "ctx", None)
    weights = (flat, flat, rows, flat, rows, flat, flat, flat, rows, flat, rows, flat)
    return jax.shard_map(
        functools.partial(per_device, mesh.shape["ctx"], mesh.shape["fsdp"]),
        mesh=mesh,
        in_specs=(tokens, P(), *weights, tokens),
        out_specs=(tokens, tokens, *weights),
        check_vma=False,
    )
```

```python
import functools

import jax
import jax.numpy as jnp
import numpy as np
from jax import lax
from jax.experimental import pallas as pl
from jax.experimental.pallas import tpu as pltpu
from jax.sharding import PartitionSpec as P

HEADS = 8
HEAD_DIM = 64
D = 512
FF = 2048
ROT = 16
HALF = 64
TOK = 128
EPS = 1e-05
F32 = jnp.float32
BF16 = jnp.bfloat16
VMEM_LIMIT = 32 * 1024 * 1024
WIDE_LIMIT = 60 * 1024 * 1024
LONGER = pl.CostEstimate(flops=30_000_000_000, bytes_accessed=0, transcendentals=0)
LONG = pl.CostEstimate(flops=12_000_000_000, bytes_accessed=0, transcendentals=0)


def mm(left, right, dims):
    return lax.dot_general(left, right, (dims, ((), ())), preferred_element_type=F32)


def mm_nn(left, right):
    return mm(left, right, ((1,), (0,)))


def mm_nt(left, right):
    return mm(left, right, ((1,), (1,)))


def mm_tn(left, right):
    return mm(left, right, ((0,), (0,)))


def vmem_call(body, out_shape, scratch=(), n_smem=0, n_in=0, n_any=0, cost=None, name=None):
    smem = pl.BlockSpec(memory_space=pltpu.SMEM)
    vmem = pl.BlockSpec(memory_space=pltpu.VMEM)
    return pl.pallas_call(
        body,
        out_shape=out_shape,
        in_specs=[smem] * n_smem + [vmem] * n_in + [pl.BlockSpec(memory_space=pl.ANY)] * n_any,
        out_specs=jax.tree.map(lambda _: vmem, out_shape),
        scratch_shapes=list(scratch),
        compiler_params=pltpu.CompilerParams(vmem_limit_bytes=VMEM_LIMIT),
        cost_estimate=cost,
        name=name,
    )


def half_pick(block, odd, to_upper):
    moved = pltpu.roll(block, 64, 1)
    return jnp.where(odd, block if to_upper else moved, moved if to_upper else block)


def low_lanes(shape):
    return lax.broadcasted_iota(jnp.int32, shape, len(shape) - 1) % 128 < 64


def pack_body(nz, w_qkv, w_up, w_down, w_out, x, g, *refs):
    vectors, (pay, piece, head_w) = refs[:8], refs[8:11]
    qkv, ups, small, sems = refs[11:15]
    lists = refs[15:]
    me = lax.axis_index("ctx").astype(jnp.int32)
    odd = (me % 2) == 1
    rows = w_qkv.shape[0]
    span = FF // nz

    def lanes(start):
        return pl.ds(pl.multiple_of(start + (me // 2) * 128, 128), 128)

    down = pl.ds(pl.multiple_of(me * 64, 64), 64)
    pairs = [(w_qkv.at[:, lanes(i * D)], qkv.at[i]) for i in range(3)]
    pairs += [(w_up.at[:, lanes(z * span)], ups.at[z]) for z in range(nz)]
    pairs += [(w_down.at[down, 0:256], pay.at[0:64, 512:768]), (w_down.at[down, 256:512], pay.at[64:128, 512:768])]
    pairs += [(x.at[0], piece.at[0:TOK, :]), (g.at[0], piece.at[TOK : 2 * TOK, :])]
    pairs += [(w_out.at[pl.ds(pl.multiple_of((me % 2) * 64, 64), 64), :], head_w)]
    pairs += list(zip(vectors, lists))
    copies = [pltpu.make_async_copy(source, target, sems.at[at]) for at, (source, target) in enumerate(pairs)]
    for copy in copies:
        copy.start()
    for copy in copies:
        copy.wait()
    low = low_lanes((rows, 128))
    small[...] = jnp.zeros_like(small)
    at = 0
    for vector in lists:
        for r in range(vector.shape[0] // 128):
            small[at : at + 1, :] = vector[r * 128 : (r + 1) * 128].astype(F32).reshape(1, 128)
            at += 1
    few = small[...]
    spare = jnp.concatenate([pltpu.roll(few, 64, 1), few, jnp.zeros((rows - 32, 128), F32)], axis=0)
    q = half_pick(qkv[0].astype(F32), odd, False)
    k = half_pick(qkv[1].astype(F32), odd, True)
    v = half_pick(qkv[2].astype(F32), odd, False)
    pay[:, 0:128] = jnp.where(low, q, k).astype(BF16)
    pay[:, 128:256] = jnp.where(low, v, spare).astype(BF16)
    for z in range(0, nz, 2):
        even = half_pick(ups[z].astype(F32), odd, False)
        later = half_pick(ups[z + 1].astype(F32), odd, True)
        pay[:, 256 + z * 64 : 256 + z * 64 + 128] = jnp.where(low, even, later).astype(BF16)


def pack_call(nz, w_qkv, w_up, w_down, w_out, x, g, vectors):
    rows = D // nz
    here = pl.BlockSpec(memory_space=pl.ANY)
    return pl.pallas_call(
        functools.partial(pack_body, nz),
        out_shape=[shape((rows, 768), BF16), shape((2 * TOK, D), BF16), shape((HEAD_DIM, D), BF16)],
        in_specs=[here] * (6 + len(vectors)),
        out_specs=[pl.BlockSpec(memory_space=pltpu.VMEM)] * 3,
        scratch_shapes=[
            pltpu.VMEM((3, rows, 128), BF16),
            pltpu.VMEM((nz, rows, 128), BF16),
            pltpu.VMEM((16, 128), F32),
            pltpu.SemaphoreType.DMA((8 + nz + len(vectors),)),
        ]
        + [pltpu.VMEM(v.shape, BF16) for v in vectors],
        compiler_params=pltpu.CompilerParams(vmem_limit_bytes=WIDE_LIMIT),
        name="pack",
    )(w_qkv, w_up, w_down, w_out, x, g, *vectors)


def unpack_body(nz, place, *refs):
    pieces = refs[:nz]
    w_all, w_up, w_down, params, held = refs[nz:]
    me, zed = place[0], place[1]
    pair = me // 2
    odd = (me % 2) == 1
    for k in range(nz):
        z = zed ^ k
        tall = pl.ds(pl.multiple_of(z * 128, 128), 128)
        flat = pl.ds(pl.multiple_of(z * 64, 64), 64)
        w_all[tall, 0:128] = pieces[k][:, 0:128]
        third = pieces[k][:, 128:256].astype(F32)
        w_all[tall, 128:256] = jnp.where(low_lanes((128, 128)), third, 0.0).astype(BF16)
        held[z] = jnp.where(low_lanes((16, 128)), pltpu.roll(third[0:16], 64, 1), third[16:32])
        w_up[tall, :] = pieces[k][:, 256:512]
        w_down[flat, 0:256] = pieces[k][0:64, 512:768]
        w_down[flat, 256:512] = pieces[k][64:128, 512:768]
    params[...] = jnp.zeros_like(params)
    for z in range(nz):
        lanes = slice(z * 128, (z + 1) * 128)
        params[0:4, lanes] = held[z, 0:4, :]
        params[4:5, lanes] = held[z, 4:5, :] + held[z, 5:6, :]
    low = low_lanes((1, 128))

    def qkv_row(group):
        index = group * 4 + pair
        z = index // 3
        return held[z, pl.ds(6 + index - 3 * z, 1), :]

    q = half_pick(qkv_row(0), odd, False)
    k = half_pick(qkv_row(1), odd, True)
    v = half_pick(qkv_row(2), odd, False)
    params[5:6, 0:128] = jnp.where(low, q, k)
    params[5:6, 128:256] = jnp.where(low, v, 0.0)
    for z in range(0, nz, 2):
        even = half_pick(held[z, pl.ds(9 + pair, 1), :], odd, False)
        later = half_pick(held[z + 1, pl.ds(9 + pair, 1), :], odd, True)
        params[6:7, z * 64 : z * 64 + 128] = jnp.where(low, even, later)


def normalized(x):
    center = x - jnp.mean(x, axis=-1, keepdims=True)
    spread = jnp.mean(center * center, axis=-1, keepdims=True)
    inv = lax.rsqrt(spread + EPS)
    return center * inv, inv


def joined(pieces, first):
    if len(pieces) == 1:
        return pieces[0][first : first + TOK, :]
    return jnp.concatenate([piece[first : first + TOK, :] for piece in pieces], axis=0)


def fold(values):
    return jnp.sum(values.reshape(values.shape[0] // 8, 8, values.shape[1]), axis=0)


def ff_body(n, nz, fast, place, *refs):
    pieces = refs[:n]
    w_up, w_down, params = refs[n : n + 3]
    outs = refs[n + 3 :]
    n_pay = nz if fast else 2
    acc_o, acc_d, vec, norms, nhats = outs[:5]
    pays = outs[5 : 5 + n_pay]
    norm2s, hiddens, dpres, gs, grad_up, grad_down = outs[5 + n_pay :]
    width = w_up.shape[1]
    zed = place[1]
    gain, shift = params[0:1, :], params[1:2, :]
    gain2, shift2 = params[2:3, :], params[3:4, :]
    b_up = params[6:7, 0:width]
    g_gain = jnp.zeros((8, D), F32)
    g_shift = jnp.zeros((8, D), F32)
    g_sum = jnp.zeros((8, D), F32)
    g_bup = jnp.zeros((8, width), F32)
    for p in range(0, n, 4):
        rows = slice(p * TOK, (p + 4) * TOK)
        nhat, _ = normalized(joined(pieces[p : p + 4], 0).astype(F32))
        g = joined(pieces[p : p + 4], TOK)
        norms[rows, :] = (nhat * gain + shift).astype(BF16)
        nhats[rows, :] = nhat.astype(BF16)
        norm2 = (nhat * gain2 + shift2).astype(BF16)
        pre = mm_nn(norm2, w_up[...]) + b_up
        cdf = 0.5 * (1.0 + lax.erf(pre * 0.7071067811865476))
        hidden = (pre * cdf).astype(BF16)
        slope = cdf + pre * (0.3989422804014327 * jnp.exp(-0.5 * pre * pre))
        dpre = (mm_nt(g, w_down[...]) * slope).astype(BF16)
        dnorm = mm_nt(dpre, w_up[...])
        acc_o[rows, :] = mm_nn(hidden, w_down[...]).astype(BF16)
        acc_d[rows, :] = (dnorm * gain2).astype(BF16)
        g_gain += fold(dnorm * nhat)
        g_shift += fold(dnorm)
        g_sum += fold(g.astype(F32))
        g_bup += fold(dpre.astype(F32))
        norm2s[rows, :] = norm2
        hiddens[rows, :] = hidden
        dpres[rows, :] = dpre
        gs[rows, :] = g
    vec[...] = jnp.zeros_like(vec)
    for row, value in ((2, g_gain), (3, g_shift), (4, g_sum), (6, g_bup)):
        vec[row : row + 1, 0 : value.shape[1]] = jnp.sum(value, axis=0, keepdims=True)
    grad_up[...] = mm_tn(dpres[...], norm2s[...]).T.astype(BF16)
    grad_down[...] = mm_tn(hiddens[...], gs[...]).astype(BF16)
    if fast:
        for k, target in enumerate(pays):
            z = zed ^ k
            tall = pl.ds(pl.multiple_of(z * 128, 128), 128)
            flat = pl.ds(pl.multiple_of(z * 64, 64), 64)
            target[:, 0:256] = grad_up[tall, :]
            target[0:64, 256:512] = grad_down[flat, 0:256]
            target[64:128, 256:512] = grad_down[flat, 256:512]
    else:
        pays[0][...] = grad_up[...]
        pays[1][...] = grad_down[...]


def attn_body(n, place, order, *refs):
    seq = n * TOK
    qblk = min(512, seq)
    pieces = refs[:n]
    w_all, params, w_out, turn, norms = refs[n : n + 5]
    mixn, dqkvn = refs[n + 5 : n + 7]
    raw, qs, ks, vs, dms, mixs, dks, dvs, dqs, dqkvs = refs[n + 7 :]
    bias = params[5:6, 0:256]

    def sorted_rows(block):
        return pl.ds(pl.multiple_of(order[block] * HALF, HALF), HALF)

    for p in range(0, n, 2):
        rows = slice(p * TOK, (p + 2) * TOK)
        qkv = mm_nn(norms[rows, :], w_all[...]) + bias
        dmix = mm_nt(joined(pieces[p : p + 2], TOK), w_out[...]).astype(BF16)
        for h in range(2 * TOK // HALF):
            here = slice(h * HALF, (h + 1) * HALF)
            where = sorted_rows(p * (TOK // HALF) + h)
            raw[where, :] = qkv[here, :]
            dms[where, :] = dmix[here, :]

    lanes = lax.broadcasted_iota(jnp.int32, (qblk, 128), 1) % 64

    def both_heads(t):
        moved = pltpu.roll(t, 64, 1)
        low = low_lanes(t.shape)
        return jnp.where(low, t, moved), jnp.where(low, moved, t)

    def swapped(t):
        return jnp.where(lanes < ROT // 2, pltpu.roll(t, 128 - ROT // 2, 1), pltpu.roll(t, ROT // 2, 1))

    for i in range(seq // qblk):
        rows = slice(i * qblk, (i + 1) * qblk)
        qk = raw[rows, 0:128]
        cos_t, sin_t = both_heads(turn[rows, :])
        turned = (qk * cos_t + swapped(qk) * sin_t).astype(BF16)
        qs[rows, :] = turned[:, 0:64] * jnp.asarray(0.125, BF16)
        ks[rows, :] = turned[:, 64:128]
        vs[rows, :] = raw[rows, 128:192].astype(BF16)

    q_at = lax.broadcasted_iota(jnp.int32, (qblk, qblk), 0)
    k_at = lax.broadcasted_iota(jnp.int32, (qblk, qblk), 1)
    causal = q_at >= k_at
    dks[...] = jnp.zeros_like(dks)
    dvs[...] = jnp.zeros_like(dvs)
    for i in range(seq // qblk):
        rows = slice(i * qblk, (i + 1) * qblk)
        span = (i + 1) * qblk
        q = qs[rows, :]
        keys = ks[0:span, :]
        values = vs[0:span, :]
        s = jnp.where(causal, mm_nt(q, ks[rows, :]), -1e30)
        if i:
            s = jnp.concatenate([mm_nt(q, ks[0 : i * qblk, :]), s], axis=1)
        top = jnp.max(s, axis=1, keepdims=True)
        e = jnp.exp(s - top)
        inv = 1.0 / jnp.sum(e, axis=1, keepdims=True)
        e_b = e.astype(BF16)
        mix = mm_nn(e_b, values) * inv
        mixs[rows, :] = mix.astype(BF16)
        dmix = (dms[rows, :].astype(F32) * inv).astype(BF16)
        delta = jnp.sum(dmix.astype(F32) * mix, axis=1, keepdims=True)
        ds = (e * (mm_nt(dmix, values) - delta)).astype(BF16)
        dqs[rows, 0:64] = mm_nn(ds, keys) * 0.125
        dks[:, 0:span] += mm_tn(q, ds)
        dvs[:, 0:span] += mm_tn(dmix, e_b)
    dqs[:, 64:128] = dks[...].T
    dqkvs[:, 128:192] = dvs[...].T.astype(BF16)
    dqkvs[:, 192:256] = jnp.zeros((seq, 64), BF16)
    for i in range(seq // qblk):
        rows = slice(i * qblk, (i + 1) * qblk)
        dqk = dqs[rows, :]
        cos_t, sin_t = both_heads(turn[rows, :])
        dqkvs[rows, 0:128] = (dqk * cos_t - swapped(dqk) * sin_t).astype(BF16)

    scale = None
    if n > HEADS:
        scale = jnp.where(place[0] % (n // HEADS) == 0, 1.0, 0.0).astype(BF16)
    for b in range(seq // HALF):
        here = slice(b * HALF, (b + 1) * HALF)
        where = sorted_rows(b)
        mix, dqkv = mixs[where, :], dqkvs[where, :]
        if scale is not None:
            mix, dqkv = mix * scale, dqkv * scale
        mixn[here, :] = mix
        dqkvn[here, :] = dqkv


def ends_body(n, nz, fast, place, *refs):
    pieces = refs[:n]
    mixn, dqkvn, norms, nhats, acc_o, acc_d, vec_in, w_all, w_out, params = refs[n : n + 10]
    at = n + 10
    if fast:
        ff_one, ff_two, ff_came = refs[at : at + 3]
        at += 3
    keep_pay, send_pay, g_out = refs[at : at + 3]
    n_pay = 4 if fast else 2
    pays = refs[at + 3 : at + 3 + n_pay]
    spare, gs, grad_w, vec = refs[at + 3 + n_pay :]
    zed = place[1]
    gain = params[0:1, :]
    g_gain = jnp.zeros((8, D), F32)
    g_shift = jnp.zeros((8, D), F32)
    g_bias = jnp.zeros((8, 256), F32)
    for p in range(0, n, 8):
        rows = slice(p * TOK, (p + 8) * TOK)
        gs[rows, :] = joined(pieces[p : p + 8], TOK)
        dqkv = dqkvn[rows, :]
        dnorm = mm_nt(dqkv, w_all[...])
        g_gain += fold(dnorm * nhats[rows, :].astype(F32))
        g_shift += fold(dnorm)
        g_bias += fold(dqkv.astype(F32))
        part_o = (mm_nn(mixn[rows, :], w_out[...]) + acc_o[rows, :].astype(F32)).astype(BF16)
        part_d = (dnorm * gain + acc_d[rows, :].astype(F32)).astype(BF16)
        for q in range(8):
            target = send_pay if (p + q) % 2 else keep_pay
            here = slice(q * TOK, (q + 1) * TOK)
            target[(p + q) // 2, :, 0:512] = part_o[here, :]
            target[(p + q) // 2, :, 512:1024] = part_d[here, :]
    vec[...] = vec_in[...]
    for row, value in ((0, g_gain), (1, g_shift), (5, g_bias)):
        vec[row : row + 1, 0 : value.shape[1]] = jnp.sum(value, axis=0, keepdims=True)
    g_out[...] = mm_tn(mixn[...], gs[...]).astype(BF16)
    grad_w[...] = mm_tn(dqkvn[...], norms[...]).T
    if fast:
        spare[...] = jnp.zeros_like(spare)
        for j in range(8):
            lanes_j = vec[:, (j // 2) * 128 : (j // 2) * 128 + 128]
            spare[8 * j : 8 * j + 8, :] = lanes_j if j % 2 else pltpu.roll(lanes_j, 64, 1)
        low = low_lanes((128, 128))
        own, near, two, ff_sum = pays
        near[:, 512:1024] = ff_one[...]
        for k, target in ((0, own), (1, near.at[:, 0:256]), (2, two), (3, near.at[:, 256:512])):
            tall = pl.ds(pl.multiple_of((zed ^ k) * 128, 128), 128)
            target[:, 0:128] = grad_w[tall, 0:128].astype(BF16)
            target[:, 128:256] = jnp.where(low, grad_w[tall, 128:256], spare[...]).astype(BF16)
        ff_sum[0:128, :] = (ff_two[...].astype(F32) + ff_came[...].astype(F32)).astype(BF16)
        ff_sum[128:192, :] = g_out[...]
    else:
        pays[0][...] = grad_w[...].astype(BF16)
        pays[1][...] = vec[...]


def close_body(fast, place, x_ref, g_ref, params, *refs):
    if fast:
        parts, (value, out, grad, copy) = refs[:5], refs[5:]
        copy[...] = value[...]
    else:
        parts, out, grad = refs[:-2], refs[-2], refs[-1]
    x = x_ref[...].astype(F32)
    nhat, inv = normalized(x)
    if fast:
        own, came_a, came_b, last_a, last_b = parts
        total_o = own[:, 0:D].astype(F32) + came_a[0].astype(F32) + last_a[...].astype(F32)
        dn = own[:, D : 2 * D].astype(F32) + came_b[0].astype(F32) + last_b[...].astype(F32)
    else:
        total = parts[0][...].astype(F32)
        for part in parts[1:]:
            total = total + part[...].astype(F32)
        total_o, dn = total[:, 0:D], total[:, D : 2 * D]
    out[...] = (x + total_o + params[4:5, :]).astype(BF16)
    lead = jnp.mean(dn, axis=-1, keepdims=True)
    along = jnp.mean(dn * nhat, axis=-1, keepdims=True)
    grad[...] = g_ref[...].astype(F32) + inv * (dn - lead - nhat * along)


def chip_body(keep, came, *outs):
    for k, out in enumerate(outs):
        out[...] = (keep[k].astype(F32) + came[k].astype(F32)).astype(BF16)


def chip_fast_body(n_later, keep, came, *refs):
    later, (first_a, first_b, own, kept_a, kept_b, *held) = refs[:n_later], refs[n_later:]
    for value, copy in zip(later, held):
        copy[...] = value[...]

    def both(k, lanes):
        return (keep[k, :, lanes].astype(F32) + came[k, :, lanes].astype(F32)).astype(BF16)

    left, right = slice(0, D), slice(D, 2 * D)
    own[:, left] = both(0, left)
    own[:, right] = both(0, right)
    first_a[0] = both(1, left)
    first_a[1] = both(3, left)
    first_b[0] = both(2, right)
    first_b[1] = both(3, right)
    kept_a[...] = both(2, left)
    kept_b[...] = both(1, right)


def cross_body(n_later, kept_a, kept_b, came_a, came_b, *refs):
    later, (second_a, second_b, *held) = refs[:n_later], refs[n_later:]
    for value, copy in zip(later, held):
        copy[...] = value[...]
    second_a[...] = (kept_a[...].astype(F32) + came_a[1].astype(F32)).astype(BF16)
    second_b[...] = (kept_b[...].astype(F32) + came_b[1].astype(F32)).astype(BF16)


def gate_body(value, *refs):
    out = refs[-1]
    out[...] = value[...]


def relay_body(two, came, out):
    out[...] = (two[...].astype(F32) + came[:, 256:512].astype(F32)).astype(BF16)


def out_body(mine, came, out):
    out[...] = (mine[...].astype(F32) + came[128:192, :].astype(F32)).astype(BF16)


def share_body(ff_own, ff_far, own, near, far, out_half, out_far, *refs):
    out = refs[-1]
    out[:, 0:512] = (ff_own[...].astype(F32) + near[:, 512:1024].astype(F32) + ff_far[0:128, :].astype(F32)).astype(BF16)
    out[:, 512:768] = (own[...].astype(F32) + near[:, 0:256].astype(F32) + far[...].astype(F32)).astype(BF16)
    g_out = (out_half[...].astype(F32) + out_far[...].astype(F32)).astype(BF16)
    out[0:64, 768:1024] = g_out[:, 0:256]
    out[64:128, 768:1024] = g_out[:, 256:512]


def finish_body(n, nz, place, *refs):
    alls = refs[:n]
    (ln1g, ln1b, gqkv, bqkv, gout, bout, ln2g, ln2b, gup, bup, gdown, bdown) = refs[n : n + 12]
    held_u, held_a, held_v, flat = refs[n + 12 :]
    me, zed = place[0], place[1]
    span = FF // nz
    total = jnp.zeros((8, D), F32)
    wide = low_lanes((8, 128))
    for k in range(n):
        who = me ^ k
        held_a[who] = alls[k][:, 512:768].astype(F32)
        held_u[who] = alls[k][:, 0:256].astype(F32)
        rows = pl.ds(pl.multiple_of(who * 64, 64), 64)
        gdown[rows, 0:256] = alls[k][0:64, 256:512].astype(F32)
        gdown[rows, 256:512] = alls[k][64:128, 256:512].astype(F32)
        spare = alls[k][0:64, 640:768].astype(F32)
        small = []
        for j in range(0, 8, 2):
            small.append(jnp.where(wide, pltpu.roll(spare[8 * j : 8 * j + 8], 64, 1), spare[8 * j + 8 : 8 * j + 16]))
        small = jnp.concatenate(small, axis=1)
        held_v[who] = small
        total = total + small
    for h in range(0, n, 2):
        even, later = held_a[h], held_a[h + 1]
        low = low_lanes((128, 128))
        at = h * 64
        gqkv[:, at : at + 128] = jnp.where(low, even[:, 0:128], pltpu.roll(later[:, 0:128], 64, 1))
        gqkv[:, D + at : D + at + 128] = jnp.where(low, pltpu.roll(even[:, 0:128], 64, 1), later[:, 0:128])
        gqkv[:, 2 * D + at : 2 * D + at + 128] = jnp.where(low, even[:, 128:256], pltpu.roll(later[:, 128:256], 64, 1))
        for z in range(0, nz, 2):
            lanes = slice(z * 64, z * 64 + 128)
            e, l = held_u[h][:, lanes], held_u[h + 1][:, lanes]
            gup[:, z * span + at : z * span + at + 128] = jnp.where(low, e, pltpu.roll(l, 64, 1))
            gup[:, (z + 1) * span + at : (z + 1) * span + at + 128] = jnp.where(low, pltpu.roll(e, 64, 1), l)
        low = low_lanes((1, 128))
        e, l = held_v[h], held_v[h + 1]
        flat[h // 2 : h // 2 + 1, :] = jnp.where(low, e[5:6, 0:128], pltpu.roll(l[5:6, 0:128], 64, 1))
        flat[4 + h // 2 : 5 + h // 2, :] = jnp.where(low, pltpu.roll(e[5:6, 0:128], 64, 1), l[5:6, 0:128])
        flat[8 + h // 2 : 9 + h // 2, :] = jnp.where(low, e[5:6, 128:256], pltpu.roll(l[5:6, 128:256], 64, 1))
        lane = pl.ds(pl.multiple_of((zed // 2) * 128, 128), 128)
        odd = (zed % 2) == 1
        e = half_pick(held_v[h, 6:7, lane], odd, False)
        l = half_pick(held_v[h + 1, 6:7, lane], odd, True)
        bup[at : at + 128] = jnp.where(low, e, l).reshape(128)
    for k in range(n):
        held_a[me ^ k] = alls[k][:, 768:1024].astype(F32)
    for p in range(2):
        rows = held_a[2 * zed + p]
        gout[64 * p : 64 * p + 64, 0:256] = rows[0:64]
        gout[64 * p : 64 * p + 64, 256:512] = rows[64:128]
    flat[12:20, :] = jnp.zeros((8, 128), F32)
    for r in range(3):
        bqkv[r * 128 : (r + 1) * 128] = flat[pl.ds(zed * 3 + r, 1), :].reshape(128)
    held_v[0] = total
    lane = pl.ds(pl.multiple_of(zed * 128, 128), 128)
    ln1g[...] = held_v[0, 0:1, lane].reshape(128)
    ln1b[...] = held_v[0, 1:2, lane].reshape(128)
    ln2g[...] = held_v[0, 2:3, lane].reshape(128)
    ln2b[...] = held_v[0, 3:4, lane].reshape(128)
    held_v[1] = total * (1.0 / n)
    bout[...] = held_v[1, 4:5, lane].reshape(128)
    bdown[...] = held_v[1, 4:5, lane].reshape(128)


def xor_pairs(size, k):
    return [(i, i ^ k) for i in range(size)]


def gather_ctx(value, n, beside=None):
    got = {0: value}
    for k in range(2, n, 2):
        got[k] = lax.ppermute(value, "ctx", xor_pairs(n, k))
    for k in range(0, n, 2):
        source = beside if k == 0 and beside is not None else got[k]
        got[k + 1] = lax.ppermute(source, "ctx", xor_pairs(n, 1))
    return [got[k] for k in range(n)]


def gather_fsdp(value, nz):
    return [value] + [lax.ppermute(value, "fsdp", xor_pairs(nz, k)) for k in range(1, nz)]


def relay_fsdp(value, nz):
    one, two = (lax.ppermute(value, "fsdp", xor_pairs(nz, k)) for k in (1, 2))
    return [value, one, two, lax.ppermute(two, "fsdp", xor_pairs(nz, 1))]


def rotary_tables(seq):
    pos = np.arange(seq, dtype=np.float32)
    inverse = (np.float32(10000.0) ** (-np.arange(ROT // 2, dtype=np.float32) * np.float32(2.0) / np.float32(ROT))).astype(np.float32)
    angles = (pos[:, None] * inverse[None, :]).astype(np.float32).astype(np.float64)
    cos_t = np.ones((seq, 64), np.float32)
    sin_t = np.zeros((seq, 64), np.float32)
    half = ROT // 2
    cos_t[:, 0:half] = np.cos(angles)
    cos_t[:, half:ROT] = np.cos(angles)
    sin_t[:, 0:half] = -np.sin(angles)
    sin_t[:, half:ROT] = np.sin(angles)
    return np.concatenate([cos_t, sin_t], axis=1)


def shape(dims, dtype=F32):
    return jax.ShapeDtypeStruct(dims, dtype)


def per_device(
    n,
    nz,
    inputs,
    block_order,
    ln1_gain,
    ln1_bias,
    w_qkv,
    b_qkv,
    w_attn_out,
    b_attn_out,
    ln2_gain,
    ln2_bias,
    w_up,
    b_up,
    w_down,
    b_down,
    cotangent,
):
    fast = n == HEADS and nz * 2 == HEADS
    seq = n * TOK
    width = FF // n
    me = lax.axis_index("ctx").astype(jnp.int32)
    zed = lax.axis_index("fsdp").astype(jnp.int32)
    place = jnp.stack([me, zed])
    x, g = inputs[0], cotangent[0]
    blocks = TOK // HALF
    chunk_at = (jnp.arange(n, dtype=jnp.int32) ^ me)[:, None] * blocks + jnp.arange(blocks, dtype=jnp.int32)[None, :]
    pick = chunk_at.reshape(-1)[:, None] == jnp.arange(n * blocks, dtype=jnp.int32)[None, :]
    order = jnp.sum(jnp.where(pick, block_order[None, :], 0), axis=1).astype(jnp.int32)
    turn = rotary_tables(seq)

    if fast:
        vectors = (ln1_gain, ln1_bias, ln2_gain, ln2_bias, b_attn_out, b_down, b_qkv, b_up)
        pack, piece, pack_w = pack_call(nz, w_qkv, w_up, w_down, w_attn_out, inputs, cotangent, vectors)
        pieces = gather_ctx(piece, n)
        far = relay_fsdp(pack, nz)
        given = vmem_call(
            functools.partial(unpack_body, nz),
            [shape((D, 256), BF16), shape((D, width), BF16), shape((width, D), BF16), shape((8, D))],
            scratch=[pltpu.VMEM((nz, 16, 128), F32)],
            n_smem=1,
            n_in=nz,
            cost=LONG,
            name="unpack",
        )(place, *far)
        pairs = []
        for c in range(n):
            for z in range(nz):
                pairs.append((c * nz + z, (2 * z + c % 2) * nz + c // 2))
        pack_w = vmem_call(gate_body, shape(pack_w.shape, BF16), n_in=2, name="gate_w")(pack_w, far[1])
        head_w = lax.ppermute(pack_w, ("ctx", "fsdp"), pairs)
    else:
        whole = [
            lax.all_gather(v, "fsdp", axis=0, tiled=True)
            for v in (ln1_gain, ln1_bias, ln2_gain, ln2_bias, b_attn_out, b_down, b_qkv, b_up)
        ]
        whole = [v.astype(F32) for v in whole]
        head = me // (n // HEADS)
        bq = lax.dynamic_index_in_dim(whole[6].reshape(3, HEADS, HEAD_DIM), head, 1, False).reshape(-1)
        bu = lax.dynamic_index_in_dim(whole[7].reshape(n, width), me, 0, False)
        params = jnp.stack(
            [whole[0], whole[1], whole[2], whole[3], whole[4] + whole[5]]
            + [jnp.pad(bq, (0, D - 3 * HEAD_DIM)), jnp.pad(bu, (0, D - width)), jnp.zeros((D,), F32)]
        )
        wq = lax.dynamic_index_in_dim(w_qkv.reshape(-1, 3, HEADS, HEAD_DIM), head, 2, False).reshape(-1, 3 * HEAD_DIM)
        given = [jnp.pad(lax.all_gather(wq, "fsdp", axis=0, tiled=True), ((0, 0), (0, 64)))]
        wu = lax.dynamic_slice_in_dim(w_up, me * width, width, 1)
        wd = lax.all_gather(w_down, "fsdp", axis=0, tiled=True)
        given += [lax.all_gather(wu, "fsdp", axis=0, tiled=True), lax.dynamic_slice_in_dim(wd, me * width, width, 0)]
        wo = lax.all_gather(w_attn_out, "fsdp", axis=0, tiled=True)
        given.append(params)
        pieces = gather_ctx(jnp.concatenate([x, g], axis=0), n)
        head_w = lax.dynamic_slice_in_dim(wo, head * HEAD_DIM, HEAD_DIM, 0)

    w_all, w_up_c, w_down_c, params = given
    whole_seq = shape((seq, D), BF16)
    half = (n // 2, TOK, 2 * D)
    rows = D // nz
    if fast:
        ff_pays = [shape((rows, 512), BF16)] * nz
        attn_pays = [shape((rows, 256), BF16), shape((rows, 1024), BF16), shape((rows, 256), BF16), shape((rows + HEAD_DIM, 512), BF16)]
    else:
        ff_pays = [shape((D, width), BF16), shape((width, D), BF16)]
        attn_pays = [shape((D, 256), BF16), shape((8, D))]
    ff_out = vmem_call(
        functools.partial(ff_body, n, nz, fast),
        [whole_seq, whole_seq, shape((8, D)), whole_seq, whole_seq] + ff_pays,
        scratch=[
            pltpu.VMEM((seq, D), BF16),
            pltpu.VMEM((seq, width), BF16),
            pltpu.VMEM((seq, width), BF16),
            pltpu.VMEM((seq, D), BF16),
            pltpu.VMEM((D, width), BF16),
            pltpu.VMEM((width, D), BF16),
        ],
        n_smem=1,
        n_in=n + 3,
        cost=pl.CostEstimate(flops=4_000_000_000, bytes_accessed=0, transcendentals=0),
        name="feed_forward",
    )(place, *pieces, w_up_c, w_down_c, params)
    acc_o, acc_d, vec_ff, norms, nhats = ff_out[:5]
    ff_pay = ff_out[5:]
    from_ff = []
    if fast:
        ff_pass = lax.ppermute(ff_pay[3], "fsdp", xor_pairs(nz, 1))
        from_ff = [ff_pay[1], ff_pay[2], ff_pass]
    mixn, dqkvn = vmem_call(
        functools.partial(attn_body, n),
        [shape((seq, 64), BF16), shape((seq, 256), BF16)],
        scratch=[
            pltpu.VMEM((seq, 256), F32),
            pltpu.VMEM((seq, 64), BF16),
            pltpu.VMEM((seq, 64), BF16),
            pltpu.VMEM((seq, 64), BF16),
            pltpu.VMEM((seq, 64), BF16),
            pltpu.VMEM((seq, 64), BF16),
            pltpu.VMEM((64, seq), F32),
            pltpu.VMEM((64, seq), F32),
            pltpu.VMEM((seq, 128), F32),
            pltpu.VMEM((seq, 256), BF16),
        ],
        n_smem=2,
        n_in=n + 5,
        cost=pl.CostEstimate(flops=6_000_000_000, bytes_accessed=0, transcendentals=0),
        name="attention",
    )(place, order, *pieces, w_all, params, head_w, turn, norms)
    ends_out = vmem_call(
        functools.partial(ends_body, n, nz, fast),
        [shape(half, BF16), shape(half, BF16), shape((HEAD_DIM, D), BF16)] + attn_pays,
        scratch=[
            pltpu.VMEM((128, 128), F32),
            pltpu.VMEM((seq, D), BF16),
            pltpu.VMEM((D, 256), F32),
            pltpu.VMEM((8, D), F32),
        ],
        n_smem=1,
        n_in=n + 10 + len(from_ff),
        cost=pl.CostEstimate(flops=3_000_000_000, bytes_accessed=0, transcendentals=0),
        name="ends",
    )(place, *pieces, mixn, dqkvn, norms, nhats, acc_o, acc_d, vec_ff, w_all, head_w, params, *from_ff)
    keep_pay, send_pay, g_out = ends_out[:3]
    attn_pay = ends_out[3:]

    came = lax.ppermute(send_pay, "ctx", xor_pairs(n, 1))
    if fast:
        chip_out = vmem_call(
            functools.partial(chip_fast_body, 0),
            [shape((2, TOK, D), BF16)] * 2 + [shape((TOK, 2 * D), BF16)] + [shape((TOK, D), BF16)] * 2 + [],
            n_in=2 + 0,

            name="chip_sum",
        )(keep_pay, came)
        first_a, first_b, own_sum, kept_a, kept_b = chip_out[:5]
        came_a = lax.ppermute(first_a, "ctx", xor_pairs(n, 2))
        came_b = lax.ppermute(first_b, "ctx", xor_pairs(n, 4))
        cross_out = vmem_call(
            functools.partial(cross_body, 0),
            [shape((TOK, D), BF16)] * 2 + [],
            n_in=4 + 0,

            name="cross",
        )(kept_a, kept_b, came_a, came_b)
        second_a, second_b = cross_out[:2]
        parts = [own_sum, came_a, came_b]
        parts += [lax.ppermute(second_a, "ctx", xor_pairs(n, 4)), lax.ppermute(second_b, "ctx", xor_pairs(n, 2))]
    else:
        chip_sum = vmem_call(chip_body, [shape((TOK, 2 * D), BF16)] * (n // 2), n_in=2, name="chip_sum")(keep_pay, came)
        parts = [chip_sum[0]] + [lax.ppermute(chip_sum[k // 2], "ctx", xor_pairs(n, k)) for k in range(2, n, 2)]
    if fast:
        ff_far = lax.ppermute(attn_pay[3], "fsdp", xor_pairs(nz, 2))
        out_half = vmem_call(out_body, shape((HEAD_DIM, D), BF16), n_in=2, cost=LONG, name="out_half")(g_out, ff_far)
        out_far = lax.ppermute(out_half, "fsdp", xor_pairs(nz, 1))
        attn_near = lax.ppermute(attn_pay[1], "fsdp", xor_pairs(nz, 1))
        attn_two = vmem_call(relay_body, shape((rows, 256), BF16), n_in=2, cost=LONG, name="relay")(attn_pay[2], attn_near)
        attn_far = lax.ppermute(attn_two, "fsdp", xor_pairs(nz, 2))
        share = vmem_call(share_body, shape((rows, 1024), BF16), n_in=7 + 2, name="share")(
            ff_pay[0], ff_far, attn_pay[0], attn_near, attn_far, out_half, out_far, parts[3], parts[4]
        )
        through = [share]
    else:
        through = []
    closed = vmem_call(
        functools.partial(close_body, fast),
        [shape((TOK, D), BF16), shape((TOK, D))] + [shape(v.shape, BF16) for v in through],
        n_smem=1,
        n_in=3 + len(parts) + len(through),
        name="close",
    )(place, x, g, params, *parts, *through)

    output, grad_inputs = closed[:2]
    if fast:
        alls = gather_ctx(share, n, closed[2])
        dz = D // nz
        outs = vmem_call(
            functools.partial(finish_body, n, nz),
            [
                shape((dz,)),
                shape((dz,)),
                shape((dz, 3 * D)),
                shape((3 * dz,)),
                shape((dz, D)),
                shape((dz,)),
                shape((dz,)),
                shape((dz,)),
                shape((dz, FF)),
                shape((FF // nz,)),
                shape((FF // nz, D)),
                shape((dz,)),
            ],
            scratch=[
                pltpu.VMEM((n, 128, 256), F32),
                pltpu.VMEM((n, 128, 256), F32),
                pltpu.VMEM((n, 8, D), F32),
                pltpu.VMEM((24, 128), F32),
            ],
            n_smem=1,
            n_in=n,
            name="finish",
        )(place, *alls)
    else:
        everyone = ("ctx", "fsdp")
        head = me // (n // HEADS)
        g_up, g_down = ff_pay
        g_qkv, vec = attn_pay

        def own(full, axis=0):
            size = full.shape[axis] // nz
            return lax.dynamic_slice_in_dim(full, zed * size, size, axis)

        def spread(part, dims, index, axis):
            full = jnp.zeros(dims, part.dtype)
            return lax.psum(lax.dynamic_update_index_in_dim(full, part, index, axis), everyone).astype(F32)

        qkv_full = spread(g_qkv[:, 0:192].reshape(D, 3, HEAD_DIM), (D, 3, HEADS, HEAD_DIM), head, 2).reshape(D, 3 * D)
        out_full = spread(g_out, (HEADS, HEAD_DIM, D), head, 0).reshape(D, D)
        up_full = spread(g_up, (D, n, width), me, 1).reshape(D, FF)
        down_full = spread(g_down, (n, width, D), me, 0).reshape(FF, D)
        bq_full = spread(vec[5, 0:192].reshape(3, HEAD_DIM), (3, HEADS, HEAD_DIM), head, 1).reshape(3 * D)
        bu_full = spread(vec[6, 0:width], (n, width), me, 0).reshape(FF)
        flat = lax.psum(vec, everyone)
        b_full = flat[4] * (1.0 / n)
        outs = [own(v) for v in (flat[0], flat[1], qkv_full, bq_full, out_full, b_full)]
        outs += [own(v) for v in (flat[2], flat[3], up_full, bu_full, down_full, b_full)]
    return (output[None], grad_inputs[None], *outs)


def solution(mesh):
    rows, flat, tokens = P("fsdp", None), P("fsdp"), P("fsdp", "ctx", None)
    weights = (flat, flat, rows, flat, rows, flat, flat, flat, rows, flat, rows, flat)
    return jax.shard_map(
        functools.partial(per_device, mesh.shape["ctx"], mesh.shape["fsdp"]),
        mesh=mesh,
        in_specs=(tokens, P(), *weights, tokens),
        out_specs=(tokens, tokens, *weights),
        check_vma=False,
    )
```
